512 devices in a mesh: tm: 16 (over y, z_hi), space: 32 (over z_lo, x, core).
Axes of the slice: x: 4, y: 4, z: 16 (z_hi: 4, z_lo: 4; z = z_hi * 4 + z_lo), core: 2. Of those that a mesh axis runs over, the one named last changes fastest.
Arguments:
- node_states: float32 [16, 3, 64, 128, 128], P('tm', None, None, 'space'), may hold values from -6 to 6
- initial_state: float32 [64, 128, 128], P(None, 'space'), may hold values from -6 to 6
- velocity: bfloat16 [3, 64, 128, 128], P(None, None, 'space'), may hold values from -1 to 1
Outputs:
- new_states: float32 [16, 3, 64, 128, 128], P('tm', None, None, 'space')
The draws below stay inside these ranges and needn't reach their ends.
All inputs are finite; a program needn't handle non-finite values.
Results may differ from the reference program's by a relative error of at most 0.0003.
Values sent between devices are 32-bit elements; how exact they have to be, the bound alone decides.
A program may use at most 64 MiB of HBM per device.

```python
import jax
import jax.numpy as jnp
import numpy as np
from jax import lax

CY = 8
CZ = 16
NODES = 64
TIME_NODES = 3
SWEEPS = 3
SLICES = 16
NX = 128


def draw_velocity(key, part):
    key = jax.random.fold_in(key, 11)
    sign_key, size_key = jax.random.split(key)
    signs = 2.0 * jax.random.randint(sign_key, (3,), 0, 2).astype(jnp.float32) - 1.0
    columns = CY * CZ
    column_index = lax.iota(jnp.int32, columns)
    y_band = jnp.where(column_index // CZ < CY // 2, 1.0, -1.0).astype(jnp.float32)
    z_band = jnp.where(column_index % CZ < (CZ + 1) // 2, 1.0, -1.0).astype(jnp.float32)
    pattern = jnp.stack([y_band, z_band, y_band])
    uniform_part = jax.random.uniform(size_key, (3, NODES, NX, columns), jnp.float32)
    magnitude = 0.5 + 0.5 * uniform_part
    values = signs[:, None, None, None] * pattern[:, None, None, :] * magnitude
    return values.astype(jnp.bfloat16)


def shard_levels(own_key, shape, shards, low, largest):
    factor_of = 1.0
    for axis_at, blocks in shards:
        heights = jax.random.uniform(jax.random.fold_in(jax.random.fold_in(own_key, 6), axis_at), (blocks,), jnp.float32, low / len(shards), largest / len(shards))
        factor_of = factor_of * jnp.repeat(jnp.exp(heights), shape[axis_at] // blocks).reshape((-1,) + (1,) * (len(shape) - 1 - axis_at))
    return factor_of


def normal_values(rng, dims, spread, most, cuts=(), kind=jnp.bfloat16):
    loudness = shard_levels(rng, dims, cuts, -0.22, 0.18) if cuts else 1.0
    values = jax.random.normal(rng, dims, jnp.float32) * spread * loudness
    return jnp.minimum(jnp.maximum(values, -most), most).astype(kind)


def setup_inputs(seed: int = 0) -> dict:
    key_of = jax.random.split(jax.random.key(seed), 4)
    node_states = normal_values(key_of[0], (SLICES, TIME_NODES, NODES, NX, CY * CZ), 1.0, 6.0, ((0, 16), (3, 32)), jnp.float32)
    initial_state = normal_values(key_of[1], (NODES, NX, CY * CZ), 1.0, 6.0, ((1, 32),), jnp.float32)
    velocity = draw_velocity(jax.random.fold_in(key_of[3], 71), 0)
    return {"node_states": node_states, "initial_state": initial_state, "velocity": velocity}


slice_step = 0.08
fine_lift = 6.0
coarse_lift = 1.0
highest = lax.Precision.HIGHEST

def lagrange_derivative(points):
    number = len(points)
    bary_weights = np.array([1.0 / np.prod([points[col_index] - points[other] for other in range(number) if other != col_index]) for col_index in range(number)])
    derivative = np.zeros((number, number))
    for row_index in range(number):
        for col_index in range(number):
            if row_index != col_index:
                derivative[row_index, col_index] = bary_weights[col_index] / bary_weights[row_index] / (points[row_index] - points[col_index])
        derivative[row_index, row_index] = -np.sum(derivative[row_index])
    return derivative

def gradient_table(points):
    derivative = lagrange_derivative(points)
    identity = np.eye(len(points))
    stacked = np.concatenate([np.kron(np.kron(derivative, identity), identity), np.kron(np.kron(identity, derivative), identity), np.kron(np.kron(identity, identity), derivative)], axis=0)
    return jnp.asarray(stacked, dtype=jnp.float32)

def level_tables():
    points = np.array([-1.0, -1.0 / np.sqrt(5.0), 1.0 / np.sqrt(5.0), 1.0])
    weights = np.array([1.0, 5.0, 5.0, 1.0]) / 6.0
    prolong = np.stack([(1.0 - points) / 2.0, (1.0 + points) / 2.0], axis=1)
    restrict_line = prolong.T * weights[None, :]
    restrict_cube = np.kron(np.kron(restrict_line, restrict_line), restrict_line)
    prolong_cube = np.kron(np.kron(prolong, prolong), prolong)
    return (gradient_table(points), gradient_table(np.array([-1.0, 1.0])), jnp.asarray(restrict_cube, dtype=jnp.float32), jnp.asarray(prolong_cube, dtype=jnp.float32))

def corner_values(flow):
    row_count = flow.shape[2]
    columns = flow.shape[3]
    return flow.reshape(3, 4, 4, 4, row_count, columns)[:, ::3, ::3, ::3].reshape(3, 8, row_count, columns)

def shift_columns(values, offset):
    zeros_pad = jnp.zeros(values.shape[:-1] + (abs(offset),), values.dtype)
    if offset > 0:
        return jnp.concatenate([zeros_pad, values[..., :-offset]], axis=-1)
    return jnp.concatenate([values[..., -offset:], zeros_pad], axis=-1)

def upwind(inside, outside, normal, lift):
    return lift * jnp.minimum(normal, 0.0) * (inside - outside)

def apply_operator(fields, flow, gradient, order, lift, lower, upper):
    number = fields.shape[0]
    row_count = fields.shape[2]
    columns = fields.shape[3]
    nodes = order ** 3
    far_node = order - 1
    gradients = jnp.einsum('kn,fnxe->fkxe', gradient, fields, precision=highest).reshape(number, 3, nodes, row_count, columns)
    result = -(flow[0] * gradients[:, 0] + flow[1] * gradients[:, 1] + flow[2] * gradients[:, 2])
    nodal_cube = fields.reshape(number, order, order, order, row_count, columns)
    flow_cube = flow.reshape(3, order, order, order, row_count, columns)
    lower_cube = lower.reshape(number, order, order, 1, columns)
    upper_cube = upper.reshape(number, order, order, 1, columns)
    layer_index = lax.iota(jnp.int32, columns) % CZ
    x_outside_low = jnp.concatenate([lower_cube, nodal_cube[:, far_node, :, :, :-1, :]], axis=3)
    x_low = upwind(nodal_cube[:, 0], x_outside_low, -flow_cube[0, 0], lift)
    x_outside_high = jnp.concatenate([nodal_cube[:, 0, :, :, 1:, :], upper_cube], axis=3)
    x_high = upwind(nodal_cube[:, far_node], x_outside_high, flow_cube[0, far_node], lift)
    y_low = upwind(nodal_cube[:, :, 0], shift_columns(nodal_cube[:, :, far_node], CZ), -flow_cube[1, :, 0], lift)
    y_high = upwind(nodal_cube[:, :, far_node], shift_columns(nodal_cube[:, :, 0], -CZ), flow_cube[1, :, far_node], lift)
    z_outside_low = jnp.where(layer_index == 0, 0.0, shift_columns(nodal_cube[:, :, :, far_node], 1))
    z_low = upwind(nodal_cube[:, :, :, 0], z_outside_low, -flow_cube[2, :, :, 0], lift)
    z_outside_high = jnp.where(layer_index == CZ - 1, 0.0, shift_columns(nodal_cube[:, :, :, 0], -1))
    z_high = upwind(nodal_cube[:, :, :, far_node], z_outside_high, flow_cube[2, :, :, far_node], lift)
    total = result.reshape(number, order, order, order, row_count, columns)
    total = total.at[:, 0].add(x_low).at[:, far_node].add(x_high)
    total = total.at[:, :, 0].add(y_low).at[:, :, far_node].add(y_high)
    total = total.at[:, :, :, 0].add(z_low).at[:, :, :, far_node].add(z_high)
    return total.reshape(number, nodes, row_count, columns)

def fine_sweeps(states, slice_begin, fine_apply):
    evaluated = fine_apply(jnp.concatenate([states, slice_begin[None]], axis=0))
    previous = evaluated[:3]
    begin_rate = evaluated[3]
    half_step = 0.5 * slice_step
    middle = slice_begin
    closing = slice_begin
    for sweep_index in range(SWEEPS):
        middle = slice_begin + half_step * (begin_rate - previous[0]) + slice_step * (5.0 * previous[0] + 8.0 * previous[1] - previous[2]) / 24.0
        middle_rate = fine_apply(middle[None])[0]
        closing = middle + half_step * (middle_rate - previous[1]) + slice_step * (8.0 * previous[1] + 5.0 * previous[2] - previous[0]) / 24.0
        closing_rate = fine_apply(closing[None])[0]
        previous = jnp.stack([begin_rate, middle_rate, closing_rate])
    return (middle, closing, previous)

def coarse_terms(slice_begin, closing, rates, restrict_cube, coarse_apply):
    quadrature = slice_step * (rates[0] + 4.0 * rates[1] + rates[2]) / 6.0
    restricted = jnp.einsum('kn,fnxe->fkxe', restrict_cube, jnp.stack([slice_begin, closing, quadrature]), precision=highest)
    coarse_old = restricted[:2]
    coarse_rates = coarse_apply(coarse_old)
    tau_term = restricted[2] - 0.5 * slice_step * (coarse_rates[0] + coarse_rates[1])
    offset = -slice_step * coarse_rates[0] + 0.5 * slice_step * (coarse_rates[0] + coarse_rates[1]) + tau_term
    return (coarse_old, offset)

def corrected(slice_begin, middle, closing, coarse_old, chain_begin, finish, prolong_cube):
    delta_begin = chain_begin - coarse_old[0]
    delta_end = finish - coarse_old[1]
    deltas = jnp.stack([delta_begin, 0.5 * (delta_begin + delta_end), delta_end])
    lifted = jnp.einsum('nk,fkxe->fnxe', prolong_cube, deltas, precision=highest)
    return jnp.stack([slice_begin, middle, closing]) + lifted

def reference(node_states, initial_state, velocity):
    gradient_fine, gradient_coarse, restrict_cube, prolong_cube = level_tables()
    flow = velocity.astype(jnp.float32)
    flow_coarse = corner_values(flow)
    columns = initial_state.shape[2]

    def fine_apply(fields):
        border = jnp.zeros((fields.shape[0], 16, columns), jnp.float32)
        return apply_operator(fields, flow, gradient_fine, 4, fine_lift, border, border)

    def coarse_apply(fields):
        border = jnp.zeros((fields.shape[0], 4, columns), jnp.float32)
        return apply_operator(fields, flow_coarse, gradient_coarse, 2, coarse_lift, border, border)
    begins = jnp.concatenate([initial_state[None], node_states[:-1, 2]], axis=0)

    def per_slice(inputs):
        states, slice_begin = inputs
        middle, closing, rates = fine_sweeps(states, slice_begin, fine_apply)
        coarse_old, offset = coarse_terms(slice_begin, closing, rates, restrict_cube, coarse_apply)
        return (middle, closing, coarse_old, offset)
    middles, closings, coarse_olds, offsets = lax.map(per_slice, (node_states, begins))
    chain_start = jnp.einsum('kn,nxe->kxe', restrict_cube, initial_state, precision=highest)

    def advance(carry, offset):
        finish = carry + slice_step * coarse_apply(carry[None])[0] + offset
        return (finish, (carry, finish))
    last_value, (chain_begins, finishes) = lax.scan(advance, chain_start, offsets)

    def finish_slice(inputs):
        slice_begin, middle, closing, coarse_old, chain_begin, finish = inputs
        return corrected(slice_begin, middle, closing, coarse_old, chain_begin, finish, prolong_cube)
    return lax.map(finish_slice, (begins, middles, closings, coarse_olds, chain_begins, finishes))
```

```python
import functools

import jax
import jax.numpy as jnp
import numpy as np
from jax import lax
from jax.experimental import pallas as pl
from jax.experimental.pallas import tpu as pltpu
from jax.sharding import PartitionSpec as P

MESH = pl.DeviceIdType.MESH
CZ = 16
LANES = 128
GROUP = 4
H = 0.08
DT = 0.5 * H
LIFT = 6.0
ROWS = 4
REACH = 3
SPAN = (2 * REACH + 1) * ROWS
MID = REACH * ROWS
FIELD = (4, 4, 2, 8, LANES)


def lagrange_derivative(points):
    number = len(points)
    weights = np.array(
        [1.0 / np.prod([points[i] - points[j] for j in range(number) if j != i]) for i in range(number)]
    )
    derivative = np.zeros((number, number))
    for i in range(number):
        for j in range(number):
            if i != j:
                derivative[i, j] = weights[j] / weights[i] / (points[i] - points[j])
        derivative[i, i] = -np.sum(derivative[i])
    return derivative


POINTS = np.array([-1.0, -1.0 / np.sqrt(5.0), 1.0 / np.sqrt(5.0), 1.0])
WEIGHTS = np.array([1.0, 5.0, 5.0, 1.0]) / 6.0
DER = lagrange_derivative(POINTS)
PRO = np.stack([(1.0 - POINTS) / 2.0, (1.0 + POINTS) / 2.0], axis=1)
RES = PRO.T * WEIGHTS[None, :]


def weighted(terms):
    total = None
    for factor, value in terms:
        factor = float(factor)
        if abs(factor) < 1e-12:
            continue
        piece = value if factor == 1.0 else factor * value
        total = piece if total is None else total + piece
    return total


def kernel(
    steps,
    columns,
    states_hbm,
    start_hbm,
    wind_hbm,
    out_hbm,
    states,
    wind,
    begin,
    nv,
    diag,
    xli,
    xhi,
    xlh,
    xhh,
    yl,
    yh,
    zl,
    zh,
    rates,
    first_rate,
    mid_state,
    end_state,
    base,
    send,
    recv,
    shuffle,
    flows,
    coef,
    old0,
    old1,
    group,
    partial,
    near,
    mid,
    far,
    result,
    load_sem,
    store_sem,
    fine_send,
    fine_recv,
    begin_send,
    begin_recv,
    flow_send,
    flow_recv,
    row_send,
    row_recv,
    group_send,
    group_recv,
    side_send,
    side_recv,
    part_send,
    part_recv,
):
    n = lax.axis_index("tm")
    s = lax.axis_index("space")
    g = n // GROUP
    z = n % GROUP
    groups = steps // GROUP

    sub = lax.broadcasted_iota(jnp.int32, (8, LANES), 0)
    lane = lax.broadcasted_iota(jnp.int32, (8, LANES), 1)
    parity = sub // 4
    row = sub % 4

    def split(even, odd):
        return jnp.where(parity == 0, jnp.float32(even), jnp.float32(odd))

    def remote(src, dst, ssem, rsem, device):
        return pltpu.make_async_remote_copy(
            src_ref=src, dst_ref=dst, send_sem=ssem, recv_sem=rsem, device_id=device, device_id_type=MESH
        )

    has = {-1: s > 0, 1: s < columns - 1}

    def inside(d):
        if d == 0:
            return None
        return s + d >= 0 if d < 0 else s + d < columns

    def both(a, b):
        if a is None:
            return b
        if b is None:
            return a
        return jnp.logical_and(a, b)

    def when(cond, run):
        if cond is None:
            run()
        else:
            pl.when(cond)(run)

    transfers = {}

    def add(name, sends, receives, make, partner):
        transfers.setdefault(name, []).append((sends, receives, make, partner))

    for k, d in enumerate((-1, 1)):
        add(
            "states",
            has[d],
            has[-d],
            functools.partial(
                remote,
                send.at[k, pl.ds(0, 3)],
                recv.at[1 - k, pl.ds(0, 3)],
                fine_send.at[k, 0],
                fine_recv.at[1 - k, 0],
                (n, s + d),
            ),
            None,
        )
        add(
            "begin_trace",
            both(n < steps - 1, has[d]),
            both(n > 0, has[-d]),
            functools.partial(
                remote,
                send.at[k, 2],
                recv.at[1 - k, 3],
                fine_send.at[k, 1],
                fine_recv.at[1 - k, 1],
                (n + 1, s + d),
            ),
            (n - 1, s - d),
        )
        add(
            "first_trace",
            both(n == 0, has[d]),
            both(n == 0, has[-d]),
            functools.partial(
                remote,
                send.at[k, 3],
                recv.at[1 - k, 3],
                fine_send.at[k, 2],
                fine_recv.at[1 - k, 1],
                (n, s + d),
            ),
            None,
        )
        for index, buffer in enumerate((old0, old1)):
            add(
                f"row{index}",
                has[d],
                has[-d],
                functools.partial(
                    remote,
                    buffer.at[1 if d < 0 else ROWS],
                    buffer.at[ROWS + 1 if d < 0 else 0],
                    row_send.at[k, index],
                    row_recv.at[1 - k, index],
                    (n, s + d),
                ),
                None,
            )
        add(
            "side",
            has[d],
            has[-d],
            functools.partial(
                remote,
                group.at[:, pl.ds(ROWS, ROWS)],
                group.at[:, pl.ds(2 * ROWS if d < 0 else 0, ROWS)],
                side_send.at[k],
                side_recv.at[1 - k],
                (n, s + d),
            ),
            None,
        )
    add(
        "begin",
        n < steps - 1,
        n > 0,
        functools.partial(remote, states_hbm.at[2], begin, begin_send, begin_recv, (n + 1, s)),
        (n - 1, s),
    )
    for index, d in enumerate((-3, -2, -1, 1, 2, 3)):
        add(
            "flow",
            inside(d),
            inside(-d),
            functools.partial(
                remote,
                flows.at[REACH],
                flows.at[REACH - d],
                flow_send.at[index],
                flow_recv.at[index],
                (n, s + d),
            ),
            (n, s - d),
        )
    for shift in (1, 2, 3):
        add(
            "group",
            None,
            None,
            functools.partial(
                remote,
                group.at[z, pl.ds(ROWS, ROWS)],
                group.at[z, pl.ds(ROWS, ROWS)],
                group_send.at[shift - 1],
                group_recv.at[shift - 1],
                (g * GROUP + (z + shift) % GROUP, s),
            ),
            (g * GROUP + (z + GROUP - shift) % GROUP, s),
        )
    slot = 0
    for distance, buffer in ((1, near), (2, mid), (3, far)):
        for d in range(-distance, distance + 1):
            add(
                "part",
                both(g + distance < groups, inside(d)),
                both(g >= distance, inside(-d)),
                functools.partial(
                    remote,
                    partial,
                    buffer.at[pl.ds((distance - d) * ROWS, ROWS)],
                    part_send.at[slot],
                    part_recv.at[slot],
                    (n + distance * GROUP, s + d),
                ),
                (n - distance * GROUP, s - d),
            )
            slot += 1

    def start(name):
        for sends, _, make, _ in transfers[name]:
            when(sends, lambda make=make: make().start())

    def arrive(name):
        for _, receives, make, _ in transfers[name]:
            when(receives, lambda make=make: make().wait_recv())

    def sent(name):
        for sends, _, make, _ in transfers[name]:
            when(sends, lambda make=make: make().wait_send())

    load_states = pltpu.make_async_copy(states_hbm, states, load_sem.at[0])
    load_wind = pltpu.make_async_copy(wind_hbm, wind, load_sem.at[1])
    load_first = pltpu.make_async_copy(start_hbm, begin, load_sem.at[2])
    load_states.start()
    load_wind.start()
    pl.when(n == 0)(load_first.start)

    recv[...] = jnp.zeros(recv.shape, jnp.float32)
    flows[...] = jnp.zeros(flows.shape, jnp.float32)
    old0[...] = jnp.zeros(old0.shape, jnp.float32)
    old1[...] = jnp.zeros(old1.shape, jnp.float32)
    group[...] = jnp.zeros(group.shape, jnp.float32)
    near[...] = jnp.zeros(near.shape, jnp.float32)
    mid[...] = jnp.zeros(mid.shape, jnp.float32)
    far[...] = jnp.zeros(far.shape, jnp.float32)

    barrier = pltpu.get_barrier_semaphore()
    expected = jnp.int32(0)

    def greet(cond, device):
        when(
            cond,
            lambda: pl.semaphore_signal(barrier, inc=1, device_id=device, device_id_type=MESH),
        )

    for d in (-1, 1):
        greet(has[d], (n, s + d))
        expected = expected + has[d].astype(jnp.int32)
    for name in ("begin_trace", "begin", "flow", "group", "part"):
        for index, (sends, receives, _, partner) in enumerate(transfers[name]):
            if name == "flow" and index in (2, 3):
                continue
            greet(receives, partner)
            expected = expected + (1 if sends is None else sends.astype(jnp.int32))

    load_states.wait()

    def pack(lower, upper, k_slot):
        for half in range(2):
            low = None
            high = None
            for r in range(4):
                b, hh = (4 * half + r) // 2, r % 2
                lv = lower[b, hh]
                hv = upper[b, hh]
                lv = pltpu.roll(lv, r, 0) if r else lv
                hv = pltpu.roll(hv, (r + 5) % 8, 0) if r != 3 else hv
                low = lv if low is None else jnp.where(row == r, lv, low)
                high = hv if high is None else jnp.where(row == r, hv, high)
            send[0, k_slot, half] = low
            send[1, k_slot, half] = high

    def unpack(k_slot):
        lows, highs = [], []
        for t in range(8):
            half, r = t // 4, t % 4
            lv = recv[0, k_slot, half]
            hv = recv[1, k_slot, half]
            lows.append(pltpu.roll(lv, 8 - r, 0) if r else lv)
            highs.append(pltpu.roll(hv, 3 - r, 0) if r != 3 else hv)
        return (
            jnp.stack(lows).reshape(4, 2, 8, LANES),
            jnp.stack(highs).reshape(4, 2, 8, LANES),
        )

    for k in range(3):
        pack(states[k, 0], states[k, 3], k)

    @pl.when(n == 0)
    def _():
        load_first.wait()
        pack(begin[0], begin[3], 3)

    pl.semaphore_wait(barrier, expected)
    start("begin_trace")
    start("first_trace")
    start("begin")
    start("states")

    load_wind.wait()
    for axis in range(3):
        nv[axis] = -wind[axis].astype(jnp.float32).reshape(FIELD)

    for axis in range(3):
        for i in range(2):
            for j in range(2):
                corner = jnp.where(parity == 0, nv[axis, 3 * i, 3 * j, 0], nv[axis, 3 * i, 3 * j, 1])
                shuffle[pl.ds(8 * (2 * i + j), 8)] = corner
        for r in range(ROWS):
            flows[REACH, r, axis] = shuffle[pl.ds(r, 8, stride=4)]
    start("flow")

    cxl = LIFT * jnp.minimum(nv[0, 0], 0.0)
    cxh = LIFT * jnp.minimum(-nv[0, 3], 0.0)
    xli[...] = jnp.where(row > 0, -cxl, 0.0)
    xlh[...] = jnp.where(row == 0, -cxl, 0.0)
    xhi[...] = jnp.where(row < 3, -cxh, 0.0)
    xhh[...] = jnp.where(row == 3, -cxh, 0.0)
    cyl = LIFT * jnp.minimum(nv[1, :, 0], 0.0)
    cyh = LIFT * jnp.minimum(-nv[1, :, 3], 0.0)
    yl[...] = jnp.where(lane >= CZ, -cyl, 0.0)
    yh[...] = jnp.where(lane < LANES - CZ, -cyh, 0.0)
    czl = jnp.where(parity == 0, LIFT * jnp.minimum(nv[2, :, :, 0], 0.0), 0.0)
    czh = jnp.where(parity == 1, LIFT * jnp.minimum(-nv[2, :, :, 1], 0.0), 0.0)
    layer = lane % CZ
    zl[...] = jnp.where(layer > 0, -czl, 0.0)
    zh[...] = jnp.where(layer < CZ - 1, -czh, 0.0)
    diag[:, :, 0] = czl
    diag[:, :, 1] = czh
    diag[0] = diag[0] + cxl
    diag[3] = diag[3] + cxh
    diag[:, 0] = diag[:, 0] + cyl
    diag[:, 3] = diag[:, 3] + cyh

    same = [[split(DER[2 * i, 2 * j], DER[2 * i + 1, 2 * j + 1]) for j in range(2)] for i in range(2)]
    cross = [[split(DER[2 * i, 2 * j + 1], DER[2 * i + 1, 2 * j]) for j in range(2)] for i in range(2)]

    def interior(u, out):
        for b in range(4):
            ub = u[:, b]
            turned = pltpu.roll(ub, 4, 2)
            along_x = jnp.stack([weighted([(DER[a, c], ub[c]) for c in range(4)]) for a in range(4)])
            along_y = weighted([(DER[b, c], ub if c == b else u[:, c]) for c in range(4)])
            along_z = jnp.stack(
                [
                    same[i][0] * ub[:, 0]
                    + cross[i][0] * turned[:, 0]
                    + same[i][1] * ub[:, 1]
                    + cross[i][1] * turned[:, 1]
                    for i in range(2)
                ],
                axis=1,
            )
            total = (
                nv[0, :, b] * along_x
                + nv[1, :, b] * along_y
                + nv[2, :, b] * along_z
                + diag[:, b] * ub
            )
            faces = jnp.stack(
                [
                    zl[:, b] * pltpu.roll(turned[:, 1], 1, 2),
                    zh[:, b] * pltpu.roll(turned[:, 0], LANES - 1, 2),
                ],
                axis=1,
            )
            total = total + faces
            if b == 0:
                total = total + yl[...] * pltpu.roll(u[:, 3], CZ, 3)
            if b == 3:
                total = total + yh[...] * pltpu.roll(u[:, 0], LANES - CZ, 3)
            out[0, b] = total[0] + xli[b] * pltpu.roll(ub[3], 1, 1)
            out[1, b] = total[1]
            out[2, b] = total[2]
            out[3, b] = total[3] + xhi[b] * pltpu.roll(ub[0], 7, 1)

    def finish_rate(out, k_slot):
        low, high = unpack(k_slot)
        lower = out[0] + xlh[...] * low
        upper = out[3] + xhh[...] * high
        out[0] = lower
        out[3] = upper
        return lower, upper

    def old_rate(k, carry):
        interior(states.at[k], rates.at[k])
        return carry

    lax.fori_loop(0, 3, old_rate, 0)
    arrive("states")
    for k in range(3):
        finish_rate(rates.at[k], k)

    base[...] = -DT * rates[0] + (H / 24.0) * (5.0 * rates[0] + 8.0 * rates[1] - rates[2])

    arrive("flow")
    top = (sub // 4) % 2 == 0
    middle = (sub // 2) % 2 == 0
    bottom = sub % 2 == 0
    signs = [jnp.where(bit, jnp.float32(-1.0), jnp.float32(1.0)) for bit in (top, middle, bottom)]
    open_y = jnp.logical_or(jnp.logical_and(middle, lane >= CZ), jnp.logical_and(jnp.logical_not(middle), lane < LANES - CZ))
    open_z = jnp.logical_or(jnp.logical_and(bottom, layer > 0), jnp.logical_and(jnp.logical_not(bottom), layer < CZ - 1))

    def coarse_coefficients(block, carry):
        wide = flows[block]
        center = jnp.ones((ROWS, 8, LANES), jnp.float32)
        for axis in range(3):
            slope = signs[axis] * wide[:, axis]
            jump = jnp.minimum(-slope, 0.0)
            center = center + H * (0.5 * slope + jump)
            coef[1 + axis, block] = (-0.5 * H) * slope
            outer = -H * jump
            if axis == 1:
                outer = jnp.where(open_y, outer, 0.0)
            if axis == 2:
                outer = jnp.where(open_z, outer, 0.0)
            coef[4 + axis, block] = outer
        coef[0, block] = center
        return carry

    lax.fori_loop(0, 2 * REACH + 1, coarse_coefficients, 0)

    def advance(u, low):
        count = u.shape[0]
        own = u[1 : count - 1]
        px = pltpu.roll(u, 4, 1)
        ox = jnp.where(top, px[0 : count - 2], px[2:count])
        px = px[1 : count - 1]
        py = jnp.where(middle, pltpu.roll(own, 6, 1), pltpu.roll(own, 2, 1))
        pz = jnp.where(bottom, pltpu.roll(own, 7, 1), pltpu.roll(own, 1, 1))
        oy = jnp.where(middle, pltpu.roll(py, CZ, 2), pltpu.roll(py, LANES - CZ, 2))
        oz = jnp.where(bottom, pltpu.roll(pz, 1, 2), pltpu.roll(pz, LANES - 1, 2))
        total = None
        for index, value in enumerate((own, px, py, pz, ox, oy, oz)):
            factors = coef[index].reshape(SPAN, 8, LANES)[low + 1 : low + count - 1]
            piece = factors * value
            total = piece if total is None else total + piece
        return total

    res_same = [split(RES[0, 2 * i], RES[1, 2 * i + 1]) for i in range(2)]
    res_cross = [split(RES[0, 2 * i + 1], RES[1, 2 * i]) for i in range(2)]
    pro_same = [split(PRO[2 * i, 0], PRO[2 * i + 1, 1]) for i in range(2)]
    pro_cross = [split(PRO[2 * i, 1], PRO[2 * i + 1, 0]) for i in range(2)]

    def restricted(field):
        for i in range(2):
            lines = weighted([(RES[i, a], field[a]) for a in range(4)])
            for j in range(2):
                pair = weighted([(RES[j, b], lines[b]) for b in range(4)])
                turned = pltpu.roll(pair, 4, 1)
                value = (
                    res_same[0] * pair[0]
                    + res_cross[0] * turned[0]
                    + res_same[1] * pair[1]
                    + res_cross[1] * turned[1]
                )
                shuffle[pl.ds(8 * (2 * i + j), 8)] = value
        return jnp.stack([shuffle[pl.ds(r, 8, stride=4)] for r in range(ROWS)])

    def prolonged(rows):
        for r in range(ROWS):
            shuffle[pl.ds(r, 8, stride=4)] = rows[r]
        corners = []
        for index in range(4):
            value = shuffle[pl.ds(8 * index, 8)]
            turned = pltpu.roll(value, 4, 0)
            corners.append(jnp.stack([pro_same[i] * value + pro_cross[i] * turned for i in range(2)]))
        lines = [
            jnp.stack([weighted([(PRO[b, 0], corners[2 * i]), (PRO[b, 1], corners[2 * i + 1])]) for b in range(4)])
            for i in range(2)
        ]
        return [weighted([(PRO[a, 0], lines[0]), (PRO[a, 1], lines[1])]) for a in range(4)]

    arrive("begin_trace")
    for _, receives, make, _ in transfers["first_trace"]:
        when(receives, lambda make=make: make().wait_recv())
    arrive("begin")
    interior(begin, first_rate)
    lower, upper = finish_rate(first_rate, 3)

    def fine_copy(k, d, slot):
        return remote(
            send.at[k, slot],
            recv.at[1 - k, slot],
            fine_send.at[k, slot],
            fine_recv.at[1 - k, slot],
            (n, s + d),
        )

    def launch(slot):
        for k, d in enumerate((-1, 1)):
            pl.when(has[d])(lambda k=k, d=d: fine_copy(k, d, slot).start())

    def await_fine(slot):
        for k, d in enumerate((-1, 1)):
            pl.when(has[-d])(lambda k=k, d=d: fine_copy(k, d, slot).wait_recv())

    def fresh(u, origin, factor, rate, lower, upper, slot):
        first = origin[0] + factor * lower
        last = origin[3] + factor * upper
        u[0] = first
        u[3] = last
        pack(first, last, slot)
        launch(slot)
        u[1:3] = origin[1:3] + factor * rate[1:3]

    base[...] = base[...] + begin[...]
    fresh(mid_state, base, DT, first_rate, lower, upper, 4)

    def to_closing(slot):
        base[...] = (
            mid_state[...]
            - DT * rates[1]
            + (H / 24.0) * (8.0 * rates[1] + 5.0 * rates[2] - rates[0])
        )
        interior(mid_state, rates.at[1])
        await_fine(slot)
        lower, upper = finish_rate(rates.at[1], slot)
        fresh(end_state, base, DT, rates.at[1], lower, upper, slot + 1)

    to_closing(4)
    rates[0] = first_rate[...]

    old0[1 : ROWS + 1] = restricted(begin)
    start("row0")

    def sweep(index, carry):
        slot = 5 + 2 * index
        base[...] = begin[...] + (H / 24.0) * (5.0 * first_rate[...] + 8.0 * rates[1])
        interior(end_state, rates.at[2])
        await_fine(slot)
        lower, upper = finish_rate(rates.at[2], slot)
        fresh(mid_state, base, -H / 24.0, rates.at[2], lower, upper, slot + 1)
        to_closing(slot + 1)
        return carry

    lax.fori_loop(0, 2, sweep, 0)

    old1[1 : ROWS + 1] = restricted(end_state)
    start("row1")
    arrive("row0")
    low = MID - 1
    before0 = old0[1 : ROWS + 1]
    h_rate0 = advance(old0[...], low) - before0
    interior(end_state, rates.at[2])
    await_fine(9)
    finish_rate(rates.at[2], 9)
    quadrature = restricted(
        [(H / 6.0) * (first_rate[a] + 4.0 * rates[1, a] + rates[2, a]) for a in range(4)]
    )
    arrive("row1")
    before1 = old1[1 : ROWS + 1]
    h_rate1 = advance(old1[...], low) - before1
    trapezoid = 0.5 * (h_rate0 + h_rate1)
    offset = -h_rate0 + trapezoid + (quadrature - trapezoid)
    is_first = n == 0
    offset = offset + jnp.where(is_first, before0 + h_rate0, 0.0)

    group[z, pl.ds(ROWS, ROWS)] = offset
    start("group")
    arrive("group")
    start("side")
    arrive("side")
    y = group[0]
    y = advance(y, MID - 4) + group[1, 1:11]
    y = advance(y, MID - 3) + group[2, 2:10]
    y = advance(y, MID - 2)[1:5] + group[3, 4:8]
    partial[...] = y
    start("part")
    arrive("part")
    y = far[...]
    for step in range(4):
        y = advance(y, step)
    y = y + mid[...]
    for step in range(4, 8):
        y = advance(y, step)
    y = y + near[...]
    for j in range(3):
        count = 12 - 2 * j
        stepped = advance(y, MID - 4 + j) + group[j, j + 1 : 11 - j]
        y = jnp.where(z > j, stepped, y[1 : count - 1])
    finish = advance(y, MID - 1) + group[z, pl.ds(ROWS, ROWS)]
    begin_rows = jnp.where(is_first, before0, y[1:5])
    delta0 = begin_rows - before0
    delta1 = finish - before1

    for index, (delta, field) in enumerate(
        ((delta0, begin), (0.5 * (delta0 + delta1), mid_state), (delta1, end_state))
    ):
        lifted = prolonged(delta)
        for a in range(4):
            result[index, a] = field[a] + lifted[a]
        pltpu.make_async_copy(result.at[index], out_hbm.at[index], store_sem.at[index]).start()
    for index in range(3):
        pltpu.make_async_copy(result.at[index], out_hbm.at[index], store_sem.at[index]).wait()

    for name in transfers:
        sent(name)
    for k, d in enumerate((-1, 1)):
        for slot in range(4, 10):
            pl.when(has[d])(lambda k=k, d=d, slot=slot: fine_copy(k, d, slot).wait_send())


def solution(mesh):
    steps = mesh.shape["tm"]
    columns = mesh.shape["space"]

    def body(node_states, initial_state, velocity):
        states = node_states.reshape((3,) + FIELD)
        first = initial_state.reshape(FIELD)
        wind = velocity.reshape(3, 4, 4, 16, LANES)
        f32 = jnp.float32
        vmem = lambda *shape: pltpu.VMEM(shape, f32)
        dma = lambda *shape: pltpu.SemaphoreType.DMA(shape)
        out = pl.pallas_call(
            functools.partial(kernel, steps, columns),
            out_shape=jax.ShapeDtypeStruct((3,) + FIELD, f32),
            in_specs=[pl.BlockSpec(memory_space=pl.ANY)] * 3,
            out_specs=pl.BlockSpec(memory_space=pl.ANY),
            scratch_shapes=[
                vmem(3, *FIELD),
                pltpu.VMEM((3, 4, 4, 16, LANES), jnp.bfloat16),
                vmem(*FIELD),
                vmem(3, *FIELD),
                vmem(*FIELD),
                vmem(4, 2, 8, LANES),
                vmem(4, 2, 8, LANES),
                vmem(4, 2, 8, LANES),
                vmem(4, 2, 8, LANES),
                vmem(4, 2, 8, LANES),
                vmem(4, 2, 8, LANES),
                vmem(4, 4, 8, LANES),
                vmem(4, 4, 8, LANES),
                vmem(3, *FIELD),
                vmem(*FIELD),
                vmem(*FIELD),
                vmem(*FIELD),
                vmem(*FIELD),
                vmem(2, 10, 2, 8, LANES),
                vmem(2, 10, 2, 8, LANES),
                vmem(32, LANES),
                vmem(2 * REACH + 1, ROWS, 3, 8, LANES),
                vmem(7, 2 * REACH + 1, ROWS, 8, LANES),
                vmem(ROWS + 2, 8, LANES),
                vmem(ROWS + 2, 8, LANES),
                vmem(GROUP, 3 * ROWS, 8, LANES),
                vmem(ROWS, 8, LANES),
                vmem(3 * ROWS, 8, LANES),
                vmem(5 * ROWS, 8, LANES),
                vmem(7 * ROWS, 8, LANES),
                vmem(3, *FIELD),
                dma(3),
                dma(3),
                dma(2, 10),
                dma(2, 10),
                pltpu.SemaphoreType.DMA,
                pltpu.SemaphoreType.DMA,
                dma(6),
                dma(6),
                dma(2, 2),
                dma(2, 2),
                dma(3),
                dma(3),
                dma(2),
                dma(2),
                dma(15),
                dma(15),
            ],
            compiler_params=pltpu.CompilerParams(
                collective_id=0, has_side_effects=True, vmem_limit_bytes=32 * 1024 * 1024
            ),
        )(states, first, wind)
        return out.reshape(1, 3, 64, ROWS, LANES)

    return jax.shard_map(
        body,
        mesh=mesh,
        in_specs=(
            P("tm", None, None, "space", None),
            P(None, "space", None),
            P(None, None, "space", None),
        ),
        out_specs=P("tm", None, None, "space", None),
        check_vma=False,
    )
```

```python
import functools

import jax
import jax.numpy as jnp
import numpy as np
from jax import lax
from jax.experimental import pallas as pl
from jax.experimental.pallas import tpu as pltpu
from jax.sharding import PartitionSpec as P

MESH = pl.DeviceIdType.MESH
CZ = 16
LANES = 128
GROUP = 4
H = 0.08
DT = 0.5 * H
LIFT = 6.0
ROWS = 4
REACH = 3
SPAN = (2 * REACH + 1) * ROWS
MID = REACH * ROWS
FIELD = (4, 4, 2, 8, LANES)


def lagrange_derivative(points):
    number = len(points)
    weights = np.array(
        [1.0 / np.prod([points[i] - points[j] for j in range(number) if j != i]) for i in range(number)]
    )
    derivative = np.zeros((number, number))
    for i in range(number):
        for j in range(number):
            if i != j:
                derivative[i, j] = weights[j] / weights[i] / (points[i] - points[j])
        derivative[i, i] = -np.sum(derivative[i])
    return derivative


POINTS = np.array([-1.0, -1.0 / np.sqrt(5.0), 1.0 / np.sqrt(5.0), 1.0])
WEIGHTS = np.array([1.0, 5.0, 5.0, 1.0]) / 6.0
DER = lagrange_derivative(POINTS)
PRO = np.stack([(1.0 - POINTS) / 2.0, (1.0 + POINTS) / 2.0], axis=1)
RES = PRO.T * WEIGHTS[None, :]


def weighted(terms):
    total = None
    for factor, value in terms:
        factor = float(factor)
        if abs(factor) < 1e-12:
            continue
        piece = value if factor == 1.0 else factor * value
        total = piece if total is None else total + piece
    return total


def kernel(
    steps,
    columns,
    states_hbm,
    start_hbm,
    wind_hbm,
    out_hbm,
    states,
    wind,
    begin,
    nv,
    diag,
    xli,
    xhi,
    xlh,
    xhh,
    yl,
    yh,
    zl,
    zh,
    rates,
    first_rate,
    mid_state,
    end_state,
    base,
    send,
    recv,
    shuffle,
    flows,
    coef,
    old0,
    old1,
    group,
    partial,
    near,
    mid,
    far,
    result,
    load_sem,
    store_sem,
    fine_send,
    fine_recv,
    begin_send,
    begin_recv,
    flow_send,
    flow_recv,
    row_send,
    row_recv,
    group_send,
    group_recv,
    side_send,
    side_recv,
    part_send,
    part_recv,
):
    n = lax.axis_index("tm")
    s = lax.axis_index("space")
    g = n // GROUP
    z = n % GROUP
    groups = steps // GROUP

    sub = lax.broadcasted_iota(jnp.int32, (8, LANES), 0)
    lane = lax.broadcasted_iota(jnp.int32, (8, LANES), 1)
    parity = sub // 4
    row = sub % 4

    def split(even, odd):
        return jnp.where(parity == 0, jnp.float32(even), jnp.float32(odd))

    def remote(src, dst, ssem, rsem, device):
        return pltpu.make_async_remote_copy(
            src_ref=src, dst_ref=dst, send_sem=ssem, recv_sem=rsem, device_id=device, device_id_type=MESH
        )

    has = {-1: s > 0, 1: s < columns - 1}

    def inside(d):
        if d == 0:
            return None
        return s + d >= 0 if d < 0 else s + d < columns

    def both(a, b):
        if a is None:
            return b
        if b is None:
            return a
        return jnp.logical_and(a, b)

    def when(cond, run):
        if cond is None:
            run()
        else:
            pl.when(cond)(run)

    transfers = {}

    def add(name, sends, receives, make, partner):
        transfers.setdefault(name, []).append((sends, receives, make, partner))

    for k, d in enumerate((-1, 1)):
        add(
            "states",
            has[d],
            has[-d],
            functools.partial(
                remote,
                send.at[k, pl.ds(0, 3)],
                recv.at[1 - k, pl.ds(0, 3)],
                fine_send.at[k, 0],
                fine_recv.at[1 - k, 0],
                (n, s + d),
            ),
            None,
        )
        add(
            "begin_trace",
            both(n < steps - 1, has[d]),
            both(n > 0, has[-d]),
            functools.partial(
                remote,
                send.at[k, 2],
                recv.at[1 - k, 3],
                fine_send.at[k, 1],
                fine_recv.at[1 - k, 1],
                (n + 1, s + d),
            ),
            (n - 1, s - d),
        )
        add(
            "first_trace",
            both(n == 0, has[d]),
            both(n == 0, has[-d]),
            functools.partial(
                remote,
                send.at[k, 3],
                recv.at[1 - k, 3],
                fine_send.at[k, 2],
                fine_recv.at[1 - k, 1],
                (n, s + d),
            ),
            None,
        )
        for index, buffer in enumerate((old0, old1)):
            add(
                f"row{index}",
                has[d],
                has[-d],
                functools.partial(
                    remote,
                    buffer.at[1 if d < 0 else ROWS],
                    buffer.at[ROWS + 1 if d < 0 else 0],
                    row_send.at[k, index],
                    row_recv.at[1 - k, index],
                    (n, s + d),
                ),
                None,
            )
        add(
            "side",
            has[d],
            has[-d],
            functools.partial(
                remote,
                group.at[:, pl.ds(ROWS, ROWS)],
                group.at[:, pl.ds(2 * ROWS if d < 0 else 0, ROWS)],
                side_send.at[k],
                side_recv.at[1 - k],
                (n, s + d),
            ),
            None,
        )
    add(
        "begin",
        n < steps - 1,
        n > 0,
        functools.partial(remote, states_hbm.at[2], begin, begin_send, begin_recv, (n + 1, s)),
        (n - 1, s),
    )
    for index, d in enumerate((-3, -2, -1, 1, 2, 3)):
        add(
            "flow",
            inside(d),
            inside(-d),
            functools.partial(
                remote,
                flows.at[REACH],
                flows.at[REACH - d],
                flow_send.at[index],
                flow_recv.at[index],
                (n, s + d),
            ),
            (n, s - d),
        )
    for shift in (1, 2, 3):
        add(
            "group",
            None,
            None,
            functools.partial(
                remote,
                group.at[z, pl.ds(ROWS, ROWS)],
                group.at[z, pl.ds(ROWS, ROWS)],
                group_send.at[shift - 1],
                group_recv.at[shift - 1],
                (g * GROUP + (z + shift) % GROUP, s),
            ),
            (g * GROUP + (z + GROUP - shift) % GROUP, s),
        )
    slot = 0
    for distance, buffer in ((1, near), (2, mid), (3, far)):
        for d in range(-distance, distance + 1):
            add(
                "part",
                both(g + distance < groups, inside(d)),
                both(g >= distance, inside(-d)),
                functools.partial(
                    remote,
                    partial,
                    buffer.at[pl.ds((distance - d) * ROWS, ROWS)],
                    part_send.at[slot],
                    part_recv.at[slot],
                    (n + distance * GROUP, s + d),
                ),
                (n - distance * GROUP, s - d),
            )
            slot += 1

    def start(name):
        for sends, _, make, _ in transfers[name]:
            when(sends, lambda make=make: make().start())

    def arrive(name):
        for _, receives, make, _ in transfers[name]:
            when(receives, lambda make=make: make().wait_recv())

    def sent(name):
        for sends, _, make, _ in transfers[name]:
            when(sends, lambda make=make: make().wait_send())

    load_states = pltpu.make_async_copy(states_hbm, states, load_sem.at[0])
    load_wind = pltpu.make_async_copy(wind_hbm, wind, load_sem.at[1])
    load_first = pltpu.make_async_copy(start_hbm, begin, load_sem.at[2])
    load_states.start()
    load_wind.start()
    pl.when(n == 0)(load_first.start)

    recv[...] = jnp.zeros(recv.shape, jnp.float32)
    flows[...] = jnp.zeros(flows.shape, jnp.float32)
    old0[...] = jnp.zeros(old0.shape, jnp.float32)
    old1[...] = jnp.zeros(old1.shape, jnp.float32)
    group[...] = jnp.zeros(group.shape, jnp.float32)
    near[...] = jnp.zeros(near.shape, jnp.float32)
    mid[...] = jnp.zeros(mid.shape, jnp.float32)
    far[...] = jnp.zeros(far.shape, jnp.float32)

    barrier = pltpu.get_barrier_semaphore()
    expected = jnp.int32(0)

    def greet(cond, device):
        when(
            cond,
            lambda: pl.semaphore_signal(barrier, inc=1, device_id=device, device_id_type=MESH),
        )

    for d in (-1, 1):
        greet(has[d], (n, s + d))
        expected = expected + has[d].astype(jnp.int32)
    for name in ("begin_trace", "begin", "flow", "group", "part"):
        for index, (sends, receives, _, partner) in enumerate(transfers[name]):
            if name == "flow" and index in (2, 3):
                continue
            greet(receives, partner)
            expected = expected + (1 if sends is None else sends.astype(jnp.int32))

    load_states.wait()

    def pack(lower, upper, k_slot):
        for half in range(2):
            low = None
            high = None
            for r in range(4):
                b, hh = (4 * half + r) // 2, r % 2
                lv = lower[b, hh]
                hv = upper[b, hh]
                lv = pltpu.roll(lv, r, 0) if r else lv
                hv = pltpu.roll(hv, (r + 5) % 8, 0) if r != 3 else hv
                low = lv if low is None else jnp.where(row == r, lv, low)
                high = hv if high is None else jnp.where(row == r, hv, high)
            send[0, k_slot, half] = low
            send[1, k_slot, half] = high

    def unpack(k_slot):
        lows, highs = [], []
        for t in range(8):
            half, r = t // 4, t % 4
            lv = recv[0, k_slot, half]
            hv = recv[1, k_slot, half]
            lows.append(pltpu.roll(lv, 8 - r, 0) if r else lv)
            highs.append(pltpu.roll(hv, 3 - r, 0) if r != 3 else hv)
        return (
            jnp.stack(lows).reshape(4, 2, 8, LANES),
            jnp.stack(highs).reshape(4, 2, 8, LANES),
        )

    for k in range(3):
        pack(states[k, 0], states[k, 3], k)

    @pl.when(n == 0)
    def _():
        load_first.wait()
        pack(begin[0], begin[3], 3)

    with jax.named_scope("greet"):
        pl.semaphore_wait(barrier, expected)
        start("begin_trace")
        start("first_trace")
        start("begin")
        start("states")

    load_wind.wait()
    for axis in range(3):
        nv[axis] = -wind[axis].astype(jnp.float32).reshape(FIELD)

    for axis in range(3):
        for i in range(2):
            for j in range(2):
                corner = jnp.where(parity == 0, nv[axis, 3 * i, 3 * j, 0], nv[axis, 3 * i, 3 * j, 1])
                shuffle[pl.ds(8 * (2 * i + j), 8)] = corner
        for r in range(ROWS):
            flows[REACH, r, axis] = shuffle[pl.ds(r, 8, stride=4)]
    start("flow")

    cxl = LIFT * jnp.minimum(nv[0, 0], 0.0)
    cxh = LIFT * jnp.minimum(-nv[0, 3], 0.0)
    xli[...] = jnp.where(row > 0, -cxl, 0.0)
    xlh[...] = jnp.where(row == 0, -cxl, 0.0)
    xhi[...] = jnp.where(row < 3, -cxh, 0.0)
    xhh[...] = jnp.where(row == 3, -cxh, 0.0)
    cyl = LIFT * jnp.minimum(nv[1, :, 0], 0.0)
    cyh = LIFT * jnp.minimum(-nv[1, :, 3], 0.0)
    yl[...] = jnp.where(lane >= CZ, -cyl, 0.0)
    yh[...] = jnp.where(lane < LANES - CZ, -cyh, 0.0)
    czl = jnp.where(parity == 0, LIFT * jnp.minimum(nv[2, :, :, 0], 0.0), 0.0)
    czh = jnp.where(parity == 1, LIFT * jnp.minimum(-nv[2, :, :, 1], 0.0), 0.0)
    layer = lane % CZ
    zl[...] = jnp.where(layer > 0, -czl, 0.0)
    zh[...] = jnp.where(layer < CZ - 1, -czh, 0.0)
    diag[:, :, 0] = czl
    diag[:, :, 1] = czh
    diag[0] = diag[0] + cxl
    diag[3] = diag[3] + cxh
    diag[:, 0] = diag[:, 0] + cyl
    diag[:, 3] = diag[:, 3] + cyh

    same = [[split(DER[2 * i, 2 * j], DER[2 * i + 1, 2 * j + 1]) for j in range(2)] for i in range(2)]
    cross = [[split(DER[2 * i, 2 * j + 1], DER[2 * i + 1, 2 * j]) for j in range(2)] for i in range(2)]

    def interior(u, out):
        for b in range(4):
            ub = u[:, b]
            turned = pltpu.roll(ub, 4, 2)
            along_x = jnp.stack([weighted([(DER[a, c], ub[c]) for c in range(4)]) for a in range(4)])
            along_y = weighted([(DER[b, c], ub if c == b else u[:, c]) for c in range(4)])
            along_z = jnp.stack(
                [
                    same[i][0] * ub[:, 0]
                    + cross[i][0] * turned[:, 0]
                    + same[i][1] * ub[:, 1]
                    + cross[i][1] * turned[:, 1]
                    for i in range(2)
                ],
                axis=1,
            )
            total = (
                nv[0, :, b] * along_x
                + nv[1, :, b] * along_y
                + nv[2, :, b] * along_z
                + diag[:, b] * ub
            )
            faces = jnp.stack(
                [
                    zl[:, b] * pltpu.roll(turned[:, 1], 1, 2),
                    zh[:, b] * pltpu.roll(turned[:, 0], LANES - 1, 2),
                ],
                axis=1,
            )
            total = total + faces
            if b == 0:
                total = total + yl[...] * pltpu.roll(u[:, 3], CZ, 3)
            if b == 3:
                total = total + yh[...] * pltpu.roll(u[:, 0], LANES - CZ, 3)
            out[0, b] = total[0] + xli[b] * pltpu.roll(ub[3], 1, 1)
            out[1, b] = total[1]
            out[2, b] = total[2]
            out[3, b] = total[3] + xhi[b] * pltpu.roll(ub[0], 7, 1)

    def finish_rate(out, k_slot):
        low, high = unpack(k_slot)
        lower = out[0] + xlh[...] * low
        upper = out[3] + xhh[...] * high
        out[0] = lower
        out[3] = upper
        return lower, upper

    def old_rate(k, carry):
        interior(states.at[k], rates.at[k])
        return carry

    with jax.named_scope("old_rates"):
        lax.fori_loop(0, 3, old_rate, 0)
        arrive("states")
        for k in range(3):
            finish_rate(rates.at[k], k)

        base[...] = -DT * rates[0] + (H / 24.0) * (5.0 * rates[0] + 8.0 * rates[1] - rates[2])

    arrive("flow")
    top = (sub // 4) % 2 == 0
    middle = (sub // 2) % 2 == 0
    bottom = sub % 2 == 0
    signs = [jnp.where(bit, jnp.float32(-1.0), jnp.float32(1.0)) for bit in (top, middle, bottom)]
    open_y = jnp.logical_or(jnp.logical_and(middle, lane >= CZ), jnp.logical_and(jnp.logical_not(middle), lane < LANES - CZ))
    open_z = jnp.logical_or(jnp.logical_and(bottom, layer > 0), jnp.logical_and(jnp.logical_not(bottom), layer < CZ - 1))

    def coarse_coefficients(block, carry):
        wide = flows[block]
        center = jnp.ones((ROWS, 8, LANES), jnp.float32)
        for axis in range(3):
            slope = signs[axis] * wide[:, axis]
            jump = jnp.minimum(-slope, 0.0)
            center = center + H * (0.5 * slope + jump)
            coef[1 + axis, block] = (-0.5 * H) * slope
            outer = -H * jump
            if axis == 1:
                outer = jnp.where(open_y, outer, 0.0)
            if axis == 2:
                outer = jnp.where(open_z, outer, 0.0)
            coef[4 + axis, block] = outer
        coef[0, block] = center
        return carry

    lax.fori_loop(0, 2 * REACH + 1, coarse_coefficients, 0)

    def advance(u, low):
        count = u.shape[0]
        own = u[1 : count - 1]
        px = pltpu.roll(u, 4, 1)
        ox = jnp.where(top, px[0 : count - 2], px[2:count])
        px = px[1 : count - 1]
        py = jnp.where(middle, pltpu.roll(own, 6, 1), pltpu.roll(own, 2, 1))
        pz = jnp.where(bottom, pltpu.roll(own, 7, 1), pltpu.roll(own, 1, 1))
        oy = jnp.where(middle, pltpu.roll(py, CZ, 2), pltpu.roll(py, LANES - CZ, 2))
        oz = jnp.where(bottom, pltpu.roll(pz, 1, 2), pltpu.roll(pz, LANES - 1, 2))
        total = None
        for index, value in enumerate((own, px, py, pz, ox, oy, oz)):
            factors = coef[index].reshape(SPAN, 8, LANES)[low + 1 : low + count - 1]
            piece = factors * value
            total = piece if total is None else total + piece
        return total

    res_same = [split(RES[0, 2 * i], RES[1, 2 * i + 1]) for i in range(2)]
    res_cross = [split(RES[0, 2 * i + 1], RES[1, 2 * i]) for i in range(2)]
    pro_same = [split(PRO[2 * i, 0], PRO[2 * i + 1, 1]) for i in range(2)]
    pro_cross = [split(PRO[2 * i, 1], PRO[2 * i + 1, 0]) for i in range(2)]

    def restricted(field):
        for i in range(2):
            lines = weighted([(RES[i, a], field[a]) for a in range(4)])
            for j in range(2):
                pair = weighted([(RES[j, b], lines[b]) for b in range(4)])
                turned = pltpu.roll(pair, 4, 1)
                value = (
                    res_same[0] * pair[0]
                    + res_cross[0] * turned[0]
                    + res_same[1] * pair[1]
                    + res_cross[1] * turned[1]
                )
                shuffle[pl.ds(8 * (2 * i + j), 8)] = value
        return jnp.stack([shuffle[pl.ds(r, 8, stride=4)] for r in range(ROWS)])

    def prolonged(rows):
        for r in range(ROWS):
            shuffle[pl.ds(r, 8, stride=4)] = rows[r]
        corners = []
        for index in range(4):
            value = shuffle[pl.ds(8 * index, 8)]
            turned = pltpu.roll(value, 4, 0)
            corners.append(jnp.stack([pro_same[i] * value + pro_cross[i] * turned for i in range(2)]))
        lines = [
            jnp.stack([weighted([(PRO[b, 0], corners[2 * i]), (PRO[b, 1], corners[2 * i + 1])]) for b in range(4)])
            for i in range(2)
        ]
        return [weighted([(PRO[a, 0], lines[0]), (PRO[a, 1], lines[1])]) for a in range(4)]

    with jax.named_scope("begin_arrives"):
        arrive("begin_trace")
        for _, receives, make, _ in transfers["first_trace"]:
            when(receives, lambda make=make: make().wait_recv())
        arrive("begin")
        interior(begin, first_rate)
        lower, upper = finish_rate(first_rate, 3)

    def fine_copy(k, d, slot):
        return remote(
            send.at[k, slot],
            recv.at[1 - k, slot],
            fine_send.at[k, slot],
            fine_recv.at[1 - k, slot],
            (n, s + d),
        )

    def launch(slot):
        for k, d in enumerate((-1, 1)):
            pl.when(has[d])(lambda k=k, d=d: fine_copy(k, d, slot).start())

    def await_fine(slot):
        for k, d in enumerate((-1, 1)):
            pl.when(has[-d])(lambda k=k, d=d: fine_copy(k, d, slot).wait_recv())

    def fresh(u, origin, factor, rate, lower, upper, slot):
        first = origin[0] + factor * lower
        last = origin[3] + factor * upper
        u[0] = first
        u[3] = last
        pack(first, last, slot)
        launch(slot)
        u[1:3] = origin[1:3] + factor * rate[1:3]

    with jax.named_scope("first_middle"):
        base[...] = base[...] + begin[...]
        fresh(mid_state, base, DT, first_rate, lower, upper, 4)

    def to_closing(slot):
        base[...] = (
            mid_state[...]
            - DT * rates[1]
            + (H / 24.0) * (8.0 * rates[1] + 5.0 * rates[2] - rates[0])
        )
        interior(mid_state, rates.at[1])
        await_fine(slot)
        lower, upper = finish_rate(rates.at[1], slot)
        fresh(end_state, base, DT, rates.at[1], lower, upper, slot + 1)

    with jax.named_scope("first_closing"):
        to_closing(4)
        rates[0] = first_rate[...]

    old0[1 : ROWS + 1] = restricted(begin)
    start("row0")

    def sweep(index, carry):
        slot = 5 + 2 * index
        base[...] = begin[...] + (H / 24.0) * (5.0 * first_rate[...] + 8.0 * rates[1])
        interior(end_state, rates.at[2])
        await_fine(slot)
        lower, upper = finish_rate(rates.at[2], slot)
        fresh(mid_state, base, -H / 24.0, rates.at[2], lower, upper, slot + 1)
        to_closing(slot + 1)
        return carry

    with jax.named_scope("sweeps"):
        lax.fori_loop(0, 2, sweep, 0)

    with jax.named_scope("offset"):
        old1[1 : ROWS + 1] = restricted(end_state)
        start("row1")
        arrive("row0")
        low = MID - 1
        before0 = old0[1 : ROWS + 1]
        h_rate0 = advance(old0[...], low) - before0
        interior(end_state, rates.at[2])
        await_fine(9)
        finish_rate(rates.at[2], 9)
        quadrature = restricted(
            [(H / 6.0) * (first_rate[a] + 4.0 * rates[1, a] + rates[2, a]) for a in range(4)]
        )
        arrive("row1")
        before1 = old1[1 : ROWS + 1]
        h_rate1 = advance(old1[...], low) - before1
        trapezoid = 0.5 * (h_rate0 + h_rate1)
        offset = -h_rate0 + trapezoid + (quadrature - trapezoid)
        is_first = n == 0
        offset = offset + jnp.where(is_first, before0 + h_rate0, 0.0)

    with jax.named_scope("gather_offsets"):
        group[z, pl.ds(ROWS, ROWS)] = offset
        start("group")
        arrive("group")

    with jax.named_scope("side_rows"):
        start("side")
        arrive("side")

    with jax.named_scope("group_sum"):
        y = group[0]
        y = advance(y, MID - 4) + group[1, 1:11]
        y = advance(y, MID - 3) + group[2, 2:10]
        y = advance(y, MID - 2)[1:5] + group[3, 4:8]
        partial[...] = y
        start("part")

    with jax.named_scope("sums_arrive"):
        arrive("part")

    with jax.named_scope("coarse_chain"):
        y = far[...]
        for step in range(4):
            y = advance(y, step)
        y = y + mid[...]
        for step in range(4, 8):
            y = advance(y, step)
        y = y + near[...]
        for j in range(3):
            count = 12 - 2 * j
            stepped = advance(y, MID - 4 + j) + group[j, j + 1 : 11 - j]
            y = jnp.where(z > j, stepped, y[1 : count - 1])
        finish = advance(y, MID - 1) + group[z, pl.ds(ROWS, ROWS)]
        begin_rows = jnp.where(is_first, before0, y[1:5])
        delta0 = begin_rows - before0
        delta1 = finish - before1

    with jax.named_scope("output"):
        for index, (delta, field) in enumerate(
            ((delta0, begin), (0.5 * (delta0 + delta1), mid_state), (delta1, end_state))
        ):
            lifted = prolonged(delta)
            for a in range(4):
                result[index, a] = field[a] + lifted[a]
            pltpu.make_async_copy(result.at[index], out_hbm.at[index], store_sem.at[index]).start()
        for index in range(3):
            pltpu.make_async_copy(result.at[index], out_hbm.at[index], store_sem.at[index]).wait()

    for name in transfers:
        sent(name)
    for k, d in enumerate((-1, 1)):
        for slot in range(4, 10):
            pl.when(has[d])(lambda k=k, d=d, slot=slot: fine_copy(k, d, slot).wait_send())


def solution(mesh):
    steps = mesh.shape["tm"]
    columns = mesh.shape["space"]

    def body(node_states, initial_state, velocity):
        states = node_states.reshape((3,) + FIELD)
        first = initial_state.reshape(FIELD)
        wind = velocity.reshape(3, 4, 4, 16, LANES)
        f32 = jnp.float32
        vmem = lambda *shape: pltpu.VMEM(shape, f32)
        dma = lambda *shape: pltpu.SemaphoreType.DMA(shape)
        out = pl.pallas_call(
            functools.partial(kernel, steps, columns),
            out_shape=jax.ShapeDtypeStruct((3,) + FIELD, f32),
            in_specs=[pl.BlockSpec(memory_space=pltpu.HBM)] * 3,
            out_specs=pl.BlockSpec(memory_space=pl.ANY),
            scratch_shapes=[
                vmem(3, *FIELD),
                pltpu.VMEM((3, 4, 4, 16, LANES), jnp.bfloat16),
                vmem(*FIELD),
                vmem(3, *FIELD),
                vmem(*FIELD),
                vmem(4, 2, 8, LANES),
                vmem(4, 2, 8, LANES),
                vmem(4, 2, 8, LANES),
                vmem(4, 2, 8, LANES),
                vmem(4, 2, 8, LANES),
                vmem(4, 2, 8, LANES),
                vmem(4, 4, 8, LANES),
                vmem(4, 4, 8, LANES),
                vmem(3, *FIELD),
                vmem(*FIELD),
                vmem(*FIELD),
                vmem(*FIELD),
                vmem(*FIELD),
                vmem(2, 10, 2, 8, LANES),
                vmem(2, 10, 2, 8, LANES),
                vmem(32, LANES),
                vmem(2 * REACH + 1, ROWS, 3, 8, LANES),
                vmem(7, 2 * REACH + 1, ROWS, 8, LANES),
                vmem(ROWS + 2, 8, LANES),
                vmem(ROWS + 2, 8, LANES),
                vmem(GROUP, 3 * ROWS, 8, LANES),
                vmem(ROWS, 8, LANES),
                vmem(3 * ROWS, 8, LANES),
                vmem(5 * ROWS, 8, LANES),
                vmem(7 * ROWS, 8, LANES),
                vmem(3, *FIELD),
                dma(3),
                dma(3),
                dma(2, 10),
                dma(2, 10),
                pltpu.SemaphoreType.DMA,
                pltpu.SemaphoreType.DMA,
                dma(6),
                dma(6),
                dma(2, 2),
                dma(2, 2),
                dma(3),
                dma(3),
                dma(2),
                dma(2),
                dma(15),
                dma(15),
            ],
            compiler_params=pltpu.CompilerParams(
                collective_id=0, has_side_effects=True, vmem_limit_bytes=60 * 1024 * 1024
            ),
        )(states, first, wind)
        return out.reshape(1, 3, 64, ROWS, LANES)

    return jax.shard_map(
        body,
        mesh=mesh,
        in_specs=(
            P("tm", None, None, "space", None),
            P(None, "space", None),
            P(None, None, "space", None),
        ),
        out_specs=P("tm", None, None, "space", None),
        check_vma=False,
    )
```

```python
import functools

import jax
import jax.numpy as jnp
import numpy as np
from jax import lax
from jax.experimental import pallas as pl
from jax.experimental.pallas import tpu as pltpu
from jax.sharding import PartitionSpec as P

MESH = pl.DeviceIdType.MESH
CZ = 16
LANES = 128
GROUP = 4
H = 0.08
DT = 0.5 * H
LIFT = 6.0
ROWS = 4
REACH = 3
SPAN = (2 * REACH + 1) * ROWS
MID = REACH * ROWS
FIELD = (4, 4, 2, 8, LANES)


def lagrange_derivative(points):
    number = len(points)
    weights = np.array(
        [1.0 / np.prod([points[i] - points[j] for j in range(number) if j != i]) for i in range(number)]
    )
    derivative = np.zeros((number, number))
    for i in range(number):
        for j in range(number):
            if i != j:
                derivative[i, j] = weights[j] / weights[i] / (points[i] - points[j])
        derivative[i, i] = -np.sum(derivative[i])
    return derivative


POINTS = np.array([-1.0, -1.0 / np.sqrt(5.0), 1.0 / np.sqrt(5.0), 1.0])
WEIGHTS = np.array([1.0, 5.0, 5.0, 1.0]) / 6.0
DER = lagrange_derivative(POINTS)
PRO = np.stack([(1.0 - POINTS) / 2.0, (1.0 + POINTS) / 2.0], axis=1)
RES = PRO.T * WEIGHTS[None, :]


def weighted(terms):
    total = None
    for factor, value in terms:
        factor = float(factor)
        if abs(factor) < 1e-12:
            continue
        piece = value if factor == 1.0 else factor * value
        total = piece if total is None else total + piece
    return total


def kernel(
    steps,
    columns,
    states_hbm,
    start_hbm,
    wind_hbm,
    out_hbm,
    states,
    wind,
    begin,
    nv,
    diag,
    xli,
    xhi,
    xlh,
    xhh,
    yl,
    yh,
    zl,
    zh,
    rates,
    first_rate,
    mid_state,
    end_state,
    base,
    send,
    recv,
    shuffle,
    flows,
    coef,
    old0,
    old1,
    group,
    partial,
    near,
    mid,
    far,
    result,
    load_sem,
    store_sem,
    fine_send,
    fine_recv,
    begin_send,
    begin_recv,
    flow_send,
    flow_recv,
    row_send,
    row_recv,
    group_send,
    group_recv,
    side_send,
    side_recv,
    part_send,
    part_recv,
):
    n = lax.axis_index("tm")
    s = lax.axis_index("space")
    g = n // GROUP
    z = n % GROUP
    groups = steps // GROUP

    sub = lax.broadcasted_iota(jnp.int32, (8, LANES), 0)
    lane = lax.broadcasted_iota(jnp.int32, (8, LANES), 1)
    parity = sub // 4
    row = sub % 4

    def split(even, odd):
        return jnp.where(parity == 0, jnp.float32(even), jnp.float32(odd))

    def remote(src, dst, ssem, rsem, device):
        return pltpu.make_async_remote_copy(
            src_ref=src, dst_ref=dst, send_sem=ssem, recv_sem=rsem, device_id=device, device_id_type=MESH
        )

    has = {-1: s > 0, 1: s < columns - 1}

    def inside(d):
        if d == 0:
            return None
        return s + d >= 0 if d < 0 else s + d < columns

    def both(a, b):
        if a is None:
            return b
        if b is None:
            return a
        return jnp.logical_and(a, b)

    def when(cond, run):
        if cond is None:
            run()
        else:
            pl.when(cond)(run)

    transfers = {}

    def add(name, sends, receives, make, partner):
        transfers.setdefault(name, []).append((sends, receives, make, partner))

    for k, d in enumerate((-1, 1)):
        add(
            "states",
            has[d],
            has[-d],
            functools.partial(
                remote,
                send.at[k, pl.ds(0, 3)],
                recv.at[1 - k, pl.ds(0, 3)],
                fine_send.at[k, 0],
                fine_recv.at[1 - k, 0],
                (n, s + d),
            ),
            None,
        )
        add(
            "begin_trace",
            both(n < steps - 1, has[d]),
            both(n > 0, has[-d]),
            functools.partial(
                remote,
                send.at[k, 2],
                recv.at[1 - k, 3],
                fine_send.at[k, 1],
                fine_recv.at[1 - k, 1],
                (n + 1, s + d),
            ),
            (n - 1, s - d),
        )
        add(
            "first_trace",
            both(n == 0, has[d]),
            both(n == 0, has[-d]),
            functools.partial(
                remote,
                send.at[k, 3],
                recv.at[1 - k, 3],
                fine_send.at[k, 2],
                fine_recv.at[1 - k, 1],
                (n, s + d),
            ),
            None,
        )
        for index, buffer in enumerate((old0, old1)):
            add(
                f"row{index}",
                has[d],
                has[-d],
                functools.partial(
                    remote,
                    buffer.at[1 if d < 0 else ROWS],
                    buffer.at[ROWS + 1 if d < 0 else 0],
                    row_send.at[k, index],
                    row_recv.at[1 - k, index],
                    (n, s + d),
                ),
                None,
            )
        add(
            "side",
            has[d],
            has[-d],
            functools.partial(
                remote,
                group.at[:, pl.ds(ROWS, ROWS)],
                group.at[:, pl.ds(2 * ROWS if d < 0 else 0, ROWS)],
                side_send.at[k],
                side_recv.at[1 - k],
                (n, s + d),
            ),
            None,
        )
    add(
        "begin",
        n < steps - 1,
        n > 0,
        functools.partial(remote, states_hbm.at[2], begin, begin_send, begin_recv, (n + 1, s)),
        (n - 1, s),
    )
    for index, d in enumerate((-3, -2, -1, 1, 2, 3)):
        needed = None if abs(d) == 1 else g >= abs(d)
        add(
            f"flow{abs(d)}",
            both(needed, inside(d)),
            both(needed, inside(-d)),
            functools.partial(
                remote,
                flows.at[REACH],
                flows.at[REACH - d],
                flow_send.at[index],
                flow_recv.at[index],
                (n, s + d),
            ),
            (n, s - d),
        )
    for shift in (1, 2, 3):
        add(
            "group",
            None,
            None,
            functools.partial(
                remote,
                group.at[z, pl.ds(ROWS, ROWS)],
                group.at[z, pl.ds(ROWS, ROWS)],
                group_send.at[shift - 1],
                group_recv.at[shift - 1],
                (g * GROUP + (z + shift) % GROUP, s),
            ),
            (g * GROUP + (z + GROUP - shift) % GROUP, s),
        )
    slot = 0
    for distance, buffer in ((3, far), (2, mid), (1, near)):
        for d in range(-distance, distance + 1):
            add(
                "part",
                both(g + distance < groups, inside(d)),
                both(g >= distance, inside(-d)),
                functools.partial(
                    remote,
                    partial,
                    buffer.at[pl.ds((distance - d) * ROWS, ROWS)],
                    part_send.at[slot],
                    part_recv.at[slot],
                    (n + distance * GROUP, s + d),
                ),
                (n - distance * GROUP, s - d),
            )
            slot += 1

    def start(name):
        for sends, _, make, _ in transfers[name]:
            when(sends, lambda make=make: make().start())

    def arrive(name):
        for _, receives, make, _ in transfers[name]:
            when(receives, lambda make=make: make().wait_recv())

    def sent(name):
        for sends, _, make, _ in transfers[name]:
            when(sends, lambda make=make: make().wait_send())

    load_states = pltpu.make_async_copy(states_hbm, states, load_sem.at[0])
    load_wind = pltpu.make_async_copy(wind_hbm, wind, load_sem.at[1])
    load_first = pltpu.make_async_copy(start_hbm, begin, load_sem.at[2])
    load_states.start()
    load_wind.start()
    pl.when(n == 0)(load_first.start)

    recv[...] = jnp.zeros(recv.shape, jnp.float32)
    flows[...] = jnp.zeros(flows.shape, jnp.float32)
    old0[...] = jnp.zeros(old0.shape, jnp.float32)
    old1[...] = jnp.zeros(old1.shape, jnp.float32)
    group[...] = jnp.zeros(group.shape, jnp.float32)
    near[...] = jnp.zeros(near.shape, jnp.float32)
    mid[...] = jnp.zeros(mid.shape, jnp.float32)
    far[...] = jnp.zeros(far.shape, jnp.float32)

    barrier = pltpu.get_barrier_semaphore()
    expected = jnp.int32(0)

    def greet(cond, device):
        when(
            cond,
            lambda: pl.semaphore_signal(barrier, inc=1, device_id=device, device_id_type=MESH),
        )

    for d in (-1, 1):
        greet(has[d], (n, s + d))
        expected = expected + has[d].astype(jnp.int32)
    for name in ("begin_trace", "begin", "flow2", "flow3", "group", "part"):
        for sends, receives, _, partner in transfers[name]:
            greet(receives, partner)
            expected = expected + (1 if sends is None else sends.astype(jnp.int32))

    load_states.wait()

    def pack(lower, upper, k_slot):
        for half in range(2):
            low = None
            high = None
            for r in range(4):
                b, hh = (4 * half + r) // 2, r % 2
                lv = lower[b, hh]
                hv = upper[b, hh]
                lv = pltpu.roll(lv, r, 0) if r else lv
                hv = pltpu.roll(hv, (r + 5) % 8, 0) if r != 3 else hv
                low = lv if low is None else jnp.where(row == r, lv, low)
                high = hv if high is None else jnp.where(row == r, hv, high)
            send[0, k_slot, half] = low
            send[1, k_slot, half] = high

    def unpack(k_slot):
        lows, highs = [], []
        for t in range(8):
            half, r = t // 4, t % 4
            lv = recv[0, k_slot, half]
            hv = recv[1, k_slot, half]
            lows.append(pltpu.roll(lv, 8 - r, 0) if r else lv)
            highs.append(pltpu.roll(hv, 3 - r, 0) if r != 3 else hv)
        return (
            jnp.stack(lows).reshape(4, 2, 8, LANES),
            jnp.stack(highs).reshape(4, 2, 8, LANES),
        )

    for k in range(3):
        pack(states[k, 0], states[k, 3], k)

    @pl.when(n == 0)
    def _():
        load_first.wait()
        pack(begin[0], begin[3], 3)

    pl.semaphore_wait(barrier, expected)
    start("begin_trace")
    start("first_trace")
    start("begin")
    start("states")

    load_wind.wait()
    for axis in range(3):
        nv[axis] = -wind[axis].astype(jnp.float32).reshape(FIELD)

    for axis in range(3):
        for i in range(2):
            for j in range(2):
                corner = jnp.where(parity == 0, nv[axis, 3 * i, 3 * j, 0], nv[axis, 3 * i, 3 * j, 1])
                shuffle[pl.ds(8 * (2 * i + j), 8)] = corner
        for r in range(ROWS):
            flows[REACH, r, axis] = shuffle[pl.ds(r, 8, stride=4)]

    cxl = LIFT * jnp.minimum(nv[0, 0], 0.0)
    cxh = LIFT * jnp.minimum(-nv[0, 3], 0.0)
    xli[...] = jnp.where(row > 0, -cxl, 0.0)
    xlh[...] = jnp.where(row == 0, -cxl, 0.0)
    xhi[...] = jnp.where(row < 3, -cxh, 0.0)
    xhh[...] = jnp.where(row == 3, -cxh, 0.0)
    cyl = LIFT * jnp.minimum(nv[1, :, 0], 0.0)
    cyh = LIFT * jnp.minimum(-nv[1, :, 3], 0.0)
    yl[...] = jnp.where(lane >= CZ, -cyl, 0.0)
    yh[...] = jnp.where(lane < LANES - CZ, -cyh, 0.0)
    czl = jnp.where(parity == 0, LIFT * jnp.minimum(nv[2, :, :, 0], 0.0), 0.0)
    czh = jnp.where(parity == 1, LIFT * jnp.minimum(-nv[2, :, :, 1], 0.0), 0.0)
    layer = lane % CZ
    zl[...] = jnp.where(layer > 0, -czl, 0.0)
    zh[...] = jnp.where(layer < CZ - 1, -czh, 0.0)
    diag[:, :, 0] = czl
    diag[:, :, 1] = czh
    diag[0] = diag[0] + cxl
    diag[3] = diag[3] + cxh
    diag[:, 0] = diag[:, 0] + cyl
    diag[:, 3] = diag[:, 3] + cyh

    same = [[split(DER[2 * i, 2 * j], DER[2 * i + 1, 2 * j + 1]) for j in range(2)] for i in range(2)]
    cross = [[split(DER[2 * i, 2 * j + 1], DER[2 * i + 1, 2 * j]) for j in range(2)] for i in range(2)]

    def interior(u, out):
        for b in range(4):
            ub = u[:, b]
            turned = pltpu.roll(ub, 4, 2)
            along_x = jnp.stack([weighted([(DER[a, c], ub[c]) for c in range(4)]) for a in range(4)])
            along_y = weighted([(DER[b, c], ub if c == b else u[:, c]) for c in range(4)])
            along_z = jnp.stack(
                [
                    same[i][0] * ub[:, 0]
                    + cross[i][0] * turned[:, 0]
                    + same[i][1] * ub[:, 1]
                    + cross[i][1] * turned[:, 1]
                    for i in range(2)
                ],
                axis=1,
            )
            total = (
                nv[0, :, b] * along_x
                + nv[1, :, b] * along_y
                + nv[2, :, b] * along_z
                + diag[:, b] * ub
            )
            faces = jnp.stack(
                [
                    zl[:, b] * pltpu.roll(turned[:, 1], 1, 2),
                    zh[:, b] * pltpu.roll(turned[:, 0], LANES - 1, 2),
                ],
                axis=1,
            )
            total = total + faces
            if b == 0:
                total = total + yl[...] * pltpu.roll(u[:, 3], CZ, 3)
            if b == 3:
                total = total + yh[...] * pltpu.roll(u[:, 0], LANES - CZ, 3)
            out[0, b] = total[0] + xli[b] * pltpu.roll(ub[3], 1, 1)
            out[1, b] = total[1]
            out[2, b] = total[2]
            out[3, b] = total[3] + xhi[b] * pltpu.roll(ub[0], 7, 1)

    def finish_rate(out, k_slot):
        low, high = unpack(k_slot)
        lower = out[0] + xlh[...] * low
        upper = out[3] + xhh[...] * high
        out[0] = lower
        out[3] = upper
        return lower, upper

    def old_rate(k, carry):
        interior(states.at[k], rates.at[k])
        return carry

    lax.fori_loop(0, 3, old_rate, 0)
    arrive("states")
    for k in range(3):
        finish_rate(rates.at[k], k)

    base[...] = -DT * rates[0] + (H / 24.0) * (5.0 * rates[0] + 8.0 * rates[1] - rates[2])

    top = (sub // 4) % 2 == 0
    middle = (sub // 2) % 2 == 0
    bottom = sub % 2 == 0
    signs = [jnp.where(bit, jnp.float32(-1.0), jnp.float32(1.0)) for bit in (top, middle, bottom)]
    open_y = jnp.logical_or(jnp.logical_and(middle, lane >= CZ), jnp.logical_and(jnp.logical_not(middle), lane < LANES - CZ))
    open_z = jnp.logical_or(jnp.logical_and(bottom, layer > 0), jnp.logical_and(jnp.logical_not(bottom), layer < CZ - 1))

    def coarse_coefficients(block, carry):
        wide = flows[block]
        center = jnp.ones((ROWS, 8, LANES), jnp.float32)
        for axis in range(3):
            slope = signs[axis] * wide[:, axis]
            jump = jnp.minimum(-slope, 0.0)
            center = center + H * (0.5 * slope + jump)
            coef[1 + axis, block] = (-0.5 * H) * slope
            outer = -H * jump
            if axis == 1:
                outer = jnp.where(open_y, outer, 0.0)
            if axis == 2:
                outer = jnp.where(open_z, outer, 0.0)
            coef[4 + axis, block] = outer
        coef[0, block] = center
        return carry

    def advance(u, low):
        count = u.shape[0]
        own = u[1 : count - 1]
        px = pltpu.roll(u, 4, 1)
        ox = jnp.where(top, px[0 : count - 2], px[2:count])
        px = px[1 : count - 1]
        py = jnp.where(middle, pltpu.roll(own, 6, 1), pltpu.roll(own, 2, 1))
        pz = jnp.where(bottom, pltpu.roll(own, 7, 1), pltpu.roll(own, 1, 1))
        oy = jnp.where(middle, pltpu.roll(py, CZ, 2), pltpu.roll(py, LANES - CZ, 2))
        oz = jnp.where(bottom, pltpu.roll(pz, 1, 2), pltpu.roll(pz, LANES - 1, 2))
        total = None
        for index, value in enumerate((own, px, py, pz, ox, oy, oz)):
            factors = coef[index].reshape(SPAN, 8, LANES)[low + 1 : low + count - 1]
            piece = factors * value
            total = piece if total is None else total + piece
        return total

    res_same = [split(RES[0, 2 * i], RES[1, 2 * i + 1]) for i in range(2)]
    res_cross = [split(RES[0, 2 * i + 1], RES[1, 2 * i]) for i in range(2)]
    pro_same = [split(PRO[2 * i, 0], PRO[2 * i + 1, 1]) for i in range(2)]
    pro_cross = [split(PRO[2 * i, 1], PRO[2 * i + 1, 0]) for i in range(2)]

    def restricted(field):
        for i in range(2):
            lines = weighted([(RES[i, a], field[a]) for a in range(4)])
            for j in range(2):
                pair = weighted([(RES[j, b], lines[b]) for b in range(4)])
                turned = pltpu.roll(pair, 4, 1)
                value = (
                    res_same[0] * pair[0]
                    + res_cross[0] * turned[0]
                    + res_same[1] * pair[1]
                    + res_cross[1] * turned[1]
                )
                shuffle[pl.ds(8 * (2 * i + j), 8)] = value
        return jnp.stack([shuffle[pl.ds(r, 8, stride=4)] for r in range(ROWS)])

    def prolonged(rows):
        for r in range(ROWS):
            shuffle[pl.ds(r, 8, stride=4)] = rows[r]
        corners = []
        for index in range(4):
            value = shuffle[pl.ds(8 * index, 8)]
            turned = pltpu.roll(value, 4, 0)
            corners.append(jnp.stack([pro_same[i] * value + pro_cross[i] * turned for i in range(2)]))
        lines = [
            jnp.stack([weighted([(PRO[b, 0], corners[2 * i]), (PRO[b, 1], corners[2 * i + 1])]) for b in range(4)])
            for i in range(2)
        ]
        return [weighted([(PRO[a, 0], lines[0]), (PRO[a, 1], lines[1])]) for a in range(4)]

    arrive("begin_trace")
    for _, receives, make, _ in transfers["first_trace"]:
        when(receives, lambda make=make: make().wait_recv())
    arrive("begin")
    interior(begin, first_rate)
    lower, upper = finish_rate(first_rate, 3)

    def fine_copy(k, d, slot):
        return remote(
            send.at[k, slot],
            recv.at[1 - k, slot],
            fine_send.at[k, slot],
            fine_recv.at[1 - k, slot],
            (n, s + d),
        )

    def launch(slot):
        for k, d in enumerate((-1, 1)):
            pl.when(has[d])(lambda k=k, d=d: fine_copy(k, d, slot).start())

    def await_fine(slot):
        for k, d in enumerate((-1, 1)):
            pl.when(has[-d])(lambda k=k, d=d: fine_copy(k, d, slot).wait_recv())

    def fresh(u, origin, factor, rate, lower, upper, slot):
        first = origin[0] + factor * lower
        last = origin[3] + factor * upper
        u[0] = first
        u[3] = last
        pack(first, last, slot)
        launch(slot)
        u[1:3] = origin[1:3] + factor * rate[1:3]

    base[...] = base[...] + begin[...]
    fresh(mid_state, base, DT, first_rate, lower, upper, 4)

    def to_closing(slot):
        base[...] = (
            mid_state[...]
            - DT * rates[1]
            + (H / 24.0) * (8.0 * rates[1] + 5.0 * rates[2] - rates[0])
        )
        interior(mid_state, rates.at[1])
        await_fine(slot)
        lower, upper = finish_rate(rates.at[1], slot)
        fresh(end_state, base, DT, rates.at[1], lower, upper, slot + 1)

    start("flow1")
    to_closing(4)
    rates[0] = first_rate[...]

    old0[1 : ROWS + 1] = restricted(begin)
    start("row0")
    start("flow2")

    def sweep(index, carry):
        slot = 5 + 2 * index
        base[...] = begin[...] + (H / 24.0) * (5.0 * first_rate[...] + 8.0 * rates[1])
        interior(end_state, rates.at[2])
        await_fine(slot)
        lower, upper = finish_rate(rates.at[2], slot)
        fresh(mid_state, base, -H / 24.0, rates.at[2], lower, upper, slot + 1)
        to_closing(slot + 1)
        return carry

    sweep(0, 0)
    start("flow3")
    sweep(1, 0)

    old1[1 : ROWS + 1] = restricted(end_state)
    start("row1")
    interior(end_state, rates.at[2])
    for name in ("flow1", "flow2", "flow3", "row0"):
        arrive(name)
    lax.fori_loop(0, 2 * REACH + 1, coarse_coefficients, 0)
    low = MID - 1
    before0 = old0[1 : ROWS + 1]
    h_rate0 = advance(old0[...], low) - before0
    await_fine(9)
    finish_rate(rates.at[2], 9)
    quadrature = restricted(
        [(H / 6.0) * (first_rate[a] + 4.0 * rates[1, a] + rates[2, a]) for a in range(4)]
    )
    arrive("row1")
    before1 = old1[1 : ROWS + 1]
    h_rate1 = advance(old1[...], low) - before1
    trapezoid = 0.5 * (h_rate0 + h_rate1)
    offset = -h_rate0 + trapezoid + (quadrature - trapezoid)
    is_first = n == 0
    offset = offset + jnp.where(is_first, before0 + h_rate0, 0.0)

    group[z, pl.ds(ROWS, ROWS)] = offset
    start("group")
    arrive("group")
    start("side")
    arrive("side")
    y = group[0]
    y = advance(y, MID - 4) + group[1, 1:11]
    y = advance(y, MID - 3) + group[2, 2:10]
    y = advance(y, MID - 2)[1:5] + group[3, 4:8]
    partial[...] = y
    start("part")
    arrive("part")
    y = far[...]
    for step in range(4):
        y = advance(y, step)
    y = y + mid[...]
    for step in range(4, 8):
        y = advance(y, step)
    y = y + near[...]
    for j in range(3):
        count = 12 - 2 * j
        stepped = advance(y, MID - 4 + j) + group[j, j + 1 : 11 - j]
        y = jnp.where(z > j, stepped, y[1 : count - 1])
    finish = advance(y, MID - 1) + group[z, pl.ds(ROWS, ROWS)]
    begin_rows = jnp.where(is_first, before0, y[1:5])
    delta0 = begin_rows - before0
    delta1 = finish - before1

    for index, (delta, field) in enumerate(
        ((delta0, begin), (0.5 * (delta0 + delta1), mid_state), (delta1, end_state))
    ):
        lifted = prolonged(delta)
        for a in range(4):
            result[index, a] = field[a] + lifted[a]
        pltpu.make_async_copy(result.at[index], out_hbm.at[index], store_sem.at[index]).start()
    for index in range(3):
        pltpu.make_async_copy(result.at[index], out_hbm.at[index], store_sem.at[index]).wait()

    for name in transfers:
        sent(name)
    for k, d in enumerate((-1, 1)):
        for slot in range(4, 10):
            pl.when(has[d])(lambda k=k, d=d, slot=slot: fine_copy(k, d, slot).wait_send())


def solution(mesh):
    steps = mesh.shape["tm"]
    columns = mesh.shape["space"]

    def body(node_states, initial_state, velocity):
        states = node_states.reshape((3,) + FIELD)
        first = initial_state.reshape(FIELD)
        wind = velocity.reshape(3, 4, 4, 16, LANES)
        f32 = jnp.float32
        vmem = lambda *shape: pltpu.VMEM(shape, f32)
        dma = lambda *shape: pltpu.SemaphoreType.DMA(shape)
        out = pl.pallas_call(
            functools.partial(kernel, steps, columns),
            out_shape=jax.ShapeDtypeStruct((3,) + FIELD, f32),
            in_specs=[pl.BlockSpec(memory_space=pltpu.HBM)] * 3,
            out_specs=pl.BlockSpec(memory_space=pl.ANY),
            scratch_shapes=[
                vmem(3, *FIELD),
                pltpu.VMEM((3, 4, 4, 16, LANES), jnp.bfloat16),
                vmem(*FIELD),
                vmem(3, *FIELD),
                vmem(*FIELD),
                vmem(4, 2, 8, LANES),
                vmem(4, 2, 8, LANES),
                vmem(4, 2, 8, LANES),
                vmem(4, 2, 8, LANES),
                vmem(4, 2, 8, LANES),
                vmem(4, 2, 8, LANES),
                vmem(4, 4, 8, LANES),
                vmem(4, 4, 8, LANES),
                vmem(3, *FIELD),
                vmem(*FIELD),
                vmem(*FIELD),
                vmem(*FIELD),
                vmem(*FIELD),
                vmem(2, 10, 2, 8, LANES),
                vmem(2, 10, 2, 8, LANES),
                vmem(32, LANES),
                vmem(2 * REACH + 1, ROWS, 3, 8, LANES),
                vmem(7, 2 * REACH + 1, ROWS, 8, LANES),
                vmem(ROWS + 2, 8, LANES),
                vmem(ROWS + 2, 8, LANES),
                vmem(GROUP, 3 * ROWS, 8, LANES),
                vmem(ROWS, 8, LANES),
                vmem(3 * ROWS, 8, LANES),
                vmem(5 * ROWS, 8, LANES),
                vmem(7 * ROWS, 8, LANES),
                vmem(3, *FIELD),
                dma(3),
                dma(3),
                dma(2, 10),
                dma(2, 10),
                pltpu.SemaphoreType.DMA,
                pltpu.SemaphoreType.DMA,
                dma(6),
                dma(6),
                dma(2, 2),
                dma(2, 2),
                dma(3),
                dma(3),
                dma(2),
                dma(2),
                dma(15),
                dma(15),
            ],
            compiler_params=pltpu.CompilerParams(
                collective_id=0, has_side_effects=True, vmem_limit_bytes=60 * 1024 * 1024
            ),
        )(states, first, wind)
        return out.reshape(1, 3, 64, ROWS, LANES)

    return jax.shard_map(
        body,
        mesh=mesh,
        in_specs=(
            P("tm", None, None, "space", None),
            P(None, "space", None),
            P(None, None, "space", None),
        ),
        out_specs=P("tm", None, None, "space", None),
        check_vma=False,
    )
```

```python
import functools

import jax
import jax.numpy as jnp
import numpy as np
from jax import lax
from jax.experimental import pallas as pl
from jax.experimental.pallas import tpu as pltpu
from jax.sharding import PartitionSpec as P

MESH = pl.DeviceIdType.MESH
CZ = 16
LANES = 128
GROUP = 4
H = 0.08
DT = 0.5 * H
LIFT = 6.0
ROWS = 4
REACH = 3
SPAN = (2 * REACH + 1) * ROWS
MID = REACH * ROWS
FIELD = (4, 4, 2, 8, LANES)


def lagrange_derivative(points):
    number = len(points)
    weights = np.array(
        [1.0 / np.prod([points[i] - points[j] for j in range(number) if j != i]) for i in range(number)]
    )
    derivative = np.zeros((number, number))
    for i in range(number):
        for j in range(number):
            if i != j:
                derivative[i, j] = weights[j] / weights[i] / (points[i] - points[j])
        derivative[i, i] = -np.sum(derivative[i])
    return derivative


POINTS = np.array([-1.0, -1.0 / np.sqrt(5.0), 1.0 / np.sqrt(5.0), 1.0])
WEIGHTS = np.array([1.0, 5.0, 5.0, 1.0]) / 6.0
DER = lagrange_derivative(POINTS)
PRO = np.stack([(1.0 - POINTS) / 2.0, (1.0 + POINTS) / 2.0], axis=1)
RES = PRO.T * WEIGHTS[None, :]


def weighted(terms):
    total = None
    for factor, value in terms:
        factor = float(factor)
        if abs(factor) < 1e-12:
            continue
        piece = value if factor == 1.0 else factor * value
        total = piece if total is None else total + piece
    return total


def kernel(
    steps,
    columns,
    states_hbm,
    start_hbm,
    wind_hbm,
    out_hbm,
    states,
    wind,
    begin,
    nv,
    diag,
    xli,
    xhi,
    xlh,
    xhh,
    yl,
    yh,
    zl,
    zh,
    rates,
    first_rate,
    mid_state,
    end_state,
    base,
    send,
    recv,
    duo_begin,
    duo_first,
    duo_rates,
    duo_mid,
    duo_end,
    duo_base,
    duo_send,
    duo_recv,
    leaving,
    passed,
    shuffle,
    flows,
    coef,
    old0,
    old1,
    group,
    partial,
    near,
    mid,
    far,
    result,
    load_sem,
    store_sem,
    fine_send,
    fine_recv,
    duo_out,
    duo_in,
    hop_send,
    hop_recv,
    begin_send,
    begin_recv,
    flow_send,
    flow_recv,
    row_send,
    row_recv,
    group_send,
    group_recv,
    side_send,
    side_recv,
    part_send,
    part_recv,
):
    n = lax.axis_index("tm")
    s = lax.axis_index("space")
    g = n // GROUP
    z = n % GROUP
    groups = steps // GROUP

    sub = lax.broadcasted_iota(jnp.int32, (8, LANES), 0)
    lane = lax.broadcasted_iota(jnp.int32, (8, LANES), 1)
    parity = sub // 4
    row = sub % 4

    def split(even, odd):
        return jnp.where(parity == 0, jnp.float32(even), jnp.float32(odd))

    def remote(src, dst, ssem, rsem, device):
        return pltpu.make_async_remote_copy(
            src_ref=src, dst_ref=dst, send_sem=ssem, recv_sem=rsem, device_id=device, device_id_type=MESH
        )

    has = {-1: s > 0, 1: s < columns - 1}

    def inside(d):
        if d == 0:
            return None
        return s + d >= 0 if d < 0 else s + d < columns

    def both(a, b):
        if a is None:
            return b
        if b is None:
            return a
        return jnp.logical_and(a, b)

    def when(cond, run):
        if cond is None:
            run()
        else:
            pl.when(cond)(run)

    transfers = {}

    def add(name, sends, receives, make, partner):
        transfers.setdefault(name, []).append((sends, receives, make, partner))

    for k, d in enumerate((-1, 1)):
        add(
            "states",
            has[d],
            has[-d],
            functools.partial(
                remote,
                send.at[k, pl.ds(0, 3)],
                recv.at[1 - k, pl.ds(0, 3)],
                fine_send.at[k, 0],
                fine_recv.at[1 - k, 0],
                (n, s + d),
            ),
            None,
        )
        add(
            "begin_trace",
            both(n < steps - 1, has[d]),
            both(n > 0, has[-d]),
            functools.partial(
                remote,
                send.at[k, 2],
                recv.at[1 - k, 3],
                fine_send.at[k, 1],
                fine_recv.at[1 - k, 1],
                (n + 1, s + d),
            ),
            (n - 1, s - d),
        )
        add(
            "first_trace",
            both(n == 0, has[d]),
            both(n == 0, has[-d]),
            functools.partial(
                remote,
                send.at[k, 3],
                recv.at[1 - k, 3],
                fine_send.at[k, 2],
                fine_recv.at[1 - k, 1],
                (n, s + d),
            ),
            None,
        )
        for index, buffer in enumerate((old0, old1)):
            add(
                f"row{index}",
                has[d],
                has[-d],
                functools.partial(
                    remote,
                    buffer.at[:, 1 if d < 0 else ROWS],
                    buffer.at[:, ROWS + 1 if d < 0 else 0],
                    row_send.at[k, index],
                    row_recv.at[1 - k, index],
                    (n, s + d),
                ),
                None,
            )
        for shift in range(GROUP):
            part_of = (z + GROUP - shift) % GROUP
            add(
                f"side{shift}",
                has[d],
                has[-d],
                functools.partial(
                    remote,
                    group.at[part_of, pl.ds(ROWS, ROWS)],
                    group.at[part_of, pl.ds(2 * ROWS if d < 0 else 0, ROWS)],
                    side_send.at[k, shift],
                    side_recv.at[1 - k, shift],
                    (n, s + d),
                ),
                None,
            )
    for piece in range(8):
        where_to = (piece // 2, pl.ds(2 * (piece % 2), 2))
        add(
            f"begin{piece}",
            n < steps - 1,
            n > 0,
            functools.partial(
                remote,
                states_hbm.at[(2,) + where_to],
                begin.at[where_to],
                begin_send.at[piece],
                begin_recv.at[piece],
                (n + 1, s),
            ),
            (n - 1, s),
        )
    add(
        "hop",
        n < steps - 1,
        n > 0,
        functools.partial(remote, leaving, passed, hop_send, hop_recv, (n + 1, s)),
        None,
    )
    for index, d in enumerate((-3, -2, -1, 1, 2, 3)):
        needed = None if abs(d) == 1 else g >= abs(d)
        add(
            f"flow{abs(d)}",
            both(needed, inside(d)),
            both(needed, inside(-d)),
            functools.partial(
                remote,
                flows.at[REACH],
                flows.at[REACH - d],
                flow_send.at[index],
                flow_recv.at[index],
                (n, s + d),
            ),
            (n, s - d),
        )
    for shift in (1, 2, 3):
        add(
            "group",
            None,
            None,
            functools.partial(
                remote,
                group.at[z, pl.ds(ROWS, ROWS)],
                group.at[z, pl.ds(ROWS, ROWS)],
                group_send.at[shift - 1],
                group_recv.at[shift - 1],
                (g * GROUP + (z + shift) % GROUP, s),
            ),
            (g * GROUP + (z + GROUP - shift) % GROUP, s),
        )
    slot = 0
    for distance, buffer in ((3, far), (2, mid), (1, near)):
        for d in range(-distance, distance + 1):
            add(
                "part",
                both(g + distance < groups, inside(d)),
                both(g >= distance, inside(-d)),
                functools.partial(
                    remote,
                    partial,
                    buffer.at[pl.ds((distance - d) * ROWS, ROWS)],
                    part_send.at[slot],
                    part_recv.at[slot],
                    (n + distance * GROUP, s + d),
                ),
                (n - distance * GROUP, s - d),
            )
            slot += 1

    def start(name):
        for sends, _, make, _ in transfers[name]:
            when(sends, lambda make=make: make().start())

    def arrive(name):
        for _, receives, make, _ in transfers[name]:
            when(receives, lambda make=make: make().wait_recv())

    def sent(name):
        for sends, _, make, _ in transfers[name]:
            when(sends, lambda make=make: make().wait_send())

    load_states = pltpu.make_async_copy(states_hbm, states, load_sem.at[0])
    load_wind = pltpu.make_async_copy(wind_hbm, wind, load_sem.at[1])
    load_first = pltpu.make_async_copy(start_hbm, begin, load_sem.at[2])
    load_states.start()
    load_wind.start()
    pl.when(n == 0)(load_first.start)

    recv[...] = jnp.zeros(recv.shape, jnp.float32)
    duo_recv[...] = jnp.zeros(duo_recv.shape, jnp.float32)
    passed[...] = jnp.zeros(passed.shape, jnp.float32)
    duo_begin[0] = jnp.zeros(FIELD, jnp.float32)
    duo_first[0] = jnp.zeros(FIELD, jnp.float32)
    flows[...] = jnp.zeros(flows.shape, jnp.float32)
    old0[...] = jnp.zeros(old0.shape, jnp.float32)
    old1[...] = jnp.zeros(old1.shape, jnp.float32)
    group[...] = jnp.zeros(group.shape, jnp.float32)
    near[...] = jnp.zeros(near.shape, jnp.float32)
    mid[...] = jnp.zeros(mid.shape, jnp.float32)
    far[...] = jnp.zeros(far.shape, jnp.float32)

    barrier = pltpu.get_barrier_semaphore()
    expected = jnp.int32(0)

    def greet(cond, device):
        when(
            cond,
            lambda: pl.semaphore_signal(barrier, inc=1, device_id=device, device_id_type=MESH),
        )

    for d in (-1, 1):
        greet(has[d], (n, s + d))
        expected = expected + has[d].astype(jnp.int32)
    for name in ("begin_trace", "begin0", "flow2", "flow3", "group", "part"):
        for sends, receives, _, partner in transfers[name]:
            greet(receives, partner)
            expected = expected + (1 if sends is None else sends.astype(jnp.int32))

    load_states.wait()

    def pack(lower, upper, low_to, high_to):
        for half in range(2):
            low = None
            high = None
            for r in range(4):
                b, hh = (4 * half + r) // 2, r % 2
                lv = lower[b, hh]
                hv = upper[b, hh]
                lv = pltpu.roll(lv, r, 0) if r else lv
                hv = pltpu.roll(hv, (r + 5) % 8, 0) if r != 3 else hv
                low = lv if low is None else jnp.where(row == r, lv, low)
                high = hv if high is None else jnp.where(row == r, hv, high)
            low_to[half] = low
            high_to[half] = high

    def unpack(low_from, high_from):
        lows, highs = [], []
        for t in range(8):
            half, r = t // 4, t % 4
            lv = low_from[half]
            hv = high_from[half]
            lows.append(pltpu.roll(lv, 8 - r, 0) if r else lv)
            highs.append(pltpu.roll(hv, 3 - r, 0) if r != 3 else hv)
        return (
            jnp.stack(lows).reshape(4, 2, 8, LANES),
            jnp.stack(highs).reshape(4, 2, 8, LANES),
        )

    for k in range(3):
        pack(states[k, 0], states[k, 3], send.at[0, k], send.at[1, k])

    @pl.when(n == 0)
    def _():
        load_first.wait()
        pack(begin[0], begin[3], send.at[0, 3], send.at[1, 3])

    pl.semaphore_wait(barrier, expected)
    start("begin_trace")
    start("first_trace")
    start("states")
    start("begin0")
    start("begin1")

    load_wind.wait()
    for axis in range(3):
        nv[axis] = -wind[axis].astype(jnp.float32).reshape(FIELD)

    for axis in range(3):
        for i in range(2):
            for j in range(2):
                corner = jnp.where(parity == 0, nv[axis, 3 * i, 3 * j, 0], nv[axis, 3 * i, 3 * j, 1])
                shuffle[pl.ds(8 * (2 * i + j), 8)] = corner
        for r in range(ROWS):
            flows[REACH, r, axis] = shuffle[pl.ds(r, 8, stride=4)]

    cxl = LIFT * jnp.minimum(nv[0, 0], 0.0)
    cxh = LIFT * jnp.minimum(-nv[0, 3], 0.0)
    xli[...] = jnp.where(row > 0, -cxl, 0.0)
    xlh[...] = jnp.where(row == 0, -cxl, 0.0)
    xhi[...] = jnp.where(row < 3, -cxh, 0.0)
    xhh[...] = jnp.where(row == 3, -cxh, 0.0)
    cyl = LIFT * jnp.minimum(nv[1, :, 0], 0.0)
    cyh = LIFT * jnp.minimum(-nv[1, :, 3], 0.0)
    yl[...] = jnp.where(lane >= CZ, -cyl, 0.0)
    yh[...] = jnp.where(lane < LANES - CZ, -cyh, 0.0)
    czl = jnp.where(parity == 0, LIFT * jnp.minimum(nv[2, :, :, 0], 0.0), 0.0)
    czh = jnp.where(parity == 1, LIFT * jnp.minimum(-nv[2, :, :, 1], 0.0), 0.0)
    layer = lane % CZ
    zl[...] = jnp.where(layer > 0, -czl, 0.0)
    zh[...] = jnp.where(layer < CZ - 1, -czh, 0.0)
    diag[:, :, 0] = czl
    diag[:, :, 1] = czh
    diag[0] = diag[0] + cxl
    diag[3] = diag[3] + cxh
    diag[:, 0] = diag[:, 0] + cyl
    diag[:, 3] = diag[:, 3] + cyh

    same = [[split(DER[2 * i, 2 * j], DER[2 * i + 1, 2 * j + 1]) for j in range(2)] for i in range(2)]
    cross = [[split(DER[2 * i, 2 * j + 1], DER[2 * i + 1, 2 * j]) for j in range(2)] for i in range(2)]

    def interior(u, out):
        for b in range(4):
            ub = u[:, b]
            turned = pltpu.roll(ub, 4, 2)
            along_x = jnp.stack([weighted([(DER[a, c], ub[c]) for c in range(4)]) for a in range(4)])
            along_y = weighted([(DER[b, c], ub if c == b else u[:, c]) for c in range(4)])
            along_z = jnp.stack(
                [
                    same[i][0] * ub[:, 0]
                    + cross[i][0] * turned[:, 0]
                    + same[i][1] * ub[:, 1]
                    + cross[i][1] * turned[:, 1]
                    for i in range(2)
                ],
                axis=1,
            )
            total = (
                nv[0, :, b] * along_x
                + nv[1, :, b] * along_y
                + nv[2, :, b] * along_z
                + diag[:, b] * ub
            )
            faces = jnp.stack(
                [
                    zl[:, b] * pltpu.roll(turned[:, 1], 1, 2),
                    zh[:, b] * pltpu.roll(turned[:, 0], LANES - 1, 2),
                ],
                axis=1,
            )
            total = total + faces
            if b == 0:
                total = total + yl[...] * pltpu.roll(u[:, 3], CZ, 3)
            if b == 3:
                total = total + yh[...] * pltpu.roll(u[:, 0], LANES - CZ, 3)
            out[0, b] = total[0] + xli[b] * pltpu.roll(ub[3], 1, 1)
            out[1, b] = total[1]
            out[2, b] = total[2]
            out[3, b] = total[3] + xhi[b] * pltpu.roll(ub[0], 7, 1)

    def finish_rate(out, low_from, high_from):
        low, high = unpack(low_from, high_from)
        lower = out[0] + xlh[...] * low
        upper = out[3] + xhh[...] * high
        out[0] = lower
        out[3] = upper
        return lower, upper

    def old_rate(k, carry):
        interior(states.at[k], rates.at[k])
        return carry

    lax.fori_loop(0, 3, old_rate, 0)
    arrive("states")
    for k in range(3):
        finish_rate(rates.at[k], recv.at[0, k], recv.at[1, k])

    base[...] = -DT * rates[0] + (H / 24.0) * (5.0 * rates[0] + 8.0 * rates[1] - rates[2])

    top = (sub // 4) % 2 == 0
    middle = (sub // 2) % 2 == 0
    bottom = sub % 2 == 0
    signs = [jnp.where(bit, jnp.float32(-1.0), jnp.float32(1.0)) for bit in (top, middle, bottom)]
    open_y = jnp.logical_or(jnp.logical_and(middle, lane >= CZ), jnp.logical_and(jnp.logical_not(middle), lane < LANES - CZ))
    open_z = jnp.logical_or(jnp.logical_and(bottom, layer > 0), jnp.logical_and(jnp.logical_not(bottom), layer < CZ - 1))

    def coarse_coefficients(block, carry):
        wide = flows[block]
        center = jnp.ones((ROWS, 8, LANES), jnp.float32)
        for axis in range(3):
            slope = signs[axis] * wide[:, axis]
            jump = jnp.minimum(-slope, 0.0)
            center = center + H * (0.5 * slope + jump)
            coef[1 + axis, block] = (-0.5 * H) * slope
            outer = -H * jump
            if axis == 1:
                outer = jnp.where(open_y, outer, 0.0)
            if axis == 2:
                outer = jnp.where(open_z, outer, 0.0)
            coef[4 + axis, block] = outer
        coef[0, block] = center
        return carry

    def advance(u, low):
        count = u.shape[0]
        own = u[1 : count - 1]
        px = pltpu.roll(u, 4, 1)
        ox = jnp.where(top, px[0 : count - 2], px[2:count])
        px = px[1 : count - 1]
        py = jnp.where(middle, pltpu.roll(own, 6, 1), pltpu.roll(own, 2, 1))
        pz = jnp.where(bottom, pltpu.roll(own, 7, 1), pltpu.roll(own, 1, 1))
        oy = jnp.where(middle, pltpu.roll(py, CZ, 2), pltpu.roll(py, LANES - CZ, 2))
        oz = jnp.where(bottom, pltpu.roll(pz, 1, 2), pltpu.roll(pz, LANES - 1, 2))
        total = None
        for index, value in enumerate((own, px, py, pz, ox, oy, oz)):
            factors = coef[index].reshape(SPAN, 8, LANES)[low + 1 : low + count - 1]
            piece = factors * value
            total = piece if total is None else total + piece
        return total

    res_same = [split(RES[0, 2 * i], RES[1, 2 * i + 1]) for i in range(2)]
    res_cross = [split(RES[0, 2 * i + 1], RES[1, 2 * i]) for i in range(2)]
    pro_same = [split(PRO[2 * i, 0], PRO[2 * i + 1, 1]) for i in range(2)]
    pro_cross = [split(PRO[2 * i, 1], PRO[2 * i + 1, 0]) for i in range(2)]

    def restricted(field):
        for i in range(2):
            lines = weighted([(RES[i, a], field[a]) for a in range(4)])
            for j in range(2):
                pair = weighted([(RES[j, b], lines[b]) for b in range(4)])
                turned = pltpu.roll(pair, 4, 1)
                value = (
                    res_same[0] * pair[0]
                    + res_cross[0] * turned[0]
                    + res_same[1] * pair[1]
                    + res_cross[1] * turned[1]
                )
                shuffle[pl.ds(8 * (2 * i + j), 8)] = value
        return jnp.stack([shuffle[pl.ds(r, 8, stride=4)] for r in range(ROWS)])

    def prolonged(rows):
        for r in range(ROWS):
            shuffle[pl.ds(r, 8, stride=4)] = rows[r]
        corners = []
        for index in range(4):
            value = shuffle[pl.ds(8 * index, 8)]
            turned = pltpu.roll(value, 4, 0)
            corners.append(jnp.stack([pro_same[i] * value + pro_cross[i] * turned for i in range(2)]))
        lines = [
            jnp.stack([weighted([(PRO[b, 0], corners[2 * i]), (PRO[b, 1], corners[2 * i + 1])]) for b in range(4)])
            for i in range(2)
        ]
        return [weighted([(PRO[a, 0], lines[0]), (PRO[a, 1], lines[1])]) for a in range(4)]

    coarse_coefficients(REACH, 0)

    @pl.when(n == 0)
    def _():
        for _, receives, make, _ in transfers["first_trace"]:
            when(receives, lambda make=make: make().wait_recv())
        duo_begin[0] = begin[...]
        interior(begin, duo_first.at[0])
        finish_rate(duo_first.at[0], recv.at[0, 3], recv.at[1, 3])

    duo_begin[1] = states[2]
    duo_first[1] = rates[2]
    duo_rates[0] = rates[...]
    duo_rates[1] = jnp.zeros((3,) + FIELD, jnp.float32)

    def duo_copy(k, d, slot):
        return remote(
            duo_send.at[k, slot],
            duo_recv.at[1 - k, slot],
            duo_out.at[k, slot],
            duo_in.at[1 - k, slot],
            (n, s + d),
        )

    def duo_launch(slot):
        for k, d in enumerate((-1, 1)):
            pl.when(has[d])(lambda k=k, d=d: duo_copy(k, d, slot).start())

    def duo_await(slot):
        for k, d in enumerate((-1, 1)):
            pl.when(has[-d])(lambda k=k, d=d: duo_copy(k, d, slot).wait_recv())

    def duo_fresh(target, factor, rate, slot, halo):
        def outer(x, carry):
            if halo is None:
                lower, upper = rate(x)[0], rate(x)[3]
            else:
                lower, upper = finish_rate(rate(x), duo_recv.at[0, halo, x], duo_recv.at[1, halo, x])
            first = duo_base[x, 0] + factor * lower
            last = duo_base[x, 3] + factor * upper
            target[x, 0] = first
            target[x, 3] = last
            pack(first, last, duo_send.at[0, slot, x], duo_send.at[1, slot, x])
            return carry

        def inner(x, carry):
            target[x, 1:3] = duo_base[x, 1:3] + factor * rate(x)[1:3]
            return carry

        lax.fori_loop(0, 2, outer, 0)
        duo_launch(slot)
        lax.fori_loop(0, 2, inner, 0)

    def opening(x, carry):
        duo_base[x] = (
            duo_begin[x]
            - DT * duo_rates[x, 0]
            + (H / 24.0) * (5.0 * duo_rates[x, 0] + 8.0 * duo_rates[x, 1] - duo_rates[x, 2])
        )
        return carry

    lax.fori_loop(0, 2, opening, 0)
    duo_fresh(duo_mid, DT, lambda x: duo_first.at[x], 0, None)
    start("begin2")

    def duo_closing(slot):
        def prepare(x, carry):
            duo_base[x] = (
                duo_mid[x]
                - DT * duo_rates[x, 1]
                + (H / 24.0) * (8.0 * duo_rates[x, 1] + 5.0 * duo_rates[x, 2] - duo_rates[x, 0])
            )
            interior(duo_mid.at[x], duo_rates.at[x, 1])
            return carry

        lax.fori_loop(0, 2, prepare, 0)
        duo_await(slot)
        duo_fresh(duo_end, DT, lambda x: duo_rates.at[x, 1], slot + 1, slot)

    def duo_middle(slot):
        def prepare(x, carry):
            duo_base[x] = duo_begin[x] + (H / 24.0) * (5.0 * duo_first[x] + 8.0 * duo_rates[x, 1])
            interior(duo_end.at[x], duo_rates.at[x, 2])
            return carry

        lax.fori_loop(0, 2, prepare, 0)
        duo_await(slot)
        duo_fresh(duo_mid, -H / 24.0, lambda x: duo_rates.at[x, 2], slot + 1, slot)

    duo_closing(0)
    start("begin3")
    for x in range(2):
        duo_rates[x, 0] = duo_first[x]
        old0[x, 1 : ROWS + 1] = restricted(duo_begin.at[x])
    start("row0")
    start("flow1")
    duo_middle(1)
    start("begin4")
    duo_closing(2)
    start("begin5")
    start("flow2")
    duo_middle(3)
    start("begin6")
    duo_closing(4)
    for x in range(2):
        old1[x, 1 : ROWS + 1] = restricted(duo_end.at[x])
    start("row1")
    start("begin7")

    def last_rate(x, carry):
        interior(duo_end.at[x], duo_rates.at[x, 2])
        return carry

    lax.fori_loop(0, 2, last_rate, 0)
    arrive("row0")
    low = MID - 1
    h_rates0 = [advance(old0[x], low) - old0[x, 1 : ROWS + 1] for x in range(2)]
    duo_await(5)
    offsets = []
    for x in range(2):
        finish_rate(duo_rates.at[x, 2], duo_recv.at[0, 5, x], duo_recv.at[1, 5, x])
    quadratures = [
        restricted(
            [
                (H / 6.0) * (duo_first[x, a] + 4.0 * duo_rates[x, 1, a] + duo_rates[x, 2, a])
                for a in range(4)
            ]
        )
        for x in range(2)
    ]
    arrive("row1")
    for x in (1, 0):
        h_rate0 = h_rates0[x]
        h_rate1 = advance(old1[x], low) - old1[x, 1 : ROWS + 1]
        trapezoid = 0.5 * (h_rate0 + h_rate1)
        offset = -h_rate0 + trapezoid + (quadratures[x] - trapezoid)
        if x == 1:
            leaving[...] = offset
            start("hop")
    is_first = n == 0
    offset = offset + jnp.where(is_first, old0[0, 1 : ROWS + 1] + h_rates0[0], 0.0)

    arrive("begin_trace")
    for piece in range(8):
        arrive(f"begin{piece}")
    interior(begin, first_rate)
    lower, upper = finish_rate(first_rate, recv.at[0, 3], recv.at[1, 3])

    def fine_copy(k, d, slot):
        return remote(
            send.at[k, slot],
            recv.at[1 - k, slot],
            fine_send.at[k, slot],
            fine_recv.at[1 - k, slot],
            (n, s + d),
        )

    def launch(slot):
        for k, d in enumerate((-1, 1)):
            pl.when(has[d])(lambda k=k, d=d: fine_copy(k, d, slot).start())

    def await_fine(slot):
        for k, d in enumerate((-1, 1)):
            pl.when(has[-d])(lambda k=k, d=d: fine_copy(k, d, slot).wait_recv())

    def fresh(u, origin, factor, rate, lower, upper, slot):
        first = origin[0] + factor * lower
        last = origin[3] + factor * upper
        u[0] = first
        u[3] = last
        if slot is not None:
            pack(first, last, send.at[0, slot], send.at[1, slot])
            launch(slot)
        u[1:3] = origin[1:3] + factor * rate[1:3]

    base[...] = base[...] + begin[...]
    fresh(mid_state, base, DT, first_rate, lower, upper, 4)
    start("flow3")

    arrive("hop")
    group[z, pl.ds(ROWS, ROWS)] = offset + passed[...]
    start("group")
    start("side0")

    def to_closing(slot, out_slot):
        base[...] = (
            mid_state[...]
            - DT * rates[1]
            + (H / 24.0) * (8.0 * rates[1] + 5.0 * rates[2] - rates[0])
        )
        interior(mid_state, rates.at[1])
        await_fine(slot)
        lower, upper = finish_rate(rates.at[1], recv.at[0, slot], recv.at[1, slot])
        fresh(end_state, base, DT, rates.at[1], lower, upper, out_slot)

    def to_middle(slot):
        base[...] = begin[...] + (H / 24.0) * (5.0 * first_rate[...] + 8.0 * rates[1])
        interior(end_state, rates.at[2])
        await_fine(slot)
        lower, upper = finish_rate(rates.at[2], recv.at[0, slot], recv.at[1, slot])
        fresh(mid_state, base, -H / 24.0, rates.at[2], lower, upper, slot + 1)

    to_closing(4, 5)
    rates[0] = first_rate[...]
    before0 = restricted(begin)

    to_middle(5)
    for shift in (1, 3, 2):
        make = transfers["group"][shift - 1][2]
        make().wait_recv()
        start(f"side{shift}")
    for name in ("flow1", "flow2", "flow3"):
        arrive(name)
    lax.fori_loop(0, REACH, coarse_coefficients, 0)
    lax.fori_loop(REACH + 1, 2 * REACH + 1, coarse_coefficients, 0)
    to_closing(6, 7)
    for shift in range(GROUP):
        arrive(f"side{shift}")
    y = group[0]
    y = advance(y, MID - 4) + group[1, 1:11]
    y = advance(y, MID - 3) + group[2, 2:10]
    y = advance(y, MID - 2)[1:5] + group[3, 4:8]
    partial[...] = y
    start("part")
    to_middle(7)
    to_closing(8, None)
    before1 = restricted(end_state)
    arrive("part")
    y = far[...]
    for step in range(4):
        y = advance(y, step)
    y = y + mid[...]
    for step in range(4, 8):
        y = advance(y, step)
    y = y + near[...]
    for j in range(3):
        count = 12 - 2 * j
        stepped = advance(y, MID - 4 + j) + group[j, j + 1 : 11 - j]
        y = jnp.where(z > j, stepped, y[1 : count - 1])
    finish = advance(y, MID - 1) + group[z, pl.ds(ROWS, ROWS)]
    begin_rows = jnp.where(is_first, before0, y[1:5])
    delta0 = begin_rows - before0
    delta1 = finish - before1

    for index, (delta, field) in enumerate(
        ((delta0, begin), (0.5 * (delta0 + delta1), mid_state), (delta1, end_state))
    ):
        lifted = prolonged(delta)
        for a in range(4):
            result[index, a] = field[a] + lifted[a]
        pltpu.make_async_copy(result.at[index], out_hbm.at[index], store_sem.at[index]).start()
    for index in range(3):
        pltpu.make_async_copy(result.at[index], out_hbm.at[index], store_sem.at[index]).wait()

    for name in transfers:
        sent(name)
    for k, d in enumerate((-1, 1)):
        for slot in range(4, 9):
            pl.when(has[d])(lambda k=k, d=d, slot=slot: fine_copy(k, d, slot).wait_send())
        for slot in range(6):
            pl.when(has[d])(lambda k=k, d=d, slot=slot: duo_copy(k, d, slot).wait_send())


def solution(mesh):
    steps = mesh.shape["tm"]
    columns = mesh.shape["space"]

    def body(node_states, initial_state, velocity):
        states = node_states.reshape((3,) + FIELD)
        first = initial_state.reshape(FIELD)
        wind = velocity.reshape(3, 4, 4, 16, LANES)
        f32 = jnp.float32
        vmem = lambda *shape: pltpu.VMEM(shape, f32)
        dma = lambda *shape: pltpu.SemaphoreType.DMA(shape)
        out = pl.pallas_call(
            functools.partial(kernel, steps, columns),
            out_shape=jax.ShapeDtypeStruct((3,) + FIELD, f32),
            in_specs=[pl.BlockSpec(memory_space=pltpu.HBM)] * 3,
            out_specs=pl.BlockSpec(memory_space=pl.ANY),
            scratch_shapes=[
                vmem(3, *FIELD),
                pltpu.VMEM((3, 4, 4, 16, LANES), jnp.bfloat16),
                vmem(*FIELD),
                vmem(3, *FIELD),
                vmem(*FIELD),
                vmem(4, 2, 8, LANES),
                vmem(4, 2, 8, LANES),
                vmem(4, 2, 8, LANES),
                vmem(4, 2, 8, LANES),
                vmem(4, 2, 8, LANES),
                vmem(4, 2, 8, LANES),
                vmem(4, 4, 8, LANES),
                vmem(4, 4, 8, LANES),
                vmem(3, *FIELD),
                vmem(*FIELD),
                vmem(*FIELD),
                vmem(*FIELD),
                vmem(*FIELD),
                vmem(2, 9, 2, 8, LANES),
                vmem(2, 9, 2, 8, LANES),
                vmem(2, *FIELD),
                vmem(2, *FIELD),
                vmem(2, 3, *FIELD),
                vmem(2, *FIELD),
                vmem(2, *FIELD),
                vmem(2, *FIELD),
                vmem(2, 6, 2, 2, 8, LANES),
                vmem(2, 6, 2, 2, 8, LANES),
                vmem(ROWS, 8, LANES),
                vmem(ROWS, 8, LANES),
                vmem(32, LANES),
                vmem(2 * REACH + 1, ROWS, 3, 8, LANES),
                vmem(7, 2 * REACH + 1, ROWS, 8, LANES),
                vmem(2, ROWS + 2, 8, LANES),
                vmem(2, ROWS + 2, 8, LANES),
                vmem(GROUP, 3 * ROWS, 8, LANES),
                vmem(ROWS, 8, LANES),
                vmem(3 * ROWS, 8, LANES),
                vmem(5 * ROWS, 8, LANES),
                vmem(7 * ROWS, 8, LANES),
                vmem(3, *FIELD),
                dma(3),
                dma(3),
                dma(2, 9),
                dma(2, 9),
                dma(2, 6),
                dma(2, 6),
                pltpu.SemaphoreType.DMA,
                pltpu.SemaphoreType.DMA,
                dma(8),
                dma(8),
                dma(6),
                dma(6),
                dma(2, 2),
                dma(2, 2),
                dma(3),
                dma(3),
                dma(2, GROUP),
                dma(2, GROUP),
                dma(15),
                dma(15),
            ],
            compiler_params=pltpu.CompilerParams(
                collective_id=0, has_side_effects=True, vmem_limit_bytes=60 * 1024 * 1024
            ),
        )(states, first, wind)
        return out.reshape(1, 3, 64, ROWS, LANES)

    return jax.shard_map(
        body,
        mesh=mesh,
        in_specs=(
            P("tm", None, None, "space", None),
            P(None, "space", None),
            P(None, None, "space", None),
        ),
        out_specs=P("tm", None, None, "space", None),
        check_vma=False,
    )
```

```python
import functools

import jax
import jax.numpy as jnp
import numpy as np
from jax import lax
from jax.experimental import pallas as pl
from jax.experimental.pallas import tpu as pltpu
from jax.sharding import PartitionSpec as P

MESH = pl.DeviceIdType.MESH
CZ = 16
LANES = 128
GROUP = 4
H = 0.08
DT = 0.5 * H
LIFT = 6.0
ROWS = 4
REACH = 1
SPAN = (2 * REACH + 1) * ROWS
MID = REACH * ROWS
FIELD = (4, 4, 2, 8, LANES)


def lagrange_derivative(points):
    number = len(points)
    weights = np.array(
        [1.0 / np.prod([points[i] - points[j] for j in range(number) if j != i]) for i in range(number)]
    )
    derivative = np.zeros((number, number))
    for i in range(number):
        for j in range(number):
            if i != j:
                derivative[i, j] = weights[j] / weights[i] / (points[i] - points[j])
        derivative[i, i] = -np.sum(derivative[i])
    return derivative


POINTS = np.array([-1.0, -1.0 / np.sqrt(5.0), 1.0 / np.sqrt(5.0), 1.0])
WEIGHTS = np.array([1.0, 5.0, 5.0, 1.0]) / 6.0
DER = lagrange_derivative(POINTS)
PRO = np.stack([(1.0 - POINTS) / 2.0, (1.0 + POINTS) / 2.0], axis=1)
RES = PRO.T * WEIGHTS[None, :]


def weighted(terms):
    total = None
    for factor, value in terms:
        factor = float(factor)
        if abs(factor) < 1e-12:
            continue
        piece = value if factor == 1.0 else factor * value
        total = piece if total is None else total + piece
    return total


def kernel(
    steps,
    columns,
    states_hbm,
    start_hbm,
    wind_hbm,
    out_hbm,
    states,
    wind,
    begin,
    nv,
    diag,
    xli,
    xhi,
    xlh,
    xhh,
    yl,
    yh,
    zl,
    zh,
    rates,
    first_rate,
    mid_state,
    end_state,
    base,
    send,
    recv,
    duo_begin,
    duo_first,
    duo_rates,
    duo_mid,
    duo_end,
    duo_base,
    duo_send,
    duo_recv,
    leaving,
    passed,
    shuffle,
    flows,
    coef,
    old0,
    old1,
    group,
    partial,
    near,
    ends,
    result,
    load_sem,
    store_sem,
    fine_send,
    fine_recv,
    duo_out,
    duo_in,
    hop_send,
    hop_recv,
    begin_send,
    begin_recv,
    flow_send,
    flow_recv,
    row_send,
    row_recv,
    group_send,
    group_recv,
    side_send,
    side_recv,
    part_send,
    part_recv,
):
    n = lax.axis_index("tm")
    s = lax.axis_index("space")
    g = n // GROUP
    z = n % GROUP
    groups = steps // GROUP

    sub = lax.broadcasted_iota(jnp.int32, (8, LANES), 0)
    lane = lax.broadcasted_iota(jnp.int32, (8, LANES), 1)
    parity = sub // 4
    row = sub % 4

    def split(even, odd):
        return jnp.where(parity == 0, jnp.float32(even), jnp.float32(odd))

    def remote(src, dst, ssem, rsem, device):
        return pltpu.make_async_remote_copy(
            src_ref=src, dst_ref=dst, send_sem=ssem, recv_sem=rsem, device_id=device, device_id_type=MESH
        )

    has = {-1: s > 0, 1: s < columns - 1}

    def inside(d):
        if d == 0:
            return None
        return s + d >= 0 if d < 0 else s + d < columns

    def both(a, b):
        if a is None:
            return b
        if b is None:
            return a
        return jnp.logical_and(a, b)

    def when(cond, run):
        if cond is None:
            run()
        else:
            pl.when(cond)(run)

    transfers = {}

    def add(name, sends, receives, make, partner):
        transfers.setdefault(name, []).append((sends, receives, make, partner))

    for k, d in enumerate((-1, 1)):
        add(
            "states",
            has[d],
            has[-d],
            functools.partial(
                remote,
                send.at[k, pl.ds(0, 3)],
                recv.at[1 - k, pl.ds(0, 3)],
                fine_send.at[k, 0],
                fine_recv.at[1 - k, 0],
                (n, s + d),
            ),
            None,
        )
        add(
            "begin_trace",
            both(n < steps - 1, has[d]),
            both(n > 0, has[-d]),
            functools.partial(
                remote,
                send.at[k, 2],
                recv.at[1 - k, 3],
                fine_send.at[k, 1],
                fine_recv.at[1 - k, 1],
                (n + 1, s + d),
            ),
            (n - 1, s - d),
        )
        add(
            "first_trace",
            both(n == 0, has[d]),
            both(n == 0, has[-d]),
            functools.partial(
                remote,
                send.at[k, 3],
                recv.at[1 - k, 3],
                fine_send.at[k, 2],
                fine_recv.at[1 - k, 1],
                (n, s + d),
            ),
            None,
        )
        for index, buffer in enumerate((old0, old1)):
            add(
                f"row{index}",
                has[d],
                has[-d],
                functools.partial(
                    remote,
                    buffer.at[:, 1 if d < 0 else ROWS],
                    buffer.at[:, ROWS + 1 if d < 0 else 0],
                    row_send.at[k, index],
                    row_recv.at[1 - k, index],
                    (n, s + d),
                ),
                None,
            )
        for j in range(GROUP - 1):
            rows = 3 - j
            add(
                f"side{j}",
                has[d],
                has[-d],
                functools.partial(
                    remote,
                    group.at[j, pl.ds(ROWS if d < 0 else 2 * ROWS - rows, rows)],
                    group.at[j, pl.ds(2 * ROWS if d < 0 else ROWS - rows, rows)],
                    side_send.at[k, j],
                    side_recv.at[1 - k, j],
                    (n, s + d),
                ),
                None,
            )
    for piece in range(8):
        where_to = (piece // 2, pl.ds(2 * (piece % 2), 2))
        add(
            f"begin{piece}",
            n < steps - 1,
            n > 0,
            functools.partial(
                remote,
                states_hbm.at[(2,) + where_to],
                begin.at[where_to],
                begin_send.at[piece],
                begin_recv.at[piece],
                (n + 1, s),
            ),
            (n - 1, s),
        )
    add(
        "hop",
        n < steps - 1,
        n > 0,
        functools.partial(remote, leaving, passed, hop_send, hop_recv, (n + 1, s)),
        None,
    )
    for index, d in enumerate((-1, 1)):
        edge = pl.ds(0 if d < 0 else 1, ROWS - 1)
        add(
            "flow",
            has[d],
            has[-d],
            functools.partial(
                remote,
                flows.at[REACH, edge],
                flows.at[REACH - d, edge],
                flow_send.at[index],
                flow_recv.at[index],
                (n, s + d),
            ),
            None,
        )
    for shift in (1, 2, 3):
        add(
            "group",
            None,
            None,
            functools.partial(
                remote,
                group.at[z, pl.ds(ROWS, ROWS)],
                group.at[z, pl.ds(ROWS, ROWS)],
                group_send.at[shift - 1],
                group_recv.at[shift - 1],
                (g * GROUP + (z + shift) % GROUP, s),
            ),
            (g * GROUP + (z + GROUP - shift) % GROUP, s),
        )
    for d in (-1, 0, 1):
        add(
            "part",
            both(g < groups - 1, inside(d)),
            both(g > 0, inside(-d)),
            functools.partial(
                remote,
                partial,
                near.at[pl.ds((1 - d) * ROWS, ROWS)],
                part_send.at[d + 1],
                part_recv.at[d + 1],
                (n + GROUP, s + d),
            ),
            (n - GROUP, s - d),
        )

    def start(name):
        for sends, _, make, _ in transfers[name]:
            when(sends, lambda make=make: make().start())

    def arrive(name):
        for _, receives, make, _ in transfers[name]:
            when(receives, lambda make=make: make().wait_recv())

    def sent(name):
        for sends, _, make, _ in transfers[name]:
            when(sends, lambda make=make: make().wait_send())

    load_states = pltpu.make_async_copy(states_hbm, states, load_sem.at[0])
    load_wind = pltpu.make_async_copy(wind_hbm, wind, load_sem.at[1])
    load_first = pltpu.make_async_copy(start_hbm, begin, load_sem.at[2])
    load_states.start()
    load_wind.start()
    pl.when(n == 0)(load_first.start)

    recv[...] = jnp.zeros(recv.shape, jnp.float32)
    duo_recv[...] = jnp.zeros(duo_recv.shape, jnp.float32)
    passed[...] = jnp.zeros(passed.shape, jnp.float32)
    duo_begin[0] = jnp.zeros(FIELD, jnp.float32)
    duo_first[0] = jnp.zeros(FIELD, jnp.float32)
    flows[...] = jnp.zeros(flows.shape, jnp.float32)
    old0[...] = jnp.zeros(old0.shape, jnp.float32)
    old1[...] = jnp.zeros(old1.shape, jnp.float32)
    group[...] = jnp.zeros(group.shape, jnp.float32)
    near[...] = jnp.zeros(near.shape, jnp.float32)

    barrier = pltpu.get_barrier_semaphore()
    expected = jnp.int32(0)

    def greet(cond, device):
        when(
            cond,
            lambda: pl.semaphore_signal(barrier, inc=1, device_id=device, device_id_type=MESH),
        )

    for d in (-1, 1):
        greet(has[d], (n, s + d))
        expected = expected + has[d].astype(jnp.int32)
    for name in ("begin_trace", "begin0", "group", "part"):
        for sends, receives, _, partner in transfers[name]:
            greet(receives, partner)
            expected = expected + (1 if sends is None else sends.astype(jnp.int32))

    load_states.wait()

    def pack(lower, upper, low_to, high_to):
        for half in range(2):
            low = None
            high = None
            for r in range(4):
                b, hh = (4 * half + r) // 2, r % 2
                lv = lower[b, hh]
                hv = upper[b, hh]
                lv = pltpu.roll(lv, r, 0) if r else lv
                hv = pltpu.roll(hv, (r + 5) % 8, 0) if r != 3 else hv
                low = lv if low is None else jnp.where(row == r, lv, low)
                high = hv if high is None else jnp.where(row == r, hv, high)
            low_to[half] = low
            high_to[half] = high

    def unpack(low_from, high_from):
        lows, highs = [], []
        for t in range(8):
            half, r = t // 4, t % 4
            lv = low_from[half]
            hv = high_from[half]
            lows.append(pltpu.roll(lv, 8 - r, 0) if r else lv)
            highs.append(pltpu.roll(hv, 3 - r, 0) if r != 3 else hv)
        return (
            jnp.stack(lows).reshape(4, 2, 8, LANES),
            jnp.stack(highs).reshape(4, 2, 8, LANES),
        )

    for k in range(3):
        pack(states[k, 0], states[k, 3], send.at[0, k], send.at[1, k])

    @pl.when(n == 0)
    def _():
        load_first.wait()
        pack(begin[0], begin[3], send.at[0, 3], send.at[1, 3])

    pl.semaphore_wait(barrier, expected)
    start("begin_trace")
    start("first_trace")
    start("states")
    start("begin0")
    start("begin1")

    load_wind.wait()
    for axis in range(3):
        nv[axis] = -wind[axis].astype(jnp.float32).reshape(FIELD)

    for axis in range(3):
        for i in range(2):
            for j in range(2):
                corner = jnp.where(parity == 0, nv[axis, 3 * i, 3 * j, 0], nv[axis, 3 * i, 3 * j, 1])
                shuffle[pl.ds(8 * (2 * i + j), 8)] = corner
        for r in range(ROWS):
            flows[REACH, r, axis] = shuffle[pl.ds(r, 8, stride=4)]

    cxl = LIFT * jnp.minimum(nv[0, 0], 0.0)
    cxh = LIFT * jnp.minimum(-nv[0, 3], 0.0)
    xli[...] = jnp.where(row > 0, -cxl, 0.0)
    xlh[...] = jnp.where(row == 0, -cxl, 0.0)
    xhi[...] = jnp.where(row < 3, -cxh, 0.0)
    xhh[...] = jnp.where(row == 3, -cxh, 0.0)
    cyl = LIFT * jnp.minimum(nv[1, :, 0], 0.0)
    cyh = LIFT * jnp.minimum(-nv[1, :, 3], 0.0)
    yl[...] = jnp.where(lane >= CZ, -cyl, 0.0)
    yh[...] = jnp.where(lane < LANES - CZ, -cyh, 0.0)
    czl = jnp.where(parity == 0, LIFT * jnp.minimum(nv[2, :, :, 0], 0.0), 0.0)
    czh = jnp.where(parity == 1, LIFT * jnp.minimum(-nv[2, :, :, 1], 0.0), 0.0)
    layer = lane % CZ
    zl[...] = jnp.where(layer > 0, -czl, 0.0)
    zh[...] = jnp.where(layer < CZ - 1, -czh, 0.0)
    diag[:, :, 0] = czl
    diag[:, :, 1] = czh
    diag[0] = diag[0] + cxl
    diag[3] = diag[3] + cxh
    diag[:, 0] = diag[:, 0] + cyl
    diag[:, 3] = diag[:, 3] + cyh

    same = [[split(DER[2 * i, 2 * j], DER[2 * i + 1, 2 * j + 1]) for j in range(2)] for i in range(2)]
    cross = [[split(DER[2 * i, 2 * j + 1], DER[2 * i + 1, 2 * j]) for j in range(2)] for i in range(2)]

    def interior(u, out):
        for b in range(4):
            ub = u[:, b]
            turned = pltpu.roll(ub, 4, 2)
            along_x = jnp.stack([weighted([(DER[a, c], ub[c]) for c in range(4)]) for a in range(4)])
            along_y = weighted([(DER[b, c], ub if c == b else u[:, c]) for c in range(4)])
            along_z = jnp.stack(
                [
                    same[i][0] * ub[:, 0]
                    + cross[i][0] * turned[:, 0]
                    + same[i][1] * ub[:, 1]
                    + cross[i][1] * turned[:, 1]
                    for i in range(2)
                ],
                axis=1,
            )
            total = (
                nv[0, :, b] * along_x
                + nv[1, :, b] * along_y
                + nv[2, :, b] * along_z
                + diag[:, b] * ub
            )
            faces = jnp.stack(
                [
                    zl[:, b] * pltpu.roll(turned[:, 1], 1, 2),
                    zh[:, b] * pltpu.roll(turned[:, 0], LANES - 1, 2),
                ],
                axis=1,
            )
            total = total + faces
            if b == 0:
                total = total + yl[...] * pltpu.roll(u[:, 3], CZ, 3)
            if b == 3:
                total = total + yh[...] * pltpu.roll(u[:, 0], LANES - CZ, 3)
            out[0, b] = total[0] + xli[b] * pltpu.roll(ub[3], 1, 1)
            out[1, b] = total[1]
            out[2, b] = total[2]
            out[3, b] = total[3] + xhi[b] * pltpu.roll(ub[0], 7, 1)

    def finish_rate(out, low_from, high_from):
        low, high = unpack(low_from, high_from)
        lower = out[0] + xlh[...] * low
        upper = out[3] + xhh[...] * high
        out[0] = lower
        out[3] = upper
        return lower, upper

    def old_rate(k, carry):
        interior(states.at[k], rates.at[k])
        return carry

    lax.fori_loop(0, 3, old_rate, 0)
    arrive("states")
    for k in range(3):
        finish_rate(rates.at[k], recv.at[0, k], recv.at[1, k])

    base[...] = -DT * rates[0] + (H / 24.0) * (5.0 * rates[0] + 8.0 * rates[1] - rates[2])

    top = (sub // 4) % 2 == 0
    middle = (sub // 2) % 2 == 0
    bottom = sub % 2 == 0
    signs = [jnp.where(bit, jnp.float32(-1.0), jnp.float32(1.0)) for bit in (top, middle, bottom)]
    open_y = jnp.logical_or(jnp.logical_and(middle, lane >= CZ), jnp.logical_and(jnp.logical_not(middle), lane < LANES - CZ))
    open_z = jnp.logical_or(jnp.logical_and(bottom, layer > 0), jnp.logical_and(jnp.logical_not(bottom), layer < CZ - 1))

    def coarse_coefficients(block, carry):
        wide = flows[block]
        center = jnp.ones((ROWS, 8, LANES), jnp.float32)
        for axis in range(3):
            slope = signs[axis] * wide[:, axis]
            jump = jnp.minimum(-slope, 0.0)
            center = center + H * (0.5 * slope + jump)
            coef[1 + axis, block] = (-0.5 * H) * slope
            outer = -H * jump
            if axis == 1:
                outer = jnp.where(open_y, outer, 0.0)
            if axis == 2:
                outer = jnp.where(open_z, outer, 0.0)
            coef[4 + axis, block] = outer
        coef[0, block] = center
        return carry

    def advance(u, low):
        count = u.shape[0]
        own = u[1 : count - 1]
        px = pltpu.roll(u, 4, 1)
        ox = jnp.where(top, px[0 : count - 2], px[2:count])
        px = px[1 : count - 1]
        py = jnp.where(middle, pltpu.roll(own, 6, 1), pltpu.roll(own, 2, 1))
        pz = jnp.where(bottom, pltpu.roll(own, 7, 1), pltpu.roll(own, 1, 1))
        oy = jnp.where(middle, pltpu.roll(py, CZ, 2), pltpu.roll(py, LANES - CZ, 2))
        oz = jnp.where(bottom, pltpu.roll(pz, 1, 2), pltpu.roll(pz, LANES - 1, 2))
        total = None
        for index, value in enumerate((own, px, py, pz, ox, oy, oz)):
            factors = coef[index].reshape(SPAN, 8, LANES)[low + 1 : low + count - 1]
            piece = factors * value
            total = piece if total is None else total + piece
        return total

    res_same = [split(RES[0, 2 * i], RES[1, 2 * i + 1]) for i in range(2)]
    res_cross = [split(RES[0, 2 * i + 1], RES[1, 2 * i]) for i in range(2)]
    pro_same = [split(PRO[2 * i, 0], PRO[2 * i + 1, 1]) for i in range(2)]
    pro_cross = [split(PRO[2 * i, 1], PRO[2 * i + 1, 0]) for i in range(2)]

    def restricted(field):
        for i in range(2):
            lines = weighted([(RES[i, a], field[a]) for a in range(4)])
            for j in range(2):
                pair = weighted([(RES[j, b], lines[b]) for b in range(4)])
                turned = pltpu.roll(pair, 4, 1)
                value = (
                    res_same[0] * pair[0]
                    + res_cross[0] * turned[0]
                    + res_same[1] * pair[1]
                    + res_cross[1] * turned[1]
                )
                shuffle[pl.ds(8 * (2 * i + j), 8)] = value
        return jnp.stack([shuffle[pl.ds(r, 8, stride=4)] for r in range(ROWS)])

    def prolonged(rows):
        for r in range(ROWS):
            shuffle[pl.ds(r, 8, stride=4)] = rows[r]
        corners = []
        for index in range(4):
            value = shuffle[pl.ds(8 * index, 8)]
            turned = pltpu.roll(value, 4, 0)
            corners.append(jnp.stack([pro_same[i] * value + pro_cross[i] * turned for i in range(2)]))
        lines = [
            jnp.stack([weighted([(PRO[b, 0], corners[2 * i]), (PRO[b, 1], corners[2 * i + 1])]) for b in range(4)])
            for i in range(2)
        ]
        return [weighted([(PRO[a, 0], lines[0]), (PRO[a, 1], lines[1])]) for a in range(4)]

    coarse_coefficients(REACH, 0)

    @pl.when(n == 0)
    def _():
        for _, receives, make, _ in transfers["first_trace"]:
            when(receives, lambda make=make: make().wait_recv())
        duo_begin[0] = begin[...]
        interior(begin, duo_first.at[0])
        finish_rate(duo_first.at[0], recv.at[0, 3], recv.at[1, 3])

    duo_begin[1] = states[2]
    duo_first[1] = rates[2]
    duo_rates[0] = rates[...]
    duo_rates[1] = jnp.zeros((3,) + FIELD, jnp.float32)

    def duo_copy(k, d, slot):
        return remote(
            duo_send.at[k, slot],
            duo_recv.at[1 - k, slot],
            duo_out.at[k, slot],
            duo_in.at[1 - k, slot],
            (n, s + d),
        )

    def duo_launch(slot):
        for k, d in enumerate((-1, 1)):
            pl.when(has[d])(lambda k=k, d=d: duo_copy(k, d, slot).start())

    def duo_await(slot):
        for k, d in enumerate((-1, 1)):
            pl.when(has[-d])(lambda k=k, d=d: duo_copy(k, d, slot).wait_recv())

    def duo_fresh(target, factor, rate, slot, halo):
        def outer(x, carry):
            if halo is None:
                lower, upper = rate(x)[0], rate(x)[3]
            else:
                lower, upper = finish_rate(rate(x), duo_recv.at[0, halo, x], duo_recv.at[1, halo, x])
            first = duo_base[x, 0] + factor * lower
            last = duo_base[x, 3] + factor * upper
            target[x, 0] = first
            target[x, 3] = last
            pack(first, last, duo_send.at[0, slot, x], duo_send.at[1, slot, x])
            return carry

        def inner(x, carry):
            target[x, 1:3] = duo_base[x, 1:3] + factor * rate(x)[1:3]
            return carry

        lax.fori_loop(0, 2, outer, 0)
        duo_launch(slot)
        lax.fori_loop(0, 2, inner, 0)

    def opening(x, carry):
        duo_base[x] = (
            duo_begin[x]
            - DT * duo_rates[x, 0]
            + (H / 24.0) * (5.0 * duo_rates[x, 0] + 8.0 * duo_rates[x, 1] - duo_rates[x, 2])
        )
        return carry

    lax.fori_loop(0, 2, opening, 0)
    duo_fresh(duo_mid, DT, lambda x: duo_first.at[x], 0, None)
    start("begin2")

    def duo_closing(slot):
        def prepare(x, carry):
            duo_base[x] = (
                duo_mid[x]
                - DT * duo_rates[x, 1]
                + (H / 24.0) * (8.0 * duo_rates[x, 1] + 5.0 * duo_rates[x, 2] - duo_rates[x, 0])
            )
            interior(duo_mid.at[x], duo_rates.at[x, 1])
            return carry

        lax.fori_loop(0, 2, prepare, 0)
        duo_await(slot)
        duo_fresh(duo_end, DT, lambda x: duo_rates.at[x, 1], slot + 1, slot)

    def duo_middle(slot):
        def prepare(x, carry):
            duo_base[x] = duo_begin[x] + (H / 24.0) * (5.0 * duo_first[x] + 8.0 * duo_rates[x, 1])
            interior(duo_end.at[x], duo_rates.at[x, 2])
            return carry

        lax.fori_loop(0, 2, prepare, 0)
        duo_await(slot)
        duo_fresh(duo_mid, -H / 24.0, lambda x: duo_rates.at[x, 2], slot + 1, slot)

    duo_closing(0)
    start("begin3")
    for x in range(2):
        duo_rates[x, 0] = duo_first[x]
        old0[x, 1 : ROWS + 1] = restricted(duo_begin.at[x])
    start("row0")
    start("flow")
    duo_middle(1)
    start("begin4")
    duo_closing(2)
    start("begin5")
    duo_middle(3)
    start("begin6")
    duo_closing(4)
    for x in range(2):
        old1[x, 1 : ROWS + 1] = restricted(duo_end.at[x])
    start("row1")
    start("begin7")

    def last_rate(x, carry):
        interior(duo_end.at[x], duo_rates.at[x, 2])
        return carry

    lax.fori_loop(0, 2, last_rate, 0)
    arrive("row0")
    low = MID - 1
    h_rates0 = [advance(old0[x], low) - old0[x, 1 : ROWS + 1] for x in range(2)]
    duo_await(5)
    offsets = []
    for x in range(2):
        finish_rate(duo_rates.at[x, 2], duo_recv.at[0, 5, x], duo_recv.at[1, 5, x])
    quadratures = [
        restricted(
            [
                (H / 6.0) * (duo_first[x, a] + 4.0 * duo_rates[x, 1, a] + duo_rates[x, 2, a])
                for a in range(4)
            ]
        )
        for x in range(2)
    ]
    arrive("row1")
    for x in (1, 0):
        h_rate0 = h_rates0[x]
        h_rate1 = advance(old1[x], low) - old1[x, 1 : ROWS + 1]
        trapezoid = 0.5 * (h_rate0 + h_rate1)
        offset = -h_rate0 + trapezoid + (quadratures[x] - trapezoid)
        if x == 1:
            leaving[...] = offset
            start("hop")
    is_first = n == 0
    offset = offset + jnp.where(is_first, old0[0, 1 : ROWS + 1] + h_rates0[0], 0.0)

    arrive("begin_trace")
    for piece in range(8):
        arrive(f"begin{piece}")
    interior(begin, first_rate)
    lower, upper = finish_rate(first_rate, recv.at[0, 3], recv.at[1, 3])

    def fine_copy(k, d, slot):
        return remote(
            send.at[k, slot],
            recv.at[1 - k, slot],
            fine_send.at[k, slot],
            fine_recv.at[1 - k, slot],
            (n, s + d),
        )

    def launch(slot):
        for k, d in enumerate((-1, 1)):
            pl.when(has[d])(lambda k=k, d=d: fine_copy(k, d, slot).start())

    def await_fine(slot):
        for k, d in enumerate((-1, 1)):
            pl.when(has[-d])(lambda k=k, d=d: fine_copy(k, d, slot).wait_recv())

    def fresh(u, origin, factor, rate, lower, upper, slot):
        first = origin[0] + factor * lower
        last = origin[3] + factor * upper
        u[0] = first
        u[3] = last
        if slot is not None:
            pack(first, last, send.at[0, slot], send.at[1, slot])
            launch(slot)
        u[1:3] = origin[1:3] + factor * rate[1:3]

    base[...] = base[...] + begin[...]
    fresh(mid_state, base, DT, first_rate, lower, upper, 4)

    arrive("hop")
    group[z, pl.ds(ROWS, ROWS)] = offset + passed[...]
    start("group")

    def to_closing(slot, out_slot):
        base[...] = (
            mid_state[...]
            - DT * rates[1]
            + (H / 24.0) * (8.0 * rates[1] + 5.0 * rates[2] - rates[0])
        )
        interior(mid_state, rates.at[1])
        await_fine(slot)
        lower, upper = finish_rate(rates.at[1], recv.at[0, slot], recv.at[1, slot])
        fresh(end_state, base, DT, rates.at[1], lower, upper, out_slot)

    def to_middle(slot):
        base[...] = begin[...] + (H / 24.0) * (5.0 * first_rate[...] + 8.0 * rates[1])
        interior(end_state, rates.at[2])
        await_fine(slot)
        lower, upper = finish_rate(rates.at[2], recv.at[0, slot], recv.at[1, slot])
        fresh(mid_state, base, -H / 24.0, rates.at[2], lower, upper, slot + 1)

    to_closing(4, 5)
    rates[0] = first_rate[...]
    before0 = restricted(begin)

    to_middle(5)
    arrive("flow")
    coarse_coefficients(REACH - 1, 0)
    coarse_coefficients(REACH + 1, 0)
    for j in range(GROUP):

        @pl.when(z != j)
        def _():
            remote(
                group.at[j, pl.ds(ROWS, ROWS)],
                group.at[j, pl.ds(ROWS, ROWS)],
                group_send.at[0],
                group_recv.at[(z + GROUP - 1 - j) % GROUP],
                (n, s),
            ).wait_recv()

        if j < GROUP - 1:
            start(f"side{j}")
    to_closing(6, 7)

    def coarse_chain():
        arrive("part")
        y = near[...]
        line = [y[4:8]]
        for j in range(GROUP):
            y = advance(y, j) + group[j, j + 1 : 11 - j]
            line.append(y[3 - j : 7 - j])
        partial[...] = y
        start("part")
        begin_rows, finish = line[0], line[1]
        for j in range(1, GROUP):
            begin_rows = jnp.where(z == j, line[j], begin_rows)
            finish = jnp.where(z == j, line[j + 1], finish)
        ends[0] = begin_rows
        ends[1] = finish

    for j in range(GROUP - 1):
        arrive(f"side{j}")
    pl.when(g == 0)(coarse_chain)
    to_middle(7)
    to_closing(8, None)
    before1 = restricted(end_state)
    pl.when(g > 0)(coarse_chain)
    begin_rows = jnp.where(is_first, before0, ends[0])
    finish = ends[1]
    delta0 = begin_rows - before0
    delta1 = finish - before1

    for index, (delta, field) in enumerate(
        ((delta0, begin), (0.5 * (delta0 + delta1), mid_state), (delta1, end_state))
    ):
        lifted = prolonged(delta)
        for a in range(4):
            result[index, a] = field[a] + lifted[a]
        pltpu.make_async_copy(result.at[index], out_hbm.at[index], store_sem.at[index]).start()
    for index in range(3):
        pltpu.make_async_copy(result.at[index], out_hbm.at[index], store_sem.at[index]).wait()

    for name in transfers:
        sent(name)
    for k, d in enumerate((-1, 1)):
        for slot in range(4, 9):
            pl.when(has[d])(lambda k=k, d=d, slot=slot: fine_copy(k, d, slot).wait_send())
        for slot in range(6):
            pl.when(has[d])(lambda k=k, d=d, slot=slot: duo_copy(k, d, slot).wait_send())


def solution(mesh):
    steps = mesh.shape["tm"]
    columns = mesh.shape["space"]

    def body(node_states, initial_state, velocity):
        states = node_states.reshape((3,) + FIELD)
        first = initial_state.reshape(FIELD)
        wind = velocity.reshape(3, 4, 4, 16, LANES)
        f32 = jnp.float32
        vmem = lambda *shape: pltpu.VMEM(shape, f32)
        dma = lambda *shape: pltpu.SemaphoreType.DMA(shape)
        out = pl.pallas_call(
            functools.partial(kernel, steps, columns),
            out_shape=jax.ShapeDtypeStruct((3,) + FIELD, f32),
            in_specs=[pl.BlockSpec(memory_space=pltpu.HBM)] * 3,
            out_specs=pl.BlockSpec(memory_space=pl.ANY),
            scratch_shapes=[
                vmem(3, *FIELD),
                pltpu.VMEM((3, 4, 4, 16, LANES), jnp.bfloat16),
                vmem(*FIELD),
                vmem(3, *FIELD),
                vmem(*FIELD),
                vmem(4, 2, 8, LANES),
                vmem(4, 2, 8, LANES),
                vmem(4, 2, 8, LANES),
                vmem(4, 2, 8, LANES),
                vmem(4, 2, 8, LANES),
                vmem(4, 2, 8, LANES),
                vmem(4, 4, 8, LANES),
                vmem(4, 4, 8, LANES),
                vmem(3, *FIELD),
                vmem(*FIELD),
                vmem(*FIELD),
                vmem(*FIELD),
                vmem(*FIELD),
                vmem(2, 9, 2, 8, LANES),
                vmem(2, 9, 2, 8, LANES),
                vmem(2, *FIELD),
                vmem(2, *FIELD),
                vmem(2, 3, *FIELD),
                vmem(2, *FIELD),
                vmem(2, *FIELD),
                vmem(2, *FIELD),
                vmem(2, 6, 2, 2, 8, LANES),
                vmem(2, 6, 2, 2, 8, LANES),
                vmem(ROWS, 8, LANES),
                vmem(ROWS, 8, LANES),
                vmem(32, LANES),
                vmem(2 * REACH + 1, ROWS, 3, 8, LANES),
                vmem(7, 2 * REACH + 1, ROWS, 8, LANES),
                vmem(2, ROWS + 2, 8, LANES),
                vmem(2, ROWS + 2, 8, LANES),
                vmem(GROUP, 3 * ROWS, 8, LANES),
                vmem(ROWS, 8, LANES),
                vmem(3 * ROWS, 8, LANES),
                vmem(2, ROWS, 8, LANES),
                vmem(3, *FIELD),
                dma(3),
                dma(3),
                dma(2, 9),
                dma(2, 9),
                dma(2, 6),
                dma(2, 6),
                pltpu.SemaphoreType.DMA,
                pltpu.SemaphoreType.DMA,
                dma(8),
                dma(8),
                dma(2),
                dma(2),
                dma(2, 2),
                dma(2, 2),
                dma(3),
                dma(3),
                dma(2, GROUP),
                dma(2, GROUP),
                dma(3),
                dma(3),
            ],
            compiler_params=pltpu.CompilerParams(
                collective_id=0, has_side_effects=True, vmem_limit_bytes=60 * 1024 * 1024
            ),
        )(states, first, wind)
        return out.reshape(1, 3, 64, ROWS, LANES)

    return jax.shard_map(
        body,
        mesh=mesh,
        in_specs=(
            P("tm", None, None, "space", None),
            P(None, "space", None),
            P(None, None, "space", None),
        ),
        out_specs=P("tm", None, None, "space", None),
        check_vma=False,
    )
```

```python
import functools

import jax
import jax.numpy as jnp
import numpy as np
from jax import lax
from jax.experimental import pallas as pl
from jax.experimental.pallas import tpu as pltpu
from jax.sharding import PartitionSpec as P

MESH = pl.DeviceIdType.MESH
CZ = 16
LANES = 128
GROUP = 4
H = 0.08
DT = 0.5 * H
LIFT = 6.0
ROWS = 4
REACH = 3
SPAN = (2 * REACH + 1) * ROWS
MID = REACH * ROWS
FIELD = (4, 4, 2, 8, LANES)


def lagrange_derivative(points):
    number = len(points)
    weights = np.array(
        [1.0 / np.prod([points[i] - points[j] for j in range(number) if j != i]) for i in range(number)]
    )
    derivative = np.zeros((number, number))
    for i in range(number):
        for j in range(number):
            if i != j:
                derivative[i, j] = weights[j] / weights[i] / (points[i] - points[j])
        derivative[i, i] = -np.sum(derivative[i])
    return derivative


POINTS = np.array([-1.0, -1.0 / np.sqrt(5.0), 1.0 / np.sqrt(5.0), 1.0])
WEIGHTS = np.array([1.0, 5.0, 5.0, 1.0]) / 6.0
DER = lagrange_derivative(POINTS)
PRO = np.stack([(1.0 - POINTS) / 2.0, (1.0 + POINTS) / 2.0], axis=1)
RES = PRO.T * WEIGHTS[None, :]


def weighted(terms):
    total = None
    for factor, value in terms:
        factor = float(factor)
        if abs(factor) < 1e-12:
            continue
        piece = value if factor == 1.0 else factor * value
        total = piece if total is None else total + piece
    return total


def kernel(
    steps,
    columns,
    states_hbm,
    start_hbm,
    wind_hbm,
    out_hbm,
    states,
    wind,
    begin,
    nv,
    diag,
    xli,
    xhi,
    xlh,
    xhh,
    yl,
    yh,
    zl,
    zh,
    rates,
    first_rate,
    mid_state,
    end_state,
    base,
    send,
    recv,
    duo_begin,
    duo_first,
    duo_rates,
    duo_mid,
    duo_end,
    duo_base,
    duo_send,
    duo_recv,
    leaving,
    passed,
    shuffle,
    flows,
    coef,
    old0,
    old1,
    group,
    partial,
    near,
    mid,
    far,
    result,
    load_sem,
    store_sem,
    fine_send,
    fine_recv,
    duo_out,
    duo_in,
    hop_send,
    hop_recv,
    begin_send,
    begin_recv,
    flow_send,
    flow_recv,
    row_send,
    row_recv,
    group_send,
    group_recv,
    side_send,
    side_recv,
    part_send,
    part_recv,
):
    n = lax.axis_index("tm")
    s = lax.axis_index("space")
    g = n // GROUP
    z = n % GROUP
    groups = steps // GROUP

    sub = lax.broadcasted_iota(jnp.int32, (8, LANES), 0)
    lane = lax.broadcasted_iota(jnp.int32, (8, LANES), 1)
    parity = sub // 4
    row = sub % 4

    def split(even, odd):
        return jnp.where(parity == 0, jnp.float32(even), jnp.float32(odd))

    def remote(src, dst, ssem, rsem, device):
        return pltpu.make_async_remote_copy(
            src_ref=src, dst_ref=dst, send_sem=ssem, recv_sem=rsem, device_id=device, device_id_type=MESH
        )

    has = {-1: s > 0, 1: s < columns - 1}

    def inside(d):
        if d == 0:
            return None
        return s + d >= 0 if d < 0 else s + d < columns

    def both(a, b):
        if a is None:
            return b
        if b is None:
            return a
        return jnp.logical_and(a, b)

    def when(cond, run):
        if cond is None:
            run()
        else:
            pl.when(cond)(run)

    transfers = {}

    def add(name, sends, receives, make, partner):
        transfers.setdefault(name, []).append((sends, receives, make, partner))

    for k, d in enumerate((-1, 1)):
        add(
            "states",
            has[d],
            has[-d],
            functools.partial(
                remote,
                send.at[k, pl.ds(0, 3)],
                recv.at[1 - k, pl.ds(0, 3)],
                fine_send.at[k, 0],
                fine_recv.at[1 - k, 0],
                (n, s + d),
            ),
            None,
        )
        add(
            "begin_trace",
            both(n < steps - 1, has[d]),
            both(n > 0, has[-d]),
            functools.partial(
                remote,
                send.at[k, 2],
                recv.at[1 - k, 3],
                fine_send.at[k, 1],
                fine_recv.at[1 - k, 1],
                (n + 1, s + d),
            ),
            (n - 1, s - d),
        )
        add(
            "first_trace",
            both(n == 0, has[d]),
            both(n == 0, has[-d]),
            functools.partial(
                remote,
                send.at[k, 3],
                recv.at[1 - k, 3],
                fine_send.at[k, 2],
                fine_recv.at[1 - k, 1],
                (n, s + d),
            ),
            None,
        )
        for index, buffer in enumerate((old0, old1)):
            add(
                f"row{index}",
                has[d],
                has[-d],
                functools.partial(
                    remote,
                    buffer.at[:, 1 if d < 0 else ROWS],
                    buffer.at[:, ROWS + 1 if d < 0 else 0],
                    row_send.at[k, index],
                    row_recv.at[1 - k, index],
                    (n, s + d),
                ),
                None,
            )
        for j in range(GROUP - 1):
            rows = 3 - j
            add(
                f"side{j}",
                has[d],
                has[-d],
                functools.partial(
                    remote,
                    group.at[j, pl.ds(ROWS if d < 0 else 2 * ROWS - rows, rows)],
                    group.at[j, pl.ds(2 * ROWS if d < 0 else ROWS - rows, rows)],
                    side_send.at[k, j],
                    side_recv.at[1 - k, j],
                    (n, s + d),
                ),
                None,
            )
    for piece in range(8):
        where_to = (piece // 2, pl.ds(2 * (piece % 2), 2))
        add(
            f"begin{piece}",
            n < steps - 1,
            n > 0,
            functools.partial(
                remote,
                states_hbm.at[(2,) + where_to],
                begin.at[where_to],
                begin_send.at[piece],
                begin_recv.at[piece],
                (n + 1, s),
            ),
            (n - 1, s),
        )
    add(
        "hop",
        n < steps - 1,
        n > 0,
        functools.partial(remote, leaving, passed, hop_send, hop_recv, (n + 1, s)),
        None,
    )
    for index, d in enumerate((-3, -2, -1, 1, 2, 3)):
        needed = None if abs(d) == 1 else g >= abs(d)
        add(
            f"flow{abs(d)}",
            both(needed, inside(d)),
            both(needed, inside(-d)),
            functools.partial(
                remote,
                flows.at[REACH],
                flows.at[REACH - d],
                flow_send.at[index],
                flow_recv.at[index],
                (n, s + d),
            ),
            (n, s - d),
        )
    for shift in (1, 2, 3):
        add(
            "group",
            None,
            None,
            functools.partial(
                remote,
                group.at[z, pl.ds(ROWS, ROWS)],
                group.at[z, pl.ds(ROWS, ROWS)],
                group_send.at[shift - 1],
                group_recv.at[shift - 1],
                (g * GROUP + (z + shift) % GROUP, s),
            ),
            (g * GROUP + (z + GROUP - shift) % GROUP, s),
        )
    slot = 0
    for distance, buffer in ((3, far), (2, mid), (1, near)):
        for d in range(-distance, distance + 1):
            add(
                "part",
                both(g + distance < groups, inside(d)),
                both(g >= distance, inside(-d)),
                functools.partial(
                    remote,
                    partial,
                    buffer.at[pl.ds((distance - d) * ROWS, ROWS)],
                    part_send.at[slot],
                    part_recv.at[slot],
                    (n + distance * GROUP, s + d),
                ),
                (n - distance * GROUP, s - d),
            )
            slot += 1

    def start(name):
        for sends, _, make, _ in transfers[name]:
            when(sends, lambda make=make: make().start())

    def arrive(name):
        for _, receives, make, _ in transfers[name]:
            when(receives, lambda make=make: make().wait_recv())

    def sent(name):
        for sends, _, make, _ in transfers[name]:
            when(sends, lambda make=make: make().wait_send())

    load_states = pltpu.make_async_copy(states_hbm, states, load_sem.at[0])
    load_wind = pltpu.make_async_copy(wind_hbm, wind, load_sem.at[1])
    load_first = pltpu.make_async_copy(start_hbm, begin, load_sem.at[2])
    load_states.start()
    load_wind.start()
    pl.when(n == 0)(load_first.start)

    recv[...] = jnp.zeros(recv.shape, jnp.float32)
    duo_recv[...] = jnp.zeros(duo_recv.shape, jnp.float32)
    passed[...] = jnp.zeros(passed.shape, jnp.float32)
    duo_begin[0] = jnp.zeros(FIELD, jnp.float32)
    duo_first[0] = jnp.zeros(FIELD, jnp.float32)
    flows[...] = jnp.zeros(flows.shape, jnp.float32)
    old0[...] = jnp.zeros(old0.shape, jnp.float32)
    old1[...] = jnp.zeros(old1.shape, jnp.float32)
    group[...] = jnp.zeros(group.shape, jnp.float32)
    near[...] = jnp.zeros(near.shape, jnp.float32)
    mid[...] = jnp.zeros(mid.shape, jnp.float32)
    far[...] = jnp.zeros(far.shape, jnp.float32)

    barrier = pltpu.get_barrier_semaphore()
    expected = jnp.int32(0)

    def greet(cond, device):
        when(
            cond,
            lambda: pl.semaphore_signal(barrier, inc=1, device_id=device, device_id_type=MESH),
        )

    for d in (-1, 1):
        greet(has[d], (n, s + d))
        expected = expected + has[d].astype(jnp.int32)
    for name in ("begin_trace", "begin0", "flow2", "flow3", "group", "part"):
        for sends, receives, _, partner in transfers[name]:
            greet(receives, partner)
            expected = expected + (1 if sends is None else sends.astype(jnp.int32))

    load_states.wait()

    def pack(lower, upper, low_to, high_to):
        for half in range(2):
            low = None
            high = None
            for r in range(4):
                b, hh = (4 * half + r) // 2, r % 2
                lv = lower[b, hh]
                hv = upper[b, hh]
                lv = pltpu.roll(lv, r, 0) if r else lv
                hv = pltpu.roll(hv, (r + 5) % 8, 0) if r != 3 else hv
                low = lv if low is None else jnp.where(row == r, lv, low)
                high = hv if high is None else jnp.where(row == r, hv, high)
            low_to[half] = low
            high_to[half] = high

    def unpack(low_from, high_from):
        lows, highs = [], []
        for t in range(8):
            half, r = t // 4, t % 4
            lv = low_from[half]
            hv = high_from[half]
            lows.append(pltpu.roll(lv, 8 - r, 0) if r else lv)
            highs.append(pltpu.roll(hv, 3 - r, 0) if r != 3 else hv)
        return (
            jnp.stack(lows).reshape(4, 2, 8, LANES),
            jnp.stack(highs).reshape(4, 2, 8, LANES),
        )

    for k in range(3):
        pack(states[k, 0], states[k, 3], send.at[0, k], send.at[1, k])

    @pl.when(n == 0)
    def _():
        load_first.wait()
        pack(begin[0], begin[3], send.at[0, 3], send.at[1, 3])

    pl.semaphore_wait(barrier, expected)
    start("begin_trace")
    start("first_trace")
    start("states")
    start("begin0")
    start("begin1")
    start("begin2")

    load_wind.wait()
    for axis in range(3):
        nv[axis] = -wind[axis].astype(jnp.float32).reshape(FIELD)

    for axis in range(3):
        for i in range(2):
            for j in range(2):
                corner = jnp.where(parity == 0, nv[axis, 3 * i, 3 * j, 0], nv[axis, 3 * i, 3 * j, 1])
                shuffle[pl.ds(8 * (2 * i + j), 8)] = corner
        for r in range(ROWS):
            flows[REACH, r, axis] = shuffle[pl.ds(r, 8, stride=4)]

    cxl = LIFT * jnp.minimum(nv[0, 0], 0.0)
    cxh = LIFT * jnp.minimum(-nv[0, 3], 0.0)
    xli[...] = jnp.where(row > 0, -cxl, 0.0)
    xlh[...] = jnp.where(row == 0, -cxl, 0.0)
    xhi[...] = jnp.where(row < 3, -cxh, 0.0)
    xhh[...] = jnp.where(row == 3, -cxh, 0.0)
    cyl = LIFT * jnp.minimum(nv[1, :, 0], 0.0)
    cyh = LIFT * jnp.minimum(-nv[1, :, 3], 0.0)
    yl[...] = jnp.where(lane >= CZ, -cyl, 0.0)
    yh[...] = jnp.where(lane < LANES - CZ, -cyh, 0.0)
    czl = jnp.where(parity == 0, LIFT * jnp.minimum(nv[2, :, :, 0], 0.0), 0.0)
    czh = jnp.where(parity == 1, LIFT * jnp.minimum(-nv[2, :, :, 1], 0.0), 0.0)
    layer = lane % CZ
    zl[...] = jnp.where(layer > 0, -czl, 0.0)
    zh[...] = jnp.where(layer < CZ - 1, -czh, 0.0)
    diag[:, :, 0] = czl
    diag[:, :, 1] = czh
    diag[0] = diag[0] + cxl
    diag[3] = diag[3] + cxh
    diag[:, 0] = diag[:, 0] + cyl
    diag[:, 3] = diag[:, 3] + cyh

    same = [[split(DER[2 * i, 2 * j], DER[2 * i + 1, 2 * j + 1]) for j in range(2)] for i in range(2)]
    cross = [[split(DER[2 * i, 2 * j + 1], DER[2 * i + 1, 2 * j]) for j in range(2)] for i in range(2)]

    def interior(u, out):
        for b in range(4):
            pair = [u[:, b, 0], u[:, b, 1]]
            turned = [pltpu.roll(half, 4, 1) for half in pair]
            for i in range(2):
                own = pair[i]
                along_z = (
                    same[i][0] * pair[0]
                    + cross[i][0] * turned[0]
                    + same[i][1] * pair[1]
                    + cross[i][1] * turned[1]
                )
                total = diag[:, b, i] * own + nv[2, :, b, i] * along_z
                if i == 0:
                    total = total + zl[:, b] * pltpu.roll(turned[1], 1, 2)
                else:
                    total = total + zh[:, b] * pltpu.roll(turned[0], LANES - 1, 2)
                others = [own if c == b else u[:, c, i] for c in range(4)]
                along_y = weighted([(DER[b, c], others[c]) for c in range(4)])
                total = total + nv[1, :, b, i] * along_y
                if b == 0:
                    total = total + yl[:, i] * pltpu.roll(others[3], CZ, 2)
                if b == 3:
                    total = total + yh[:, i] * pltpu.roll(others[0], LANES - CZ, 2)
                along_x = jnp.stack([weighted([(DER[a, c], own[c]) for c in range(4)]) for a in range(4)])
                total = total + nv[0, :, b, i] * along_x
                out[0, b, i] = total[0] + xli[b, i] * pltpu.roll(own[3], 1, 0)
                out[1:3, b, i] = total[1:3]
                out[3, b, i] = total[3] + xhi[b, i] * pltpu.roll(own[0], 7, 0)

    def finish_rate(out, low_from, high_from):
        low, high = unpack(low_from, high_from)
        lower = out[0] + xlh[...] * low
        upper = out[3] + xhh[...] * high
        out[0] = lower
        out[3] = upper
        return lower, upper

    def old_rate(k, carry):
        interior(states.at[k], rates.at[k])
        return carry

    lax.fori_loop(0, 3, old_rate, 0)
    arrive("states")
    for k in range(3):
        finish_rate(rates.at[k], recv.at[0, k], recv.at[1, k])

    base[...] = -DT * rates[0] + (H / 24.0) * (5.0 * rates[0] + 8.0 * rates[1] - rates[2])

    top = (sub // 4) % 2 == 0
    middle = (sub // 2) % 2 == 0
    bottom = sub % 2 == 0
    signs = [jnp.where(bit, jnp.float32(-1.0), jnp.float32(1.0)) for bit in (top, middle, bottom)]
    open_y = jnp.logical_or(jnp.logical_and(middle, lane >= CZ), jnp.logical_and(jnp.logical_not(middle), lane < LANES - CZ))
    open_z = jnp.logical_or(jnp.logical_and(bottom, layer > 0), jnp.logical_and(jnp.logical_not(bottom), layer < CZ - 1))

    def coarse_coefficients(block, carry):
        wide = flows[block]
        center = jnp.ones((ROWS, 8, LANES), jnp.float32)
        for axis in range(3):
            slope = signs[axis] * wide[:, axis]
            jump = jnp.minimum(-slope, 0.0)
            center = center + H * (0.5 * slope + jump)
            coef[1 + axis, block] = (-0.5 * H) * slope
            outer = -H * jump
            if axis == 1:
                outer = jnp.where(open_y, outer, 0.0)
            if axis == 2:
                outer = jnp.where(open_z, outer, 0.0)
            coef[4 + axis, block] = outer
        coef[0, block] = center
        return carry

    def advance(u, low):
        count = u.shape[0]
        own = u[1 : count - 1]
        px = pltpu.roll(u, 4, 1)
        ox = jnp.where(top, px[0 : count - 2], px[2:count])
        px = px[1 : count - 1]
        py = jnp.where(middle, pltpu.roll(own, 6, 1), pltpu.roll(own, 2, 1))
        pz = jnp.where(bottom, pltpu.roll(own, 7, 1), pltpu.roll(own, 1, 1))
        oy = jnp.where(middle, pltpu.roll(py, CZ, 2), pltpu.roll(py, LANES - CZ, 2))
        oz = jnp.where(bottom, pltpu.roll(pz, 1, 2), pltpu.roll(pz, LANES - 1, 2))
        total = None
        for index, value in enumerate((own, px, py, pz, ox, oy, oz)):
            factors = coef[index].reshape(SPAN, 8, LANES)[low + 1 : low + count - 1]
            piece = factors * value
            total = piece if total is None else total + piece
        return total

    res_same = [split(RES[0, 2 * i], RES[1, 2 * i + 1]) for i in range(2)]
    res_cross = [split(RES[0, 2 * i + 1], RES[1, 2 * i]) for i in range(2)]
    pro_same = [split(PRO[2 * i, 0], PRO[2 * i + 1, 1]) for i in range(2)]
    pro_cross = [split(PRO[2 * i, 1], PRO[2 * i + 1, 0]) for i in range(2)]

    def restricted(field):
        for i in range(2):
            lines = weighted([(RES[i, a], field[a]) for a in range(4)])
            for j in range(2):
                pair = weighted([(RES[j, b], lines[b]) for b in range(4)])
                turned = pltpu.roll(pair, 4, 1)
                value = (
                    res_same[0] * pair[0]
                    + res_cross[0] * turned[0]
                    + res_same[1] * pair[1]
                    + res_cross[1] * turned[1]
                )
                shuffle[pl.ds(8 * (2 * i + j), 8)] = value
        return jnp.stack([shuffle[pl.ds(r, 8, stride=4)] for r in range(ROWS)])

    def prolonged(rows):
        for r in range(ROWS):
            shuffle[pl.ds(r, 8, stride=4)] = rows[r]
        corners = []
        for index in range(4):
            value = shuffle[pl.ds(8 * index, 8)]
            turned = pltpu.roll(value, 4, 0)
            corners.append(jnp.stack([pro_same[i] * value + pro_cross[i] * turned for i in range(2)]))
        lines = [
            jnp.stack([weighted([(PRO[b, 0], corners[2 * i]), (PRO[b, 1], corners[2 * i + 1])]) for b in range(4)])
            for i in range(2)
        ]
        return [weighted([(PRO[a, 0], lines[0]), (PRO[a, 1], lines[1])]) for a in range(4)]

    coarse_coefficients(REACH, 0)

    @pl.when(n == 0)
    def _():
        for _, receives, make, _ in transfers["first_trace"]:
            when(receives, lambda make=make: make().wait_recv())
        duo_begin[0] = begin[...]
        interior(begin, duo_first.at[0])
        finish_rate(duo_first.at[0], recv.at[0, 3], recv.at[1, 3])

    duo_begin[1] = states[2]
    duo_first[1] = rates[2]
    duo_rates[0] = rates[...]
    duo_rates[1] = jnp.zeros((3,) + FIELD, jnp.float32)

    def duo_copy(k, d, slot):
        return remote(
            duo_send.at[k, slot],
            duo_recv.at[1 - k, slot],
            duo_out.at[k, slot],
            duo_in.at[1 - k, slot],
            (n, s + d),
        )

    def duo_launch(slot):
        for k, d in enumerate((-1, 1)):
            pl.when(has[d])(lambda k=k, d=d: duo_copy(k, d, slot).start())

    def duo_await(slot):
        for k, d in enumerate((-1, 1)):
            pl.when(has[-d])(lambda k=k, d=d: duo_copy(k, d, slot).wait_recv())

    def duo_fresh(target, factor, rate, slot, halo):
        def outer(x, carry):
            if halo is None:
                lower, upper = rate(x)[0], rate(x)[3]
            else:
                lower, upper = finish_rate(rate(x), duo_recv.at[0, halo, x], duo_recv.at[1, halo, x])
            first = duo_base[x, 0] + factor * lower
            last = duo_base[x, 3] + factor * upper
            target[x, 0] = first
            target[x, 3] = last
            pack(first, last, duo_send.at[0, slot, x], duo_send.at[1, slot, x])
            return carry

        def inner(x, carry):
            target[x, 1:3] = duo_base[x, 1:3] + factor * rate(x)[1:3]
            return carry

        lax.fori_loop(0, 2, outer, 0)
        duo_launch(slot)
        lax.fori_loop(0, 2, inner, 0)

    def opening(x, carry):
        duo_base[x] = (
            duo_begin[x]
            - DT * duo_rates[x, 0]
            + (H / 24.0) * (5.0 * duo_rates[x, 0] + 8.0 * duo_rates[x, 1] - duo_rates[x, 2])
        )
        return carry

    lax.fori_loop(0, 2, opening, 0)
    duo_fresh(duo_mid, DT, lambda x: duo_first.at[x], 0, None)
    start("begin3")

    def duo_closing(slot):
        def prepare(x, carry):
            duo_base[x] = (
                duo_mid[x]
                - DT * duo_rates[x, 1]
                + (H / 24.0) * (8.0 * duo_rates[x, 1] + 5.0 * duo_rates[x, 2] - duo_rates[x, 0])
            )
            interior(duo_mid.at[x], duo_rates.at[x, 1])
            return carry

        lax.fori_loop(0, 2, prepare, 0)
        duo_await(slot)
        duo_fresh(duo_end, DT, lambda x: duo_rates.at[x, 1], slot + 1, slot)

    def duo_middle(slot):
        def prepare(x, carry):
            duo_base[x] = duo_begin[x] + (H / 24.0) * (5.0 * duo_first[x] + 8.0 * duo_rates[x, 1])
            interior(duo_end.at[x], duo_rates.at[x, 2])
            return carry

        lax.fori_loop(0, 2, prepare, 0)
        duo_await(slot)
        duo_fresh(duo_mid, -H / 24.0, lambda x: duo_rates.at[x, 2], slot + 1, slot)

    duo_closing(0)
    start("begin4")
    for x in range(2):
        duo_rates[x, 0] = duo_first[x]
        old0[x, 1 : ROWS + 1] = restricted(duo_begin.at[x])
    start("row0")
    start("flow1")
    duo_middle(1)
    start("begin5")
    duo_closing(2)
    start("begin6")
    duo_middle(3)
    start("begin7")
    duo_closing(4)
    for x in range(2):
        old1[x, 1 : ROWS + 1] = restricted(duo_end.at[x])
    start("row1")

    def last_rate(x, carry):
        interior(duo_end.at[x], duo_rates.at[x, 2])
        return carry

    lax.fori_loop(0, 2, last_rate, 0)
    arrive("row0")
    low = MID - 1
    h_rates0 = [advance(old0[x], low) - old0[x, 1 : ROWS + 1] for x in range(2)]
    duo_await(5)
    offsets = []
    for x in range(2):
        finish_rate(duo_rates.at[x, 2], duo_recv.at[0, 5, x], duo_recv.at[1, 5, x])
    quadratures = [
        restricted(
            [
                (H / 6.0) * (duo_first[x, a] + 4.0 * duo_rates[x, 1, a] + duo_rates[x, 2, a])
                for a in range(4)
            ]
        )
        for x in range(2)
    ]
    arrive("row1")
    for x in (1, 0):
        h_rate0 = h_rates0[x]
        h_rate1 = advance(old1[x], low) - old1[x, 1 : ROWS + 1]
        trapezoid = 0.5 * (h_rate0 + h_rate1)
        offset = -h_rate0 + trapezoid + (quadratures[x] - trapezoid)
        if x == 1:
            leaving[...] = offset
            start("hop")
    is_first = n == 0
    offset = offset + jnp.where(is_first, old0[0, 1 : ROWS + 1] + h_rates0[0], 0.0)

    arrive("begin_trace")
    for piece in range(8):
        arrive(f"begin{piece}")
    interior(begin, first_rate)
    lower, upper = finish_rate(first_rate, recv.at[0, 3], recv.at[1, 3])

    def fine_copy(k, d, slot):
        return remote(
            send.at[k, slot],
            recv.at[1 - k, slot],
            fine_send.at[k, slot],
            fine_recv.at[1 - k, slot],
            (n, s + d),
        )

    def launch(slot):
        for k, d in enumerate((-1, 1)):
            pl.when(has[d])(lambda k=k, d=d: fine_copy(k, d, slot).start())

    def await_fine(slot):
        for k, d in enumerate((-1, 1)):
            pl.when(has[-d])(lambda k=k, d=d: fine_copy(k, d, slot).wait_recv())

    def fresh(u, origin, factor, rate, lower, upper, slot):
        first = origin[0] + factor * lower
        last = origin[3] + factor * upper
        u[0] = first
        u[3] = last
        if slot is not None:
            pack(first, last, send.at[0, slot], send.at[1, slot])
            launch(slot)
        u[1:3] = origin[1:3] + factor * rate[1:3]

    base[...] = base[...] + begin[...]
    fresh(mid_state, base, DT, first_rate, lower, upper, 4)

    arrive("hop")
    group[z, pl.ds(ROWS, ROWS)] = offset + passed[...]
    start("group")
    start("flow2")

    def to_closing(slot, out_slot):
        base[...] = (
            mid_state[...]
            - DT * rates[1]
            + (H / 24.0) * (8.0 * rates[1] + 5.0 * rates[2] - rates[0])
        )
        interior(mid_state, rates.at[1])
        await_fine(slot)
        lower, upper = finish_rate(rates.at[1], recv.at[0, slot], recv.at[1, slot])
        fresh(end_state, base, DT, rates.at[1], lower, upper, out_slot)

    def to_middle(slot):
        base[...] = begin[...] + (H / 24.0) * (5.0 * first_rate[...] + 8.0 * rates[1])
        interior(end_state, rates.at[2])
        await_fine(slot)
        lower, upper = finish_rate(rates.at[2], recv.at[0, slot], recv.at[1, slot])
        fresh(mid_state, base, -H / 24.0, rates.at[2], lower, upper, slot + 1)

    to_closing(4, 5)
    rates[0] = first_rate[...]
    before0 = restricted(begin)

    to_middle(5)
    for j in range(GROUP):

        @pl.when(z != j)
        def _():
            remote(
                group.at[j, pl.ds(ROWS, ROWS)],
                group.at[j, pl.ds(ROWS, ROWS)],
                group_send.at[0],
                group_recv.at[(z + GROUP - 1 - j) % GROUP],
                (n, s),
            ).wait_recv()

        if j < GROUP - 1:
            start(f"side{j}")
    start("flow3")
    arrive("flow1")
    coarse_coefficients(REACH - 1, 0)
    coarse_coefficients(REACH + 1, 0)
    to_closing(6, 7)
    for j in range(GROUP - 1):
        arrive(f"side{j}")
    y = group[0]
    y = advance(y, MID - 4) + group[1, 1:11]
    y = advance(y, MID - 3) + group[2, 2:10]
    y = advance(y, MID - 2)[1:5] + group[3, 4:8]
    partial[...] = y
    start("part")
    to_middle(7)
    to_closing(8, None)
    before1 = restricted(end_state)
    arrive("flow2")
    arrive("flow3")
    lax.fori_loop(0, REACH - 1, coarse_coefficients, 0)
    lax.fori_loop(REACH + 2, 2 * REACH + 1, coarse_coefficients, 0)
    arrive("part")
    y = far[...]
    for step in range(4):
        y = advance(y, step)
    y = y + mid[...]
    for step in range(4, 8):
        y = advance(y, step)
    y = y + near[...]
    for j in range(3):
        count = 12 - 2 * j
        stepped = advance(y, MID - 4 + j) + group[j, j + 1 : 11 - j]
        y = jnp.where(z > j, stepped, y[1 : count - 1])
    finish = advance(y, MID - 1) + group[z, pl.ds(ROWS, ROWS)]
    begin_rows = jnp.where(is_first, before0, y[1:5])
    delta0 = begin_rows - before0
    delta1 = finish - before1

    for index, (delta, field) in enumerate(
        ((delta0, begin), (0.5 * (delta0 + delta1), mid_state), (delta1, end_state))
    ):
        lifted = prolonged(delta)
        for a in range(4):
            result[index, a] = field[a] + lifted[a]
        pltpu.make_async_copy(result.at[index], out_hbm.at[index], store_sem.at[index]).start()
    for index in range(3):
        pltpu.make_async_copy(result.at[index], out_hbm.at[index], store_sem.at[index]).wait()

    for name in transfers:
        sent(name)
    for k, d in enumerate((-1, 1)):
        for slot in range(4, 9):
            pl.when(has[d])(lambda k=k, d=d, slot=slot: fine_copy(k, d, slot).wait_send())
        for slot in range(6):
            pl.when(has[d])(lambda k=k, d=d, slot=slot: duo_copy(k, d, slot).wait_send())


def solution(mesh):
    steps = mesh.shape["tm"]
    columns = mesh.shape["space"]

    def body(node_states, initial_state, velocity):
        states = node_states.reshape((3,) + FIELD)
        first = initial_state.reshape(FIELD)
        wind = velocity.reshape(3, 4, 4, 16, LANES)
        f32 = jnp.float32
        vmem = lambda *shape: pltpu.VMEM(shape, f32)
        dma = lambda *shape: pltpu.SemaphoreType.DMA(shape)
        out = pl.pallas_call(
            functools.partial(kernel, steps, columns),
            out_shape=jax.ShapeDtypeStruct((3,) + FIELD, f32),
            in_specs=[pl.BlockSpec(memory_space=pltpu.HBM)] * 3,
            out_specs=pl.BlockSpec(memory_space=pl.ANY),
            scratch_shapes=[
                vmem(3, *FIELD),
                pltpu.VMEM((3, 4, 4, 16, LANES), jnp.bfloat16),
                vmem(*FIELD),
                vmem(3, *FIELD),
                vmem(*FIELD),
                vmem(4, 2, 8, LANES),
                vmem(4, 2, 8, LANES),
                vmem(4, 2, 8, LANES),
                vmem(4, 2, 8, LANES),
                vmem(4, 2, 8, LANES),
                vmem(4, 2, 8, LANES),
                vmem(4, 4, 8, LANES),
                vmem(4, 4, 8, LANES),
                vmem(3, *FIELD),
                vmem(*FIELD),
                vmem(*FIELD),
                vmem(*FIELD),
                vmem(*FIELD),
                vmem(2, 9, 2, 8, LANES),
                vmem(2, 9, 2, 8, LANES),
                vmem(2, *FIELD),
                vmem(2, *FIELD),
                vmem(2, 3, *FIELD),
                vmem(2, *FIELD),
                vmem(2, *FIELD),
                vmem(2, *FIELD),
                vmem(2, 6, 2, 2, 8, LANES),
                vmem(2, 6, 2, 2, 8, LANES),
                vmem(ROWS, 8, LANES),
                vmem(ROWS, 8, LANES),
                vmem(32, LANES),
                vmem(2 * REACH + 1, ROWS, 3, 8, LANES),
                vmem(7, 2 * REACH + 1, ROWS, 8, LANES),
                vmem(2, ROWS + 2, 8, LANES),
                vmem(2, ROWS + 2, 8, LANES),
                vmem(GROUP, 3 * ROWS, 8, LANES),
                vmem(ROWS, 8, LANES),
                vmem(3 * ROWS, 8, LANES),
                vmem(5 * ROWS, 8, LANES),
                vmem(7 * ROWS, 8, LANES),
                vmem(3, *FIELD),
                dma(3),
                dma(3),
                dma(2, 9),
                dma(2, 9),
                dma(2, 6),
                dma(2, 6),
                pltpu.SemaphoreType.DMA,
                pltpu.SemaphoreType.DMA,
                dma(8),
                dma(8),
                dma(6),
                dma(6),
                dma(2, 2),
                dma(2, 2),
                dma(3),
                dma(3),
                dma(2, GROUP),
                dma(2, GROUP),
                dma(15),
                dma(15),
            ],
            compiler_params=pltpu.CompilerParams(
                collective_id=0, has_side_effects=True, vmem_limit_bytes=60 * 1024 * 1024
            ),
        )(states, first, wind)
        return out.reshape(1, 3, 64, ROWS, LANES)

    return jax.shard_map(
        body,
        mesh=mesh,
        in_specs=(
            P("tm", None, None, "space", None),
            P(None, "space", None),
            P(None, None, "space", None),
        ),
        out_specs=P("tm", None, None, "space", None),
        check_vma=False,
    )
```

```python
import functools

import jax
import jax.numpy as jnp
import numpy as np
from jax import lax
from jax.experimental import pallas as pl
from jax.experimental.pallas import tpu as pltpu
from jax.sharding import PartitionSpec as P

MESH = pl.DeviceIdType.MESH
CZ = 16
LANES = 128
GROUP = 4
H = 0.08
DT = 0.5 * H
LIFT = 6.0
ROWS = 4
REACH = 3
SPAN = (2 * REACH + 1) * ROWS
MID = REACH * ROWS
FIELD = (4, 4, 2, 8, LANES)


def lagrange_derivative(points):
    number = len(points)
    weights = np.array(
        [1.0 / np.prod([points[i] - points[j] for j in range(number) if j != i]) for i in range(number)]
    )
    derivative = np.zeros((number, number))
    for i in range(number):
        for j in range(number):
            if i != j:
                derivative[i, j] = weights[j] / weights[i] / (points[i] - points[j])
        derivative[i, i] = -np.sum(derivative[i])
    return derivative


POINTS = np.array([-1.0, -1.0 / np.sqrt(5.0), 1.0 / np.sqrt(5.0), 1.0])
WEIGHTS = np.array([1.0, 5.0, 5.0, 1.0]) / 6.0
DER = lagrange_derivative(POINTS)
PRO = np.stack([(1.0 - POINTS) / 2.0, (1.0 + POINTS) / 2.0], axis=1)
RES = PRO.T * WEIGHTS[None, :]


def weighted(terms):
    total = None
    for factor, value in terms:
        factor = float(factor)
        if abs(factor) < 1e-12:
            continue
        piece = value if factor == 1.0 else factor * value
        total = piece if total is None else total + piece
    return total


def kernel(
    steps,
    columns,
    states_hbm,
    start_hbm,
    wind_hbm,
    fields_hbm,
    lifted_hbm,
    states,
    wind,
    begin,
    nv,
    diag,
    xli,
    xhi,
    xlh,
    xhh,
    yl,
    yh,
    zl,
    zh,
    rates,
    first_rate,
    mid_state,
    end_state,
    base,
    send,
    recv,
    duo_begin,
    duo_first,
    duo_rates,
    duo_mid,
    duo_end,
    duo_base,
    duo_send,
    duo_recv,
    leaving,
    passed,
    shuffle,
    flows,
    coef,
    old0,
    old1,
    group,
    partial,
    near,
    mid,
    far,
    result,
    load_sem,
    store_sem,
    fine_send,
    fine_recv,
    duo_out,
    duo_in,
    hop_send,
    hop_recv,
    begin_send,
    begin_recv,
    flow_send,
    flow_recv,
    row_send,
    row_recv,
    group_send,
    group_recv,
    side_send,
    side_recv,
    part_send,
    part_recv,
):
    n = lax.axis_index("tm")
    s = lax.axis_index("space")
    g = n // GROUP
    z = n % GROUP
    groups = steps // GROUP

    sub = lax.broadcasted_iota(jnp.int32, (8, LANES), 0)
    lane = lax.broadcasted_iota(jnp.int32, (8, LANES), 1)
    parity = sub // 4
    row = sub % 4

    def split(even, odd):
        return jnp.where(parity == 0, jnp.float32(even), jnp.float32(odd))

    def remote(src, dst, ssem, rsem, device):
        return pltpu.make_async_remote_copy(
            src_ref=src, dst_ref=dst, send_sem=ssem, recv_sem=rsem, device_id=device, device_id_type=MESH
        )

    has = {-1: s > 0, 1: s < columns - 1}

    def inside(d):
        if d == 0:
            return None
        return s + d >= 0 if d < 0 else s + d < columns

    def both(a, b):
        if a is None:
            return b
        if b is None:
            return a
        return jnp.logical_and(a, b)

    def when(cond, run):
        if cond is None:
            run()
        else:
            pl.when(cond)(run)

    transfers = {}

    def add(name, sends, receives, make, partner):
        transfers.setdefault(name, []).append((sends, receives, make, partner))

    for k, d in enumerate((-1, 1)):
        add(
            "states",
            has[d],
            has[-d],
            functools.partial(
                remote,
                send.at[k, pl.ds(0, 3)],
                recv.at[1 - k, pl.ds(0, 3)],
                fine_send.at[k, 0],
                fine_recv.at[1 - k, 0],
                (n, s + d),
            ),
            None,
        )
        add(
            "begin_trace",
            both(n < steps - 1, has[d]),
            both(n > 0, has[-d]),
            functools.partial(
                remote,
                send.at[k, 2],
                recv.at[1 - k, 3],
                fine_send.at[k, 1],
                fine_recv.at[1 - k, 1],
                (n + 1, s + d),
            ),
            (n - 1, s - d),
        )
        add(
            "first_trace",
            both(n == 0, has[d]),
            both(n == 0, has[-d]),
            functools.partial(
                remote,
                send.at[k, 3],
                recv.at[1 - k, 3],
                fine_send.at[k, 2],
                fine_recv.at[1 - k, 1],
                (n, s + d),
            ),
            None,
        )
        for index, buffer in enumerate((old0, old1)):
            add(
                f"row{index}",
                has[d],
                has[-d],
                functools.partial(
                    remote,
                    buffer.at[:, 1 if d < 0 else ROWS],
                    buffer.at[:, ROWS + 1 if d < 0 else 0],
                    row_send.at[k, index],
                    row_recv.at[1 - k, index],
                    (n, s + d),
                ),
                None,
            )
        for j in range(GROUP - 1):
            rows = 3 - j
            add(
                f"side{j}",
                has[d],
                has[-d],
                functools.partial(
                    remote,
                    group.at[j, pl.ds(ROWS if d < 0 else 2 * ROWS - rows, rows)],
                    group.at[j, pl.ds(2 * ROWS if d < 0 else ROWS - rows, rows)],
                    side_send.at[k, j],
                    side_recv.at[1 - k, j],
                    (n, s + d),
                ),
                None,
            )
    def begin_copy(piece):
        where_to = (piece // 4, piece % 4)
        return remote(
            states_hbm.at[(2,) + where_to],
            begin.at[where_to],
            begin_send.at[piece],
            begin_recv.at[piece],
            (n + 1, s),
        )

    def begin_start(piece):
        pl.when(n < steps - 1)(lambda: begin_copy(piece).start())

    add(
        "hop",
        n < steps - 1,
        n > 0,
        functools.partial(remote, leaving, passed, hop_send, hop_recv, (n + 1, s)),
        None,
    )
    for index, d in enumerate((-3, -2, -1, 1, 2, 3)):
        needed = None if abs(d) == 1 else g >= abs(d)
        add(
            f"flow{abs(d)}",
            both(needed, inside(d)),
            both(needed, inside(-d)),
            functools.partial(
                remote,
                flows.at[REACH],
                flows.at[REACH - d],
                flow_send.at[index],
                flow_recv.at[index],
                (n, s + d),
            ),
            (n, s - d),
        )
    for shift in (1, 2, 3):
        add(
            "group",
            None,
            None,
            functools.partial(
                remote,
                group.at[z, pl.ds(ROWS, ROWS)],
                group.at[z, pl.ds(ROWS, ROWS)],
                group_send.at[shift - 1],
                group_recv.at[shift - 1],
                (g * GROUP + (z + shift) % GROUP, s),
            ),
            (g * GROUP + (z + GROUP - shift) % GROUP, s),
        )
    slot = 0
    for distance, buffer in ((3, far), (2, mid), (1, near)):
        for d in range(-distance, distance + 1):
            add(
                "part",
                both(g + distance < groups, inside(d)),
                both(g >= distance, inside(-d)),
                functools.partial(
                    remote,
                    partial,
                    buffer.at[pl.ds((distance - d) * ROWS, ROWS)],
                    part_send.at[slot],
                    part_recv.at[slot],
                    (n + distance * GROUP, s + d),
                ),
                (n - distance * GROUP, s - d),
            )
            slot += 1

    def start(name):
        for sends, _, make, _ in transfers[name]:
            when(sends, lambda make=make: make().start())

    def arrive(name):
        for _, receives, make, _ in transfers[name]:
            when(receives, lambda make=make: make().wait_recv())

    def sent(name):
        for sends, _, make, _ in transfers[name]:
            when(sends, lambda make=make: make().wait_send())

    load_states = pltpu.make_async_copy(states_hbm, states, load_sem.at[0])
    load_wind = pltpu.make_async_copy(wind_hbm, wind, load_sem.at[1])
    load_first = pltpu.make_async_copy(start_hbm, begin, load_sem.at[2])
    load_states.start()
    load_wind.start()
    pl.when(n == 0)(load_first.start)

    recv[...] = jnp.zeros(recv.shape, jnp.float32)
    duo_recv[...] = jnp.zeros(duo_recv.shape, jnp.float32)
    passed[...] = jnp.zeros(passed.shape, jnp.float32)
    duo_begin[0] = jnp.zeros(FIELD, jnp.float32)
    duo_first[0] = jnp.zeros(FIELD, jnp.float32)
    flows[...] = jnp.zeros(flows.shape, jnp.float32)
    old0[...] = jnp.zeros(old0.shape, jnp.float32)
    old1[...] = jnp.zeros(old1.shape, jnp.float32)
    group[...] = jnp.zeros(group.shape, jnp.float32)
    near[...] = jnp.zeros(near.shape, jnp.float32)
    mid[...] = jnp.zeros(mid.shape, jnp.float32)
    far[...] = jnp.zeros(far.shape, jnp.float32)

    barrier = pltpu.get_barrier_semaphore()
    expected = jnp.int32(0)

    def greet(cond, device):
        when(
            cond,
            lambda: pl.semaphore_signal(barrier, inc=1, device_id=device, device_id_type=MESH),
        )

    for d in (-1, 1):
        greet(has[d], (n, s + d))
        expected = expected + has[d].astype(jnp.int32)
    greet(n > 0, (n - 1, s))
    expected = expected + (n < steps - 1).astype(jnp.int32)
    for name in ("begin_trace", "flow2", "flow3", "group", "part"):
        for sends, receives, _, partner in transfers[name]:
            greet(receives, partner)
            expected = expected + (1 if sends is None else sends.astype(jnp.int32))

    load_states.wait()

    def pack(lower, upper, low_to, high_to):
        for half in range(2):
            low = None
            high = None
            for r in range(4):
                b, hh = (4 * half + r) // 2, r % 2
                lv = lower[b, hh]
                hv = upper[b, hh]
                lv = pltpu.roll(lv, r, 0) if r else lv
                hv = pltpu.roll(hv, (r + 5) % 8, 0) if r != 3 else hv
                low = lv if low is None else jnp.where(row == r, lv, low)
                high = hv if high is None else jnp.where(row == r, hv, high)
            low_to[half] = low
            high_to[half] = high

    def unpack(low_from, high_from):
        lows, highs = [], []
        for t in range(8):
            half, r = t // 4, t % 4
            lv = low_from[half]
            hv = high_from[half]
            lows.append(pltpu.roll(lv, 8 - r, 0) if r else lv)
            highs.append(pltpu.roll(hv, 3 - r, 0) if r != 3 else hv)
        return (
            jnp.stack(lows).reshape(4, 2, 8, LANES),
            jnp.stack(highs).reshape(4, 2, 8, LANES),
        )

    for k in range(3):
        pack(states[k, 0], states[k, 3], send.at[0, k], send.at[1, k])

    @pl.when(n == 0)
    def _():
        load_first.wait()
        pack(begin[0], begin[3], send.at[0, 3], send.at[1, 3])

    pl.semaphore_wait(barrier, expected)
    start("begin_trace")
    start("first_trace")
    start("states")
    for piece in range(4):
        begin_start(piece)

    load_wind.wait()
    for axis in range(3):
        nv[axis] = -wind[axis].astype(jnp.float32).reshape(FIELD)

    for axis in range(3):
        for i in range(2):
            for j in range(2):
                corner = jnp.where(parity == 0, nv[axis, 3 * i, 3 * j, 0], nv[axis, 3 * i, 3 * j, 1])
                shuffle[pl.ds(8 * (2 * i + j), 8)] = corner
        for r in range(ROWS):
            flows[REACH, r, axis] = shuffle[pl.ds(r, 8, stride=4)]

    cxl = LIFT * jnp.minimum(nv[0, 0], 0.0)
    cxh = LIFT * jnp.minimum(-nv[0, 3], 0.0)
    xli[...] = jnp.where(row > 0, -cxl, 0.0)
    xlh[...] = jnp.where(row == 0, -cxl, 0.0)
    xhi[...] = jnp.where(row < 3, -cxh, 0.0)
    xhh[...] = jnp.where(row == 3, -cxh, 0.0)
    cyl = LIFT * jnp.minimum(nv[1, :, 0], 0.0)
    cyh = LIFT * jnp.minimum(-nv[1, :, 3], 0.0)
    yl[...] = jnp.where(lane >= CZ, -cyl, 0.0)
    yh[...] = jnp.where(lane < LANES - CZ, -cyh, 0.0)
    czl = jnp.where(parity == 0, LIFT * jnp.minimum(nv[2, :, :, 0], 0.0), 0.0)
    czh = jnp.where(parity == 1, LIFT * jnp.minimum(-nv[2, :, :, 1], 0.0), 0.0)
    layer = lane % CZ
    zl[...] = jnp.where(layer > 0, -czl, 0.0)
    zh[...] = jnp.where(layer < CZ - 1, -czh, 0.0)
    diag[:, :, 0] = czl
    diag[:, :, 1] = czh
    diag[0] = diag[0] + cxl
    diag[3] = diag[3] + cxh
    diag[:, 0] = diag[:, 0] + cyl
    diag[:, 3] = diag[:, 3] + cyh

    same = [[split(DER[2 * i, 2 * j], DER[2 * i + 1, 2 * j + 1]) for j in range(2)] for i in range(2)]
    cross = [[split(DER[2 * i, 2 * j + 1], DER[2 * i + 1, 2 * j]) for j in range(2)] for i in range(2)]

    def interior(u, out):
        for b in range(4):
            pair = [u[:, b, 0], u[:, b, 1]]
            turned = [pltpu.roll(half, 4, 1) for half in pair]
            for i in range(2):
                own = pair[i]
                along_z = (
                    same[i][0] * pair[0]
                    + cross[i][0] * turned[0]
                    + same[i][1] * pair[1]
                    + cross[i][1] * turned[1]
                )
                total = diag[:, b, i] * own + nv[2, :, b, i] * along_z
                if i == 0:
                    total = total + zl[:, b] * pltpu.roll(turned[1], 1, 2)
                else:
                    total = total + zh[:, b] * pltpu.roll(turned[0], LANES - 1, 2)
                others = [own if c == b else u[:, c, i] for c in range(4)]
                along_y = weighted([(DER[b, c], others[c]) for c in range(4)])
                total = total + nv[1, :, b, i] * along_y
                if b == 0:
                    total = total + yl[:, i] * pltpu.roll(others[3], CZ, 2)
                if b == 3:
                    total = total + yh[:, i] * pltpu.roll(others[0], LANES - CZ, 2)
                along_x = jnp.stack([weighted([(DER[a, c], own[c]) for c in range(4)]) for a in range(4)])
                total = total + nv[0, :, b, i] * along_x
                out[0, b, i] = total[0] + xli[b, i] * pltpu.roll(own[3], 1, 0)
                out[1:3, b, i] = total[1:3]
                out[3, b, i] = total[3] + xhi[b, i] * pltpu.roll(own[0], 7, 0)

    def finish_rate(out, low_from, high_from):
        low, high = unpack(low_from, high_from)
        lower = out[0] + xlh[...] * low
        upper = out[3] + xhh[...] * high
        out[0] = lower
        out[3] = upper
        return lower, upper

    def old_rate(k, carry):
        interior(states.at[k], rates.at[k])
        return carry

    lax.fori_loop(0, 3, old_rate, 0)
    arrive("states")
    for k in range(3):
        finish_rate(rates.at[k], recv.at[0, k], recv.at[1, k])

    base[...] = -DT * rates[0] + (H / 24.0) * (5.0 * rates[0] + 8.0 * rates[1] - rates[2])

    top = (sub // 4) % 2 == 0
    middle = (sub // 2) % 2 == 0
    bottom = sub % 2 == 0
    signs = [jnp.where(bit, jnp.float32(-1.0), jnp.float32(1.0)) for bit in (top, middle, bottom)]
    open_y = jnp.logical_or(jnp.logical_and(middle, lane >= CZ), jnp.logical_and(jnp.logical_not(middle), lane < LANES - CZ))
    open_z = jnp.logical_or(jnp.logical_and(bottom, layer > 0), jnp.logical_and(jnp.logical_not(bottom), layer < CZ - 1))

    def coarse_coefficients(block, carry):
        wide = flows[block]
        center = jnp.ones((ROWS, 8, LANES), jnp.float32)
        for axis in range(3):
            slope = signs[axis] * wide[:, axis]
            jump = jnp.minimum(-slope, 0.0)
            center = center + H * (0.5 * slope + jump)
            coef[1 + axis, block] = (-0.5 * H) * slope
            outer = -H * jump
            if axis == 1:
                outer = jnp.where(open_y, outer, 0.0)
            if axis == 2:
                outer = jnp.where(open_z, outer, 0.0)
            coef[4 + axis, block] = outer
        coef[0, block] = center
        return carry

    def advance(u, low):
        count = u.shape[0]
        own = u[1 : count - 1]
        px = pltpu.roll(u, 4, 1)
        ox = jnp.where(top, px[0 : count - 2], px[2:count])
        px = px[1 : count - 1]
        py = jnp.where(middle, pltpu.roll(own, 6, 1), pltpu.roll(own, 2, 1))
        pz = jnp.where(bottom, pltpu.roll(own, 7, 1), pltpu.roll(own, 1, 1))
        oy = jnp.where(middle, pltpu.roll(py, CZ, 2), pltpu.roll(py, LANES - CZ, 2))
        oz = jnp.where(bottom, pltpu.roll(pz, 1, 2), pltpu.roll(pz, LANES - 1, 2))
        total = None
        for index, value in enumerate((own, px, py, pz, ox, oy, oz)):
            factors = coef[index].reshape(SPAN, 8, LANES)[low + 1 : low + count - 1]
            piece = factors * value
            total = piece if total is None else total + piece
        return total

    res_same = [split(RES[0, 2 * i], RES[1, 2 * i + 1]) for i in range(2)]
    res_cross = [split(RES[0, 2 * i + 1], RES[1, 2 * i]) for i in range(2)]
    pro_same = [split(PRO[2 * i, 0], PRO[2 * i + 1, 1]) for i in range(2)]
    pro_cross = [split(PRO[2 * i, 1], PRO[2 * i + 1, 0]) for i in range(2)]

    def restricted(field):
        for i in range(2):
            lines = weighted([(RES[i, a], field[a]) for a in range(4)])
            for j in range(2):
                pair = weighted([(RES[j, b], lines[b]) for b in range(4)])
                turned = pltpu.roll(pair, 4, 1)
                value = (
                    res_same[0] * pair[0]
                    + res_cross[0] * turned[0]
                    + res_same[1] * pair[1]
                    + res_cross[1] * turned[1]
                )
                shuffle[pl.ds(8 * (2 * i + j), 8)] = value
        return jnp.stack([shuffle[pl.ds(r, 8, stride=4)] for r in range(ROWS)])

    def prolonged(rows):
        for r in range(ROWS):
            shuffle[pl.ds(r, 8, stride=4)] = rows[r]
        corners = []
        for index in range(4):
            value = shuffle[pl.ds(8 * index, 8)]
            turned = pltpu.roll(value, 4, 0)
            corners.append(jnp.stack([pro_same[i] * value + pro_cross[i] * turned for i in range(2)]))
        lines = [
            jnp.stack([weighted([(PRO[b, 0], corners[2 * i]), (PRO[b, 1], corners[2 * i + 1])]) for b in range(4)])
            for i in range(2)
        ]
        return [weighted([(PRO[a, 0], lines[0]), (PRO[a, 1], lines[1])]) for a in range(4)]

    coarse_coefficients(REACH, 0)

    @pl.when(n == 0)
    def _():
        for _, receives, make, _ in transfers["first_trace"]:
            when(receives, lambda make=make: make().wait_recv())
        duo_begin[0] = begin[...]
        interior(begin, duo_first.at[0])
        finish_rate(duo_first.at[0], recv.at[0, 3], recv.at[1, 3])

    duo_begin[1] = states[2]
    duo_first[1] = rates[2]
    duo_rates[0] = rates[...]
    duo_rates[1] = jnp.zeros((3,) + FIELD, jnp.float32)

    def duo_copy(k, d, slot):
        return remote(
            duo_send.at[k, slot],
            duo_recv.at[1 - k, slot],
            duo_out.at[k, slot],
            duo_in.at[1 - k, slot],
            (n, s + d),
        )

    def duo_launch(slot):
        for k, d in enumerate((-1, 1)):
            pl.when(has[d])(lambda k=k, d=d: duo_copy(k, d, slot).start())

    def duo_await(slot):
        for k, d in enumerate((-1, 1)):
            pl.when(has[-d])(lambda k=k, d=d: duo_copy(k, d, slot).wait_recv())

    def duo_fresh(target, factor, rate, slot, halo):
        def outer(x, carry):
            if halo is None:
                lower, upper = rate(x)[0], rate(x)[3]
            else:
                lower, upper = finish_rate(rate(x), duo_recv.at[0, halo, x], duo_recv.at[1, halo, x])
            first = duo_base[x, 0] + factor * lower
            last = duo_base[x, 3] + factor * upper
            target[x, 0] = first
            target[x, 3] = last
            pack(first, last, duo_send.at[0, slot, x], duo_send.at[1, slot, x])
            return carry

        def inner(x, carry):
            target[x, 1:3] = duo_base[x, 1:3] + factor * rate(x)[1:3]
            return carry

        lax.fori_loop(0, 2, outer, 0)
        duo_launch(slot)
        lax.fori_loop(0, 2, inner, 0)

    def opening(x, carry):
        duo_base[x] = (
            duo_begin[x]
            - DT * duo_rates[x, 0]
            + (H / 24.0) * (5.0 * duo_rates[x, 0] + 8.0 * duo_rates[x, 1] - duo_rates[x, 2])
        )
        return carry

    lax.fori_loop(0, 2, opening, 0)
    duo_fresh(duo_mid, DT, lambda x: duo_first.at[x], 0, None)

    def duo_closing(slot):
        def prepare(x, carry):
            begin_start(4 + 2 * slot + x)
            duo_base[x] = (
                duo_mid[x]
                - DT * duo_rates[x, 1]
                + (H / 24.0) * (8.0 * duo_rates[x, 1] + 5.0 * duo_rates[x, 2] - duo_rates[x, 0])
            )
            interior(duo_mid.at[x], duo_rates.at[x, 1])
            return carry

        lax.fori_loop(0, 2, prepare, 0)
        duo_await(slot)
        duo_fresh(duo_end, DT, lambda x: duo_rates.at[x, 1], slot + 1, slot)

    def duo_middle(slot):
        def prepare(x, carry):
            begin_start(4 + 2 * slot + x)
            duo_base[x] = duo_begin[x] + (H / 24.0) * (5.0 * duo_first[x] + 8.0 * duo_rates[x, 1])
            interior(duo_end.at[x], duo_rates.at[x, 2])
            return carry

        lax.fori_loop(0, 2, prepare, 0)
        duo_await(slot)
        duo_fresh(duo_mid, -H / 24.0, lambda x: duo_rates.at[x, 2], slot + 1, slot)

    duo_closing(0)
    for x in range(2):
        duo_rates[x, 0] = duo_first[x]
        old0[x, 1 : ROWS + 1] = restricted(duo_begin.at[x])
    start("row0")
    start("flow1")
    duo_middle(1)
    duo_closing(2)
    duo_middle(3)
    duo_closing(4)
    for x in range(2):
        old1[x, 1 : ROWS + 1] = restricted(duo_end.at[x])
    start("row1")

    def last_rate(x, carry):
        begin_start(14 + x)
        interior(duo_end.at[x], duo_rates.at[x, 2])
        return carry

    lax.fori_loop(0, 2, last_rate, 0)
    arrive("row0")
    low = MID - 1
    h_rates0 = [advance(old0[x], low) - old0[x, 1 : ROWS + 1] for x in range(2)]
    duo_await(5)
    offsets = []
    for x in range(2):
        finish_rate(duo_rates.at[x, 2], duo_recv.at[0, 5, x], duo_recv.at[1, 5, x])
    quadratures = [
        restricted(
            [
                (H / 6.0) * (duo_first[x, a] + 4.0 * duo_rates[x, 1, a] + duo_rates[x, 2, a])
                for a in range(4)
            ]
        )
        for x in range(2)
    ]
    arrive("row1")
    for x in (1, 0):
        h_rate0 = h_rates0[x]
        h_rate1 = advance(old1[x], low) - old1[x, 1 : ROWS + 1]
        trapezoid = 0.5 * (h_rate0 + h_rate1)
        offset = -h_rate0 + trapezoid + (quadratures[x] - trapezoid)
        if x == 1:
            leaving[...] = offset
            start("hop")
    is_first = n == 0
    offset = offset + jnp.where(is_first, old0[0, 1 : ROWS + 1] + h_rates0[0], 0.0)

    arrive("begin_trace")
    for piece in range(16):
        pl.when(n > 0)(lambda piece=piece: begin_copy(piece).wait_recv())
    interior(begin, first_rate)
    lower, upper = finish_rate(first_rate, recv.at[0, 3], recv.at[1, 3])

    def fine_copy(k, d, slot):
        return remote(
            send.at[k, slot],
            recv.at[1 - k, slot],
            fine_send.at[k, slot],
            fine_recv.at[1 - k, slot],
            (n, s + d),
        )

    def launch(slot):
        for k, d in enumerate((-1, 1)):
            pl.when(has[d])(lambda k=k, d=d: fine_copy(k, d, slot).start())

    def await_fine(slot):
        for k, d in enumerate((-1, 1)):
            pl.when(has[-d])(lambda k=k, d=d: fine_copy(k, d, slot).wait_recv())

    def fresh(u, origin, factor, rate, lower, upper, slot):
        first = origin[0] + factor * lower
        last = origin[3] + factor * upper
        u[0] = first
        u[3] = last
        if slot is not None:
            pack(first, last, send.at[0, slot], send.at[1, slot])
            launch(slot)
        u[1:3] = origin[1:3] + factor * rate[1:3]

    base[...] = base[...] + begin[...]
    fresh(mid_state, base, DT, first_rate, lower, upper, 4)

    arrive("hop")
    group[z, pl.ds(ROWS, ROWS)] = offset + passed[...]
    start("group")
    start("flow2")

    def to_closing(slot, out_slot):
        base[...] = (
            mid_state[...]
            - DT * rates[1]
            + (H / 24.0) * (8.0 * rates[1] + 5.0 * rates[2] - rates[0])
        )
        interior(mid_state, rates.at[1])
        await_fine(slot)
        lower, upper = finish_rate(rates.at[1], recv.at[0, slot], recv.at[1, slot])
        fresh(end_state, base, DT, rates.at[1], lower, upper, out_slot)

    def to_middle(slot):
        base[...] = begin[...] + (H / 24.0) * (5.0 * first_rate[...] + 8.0 * rates[1])
        interior(end_state, rates.at[2])
        await_fine(slot)
        lower, upper = finish_rate(rates.at[2], recv.at[0, slot], recv.at[1, slot])
        fresh(mid_state, base, -H / 24.0, rates.at[2], lower, upper, slot + 1)

    to_closing(4, 5)
    rates[0] = first_rate[...]
    before0 = restricted(begin)

    to_middle(5)
    for j in range(GROUP):

        @pl.when(z != j)
        def _():
            remote(
                group.at[j, pl.ds(ROWS, ROWS)],
                group.at[j, pl.ds(ROWS, ROWS)],
                group_send.at[0],
                group_recv.at[(z + GROUP - 1 - j) % GROUP],
                (n, s),
            ).wait_recv()

        if j < GROUP - 1:
            start(f"side{j}")
    start("flow3")
    arrive("flow1")
    coarse_coefficients(REACH - 1, 0)
    coarse_coefficients(REACH + 1, 0)
    to_closing(6, 7)
    for j in range(GROUP - 1):
        arrive(f"side{j}")
    y = group[0]
    y = advance(y, MID - 4) + group[1, 1:11]
    y = advance(y, MID - 3) + group[2, 2:10]
    y = advance(y, MID - 2)[1:5] + group[3, 4:8]
    partial[...] = y
    start("part")
    to_middle(7)
    to_closing(8, None)
    stores = [
        pltpu.make_async_copy(field, fields_hbm.at[index], store_sem.at[3 + index])
        for index, field in enumerate((begin, mid_state, end_state))
    ]
    for store in stores:
        store.start()
    before1 = restricted(end_state)
    arrive("flow2")
    arrive("flow3")
    lax.fori_loop(0, REACH - 1, coarse_coefficients, 0)
    lax.fori_loop(REACH + 2, 2 * REACH + 1, coarse_coefficients, 0)
    arrive("part")
    y = far[...]
    for step in range(4):
        y = advance(y, step)
    y = y + mid[...]
    for step in range(4, 8):
        y = advance(y, step)
    y = y + near[...]
    for j in range(3):
        count = 12 - 2 * j
        stepped = advance(y, MID - 4 + j) + group[j, j + 1 : 11 - j]
        y = jnp.where(z > j, stepped, y[1 : count - 1])
    finish = advance(y, MID - 1) + group[z, pl.ds(ROWS, ROWS)]
    begin_rows = jnp.where(is_first, before0, y[1:5])
    delta0 = begin_rows - before0
    delta1 = finish - before1

    for index, delta in enumerate((delta0, 0.5 * (delta0 + delta1), delta1)):
        lifted = prolonged(delta)
        for a in range(4):
            result[index, a] = lifted[a]
        pltpu.make_async_copy(result.at[index], lifted_hbm.at[index], store_sem.at[index]).start()
    for index in range(3):
        pltpu.make_async_copy(result.at[index], lifted_hbm.at[index], store_sem.at[index]).wait()
    for store in stores:
        store.wait()

    for name in transfers:
        sent(name)
    for piece in range(16):
        pl.when(n < steps - 1)(lambda piece=piece: begin_copy(piece).wait_send())
    for k, d in enumerate((-1, 1)):
        for slot in range(4, 9):
            pl.when(has[d])(lambda k=k, d=d, slot=slot: fine_copy(k, d, slot).wait_send())
        for slot in range(6):
            pl.when(has[d])(lambda k=k, d=d, slot=slot: duo_copy(k, d, slot).wait_send())


def solution(mesh):
    steps = mesh.shape["tm"]
    columns = mesh.shape["space"]

    def body(node_states, initial_state, velocity):
        states = node_states.reshape((3,) + FIELD)
        first = initial_state.reshape(FIELD)
        wind = velocity.reshape(3, 4, 4, 16, LANES)
        f32 = jnp.float32
        vmem = lambda *shape: pltpu.VMEM(shape, f32)
        dma = lambda *shape: pltpu.SemaphoreType.DMA(shape)
        fields, lifted = pl.pallas_call(
            functools.partial(kernel, steps, columns),
            out_shape=[jax.ShapeDtypeStruct((3,) + FIELD, f32)] * 2,
            in_specs=[pl.BlockSpec(memory_space=pltpu.HBM)] * 3,
            out_specs=[pl.BlockSpec(memory_space=pl.ANY)] * 2,
            scratch_shapes=[
                vmem(3, *FIELD),
                pltpu.VMEM((3, 4, 4, 16, LANES), jnp.bfloat16),
                vmem(*FIELD),
                vmem(3, *FIELD),
                vmem(*FIELD),
                vmem(4, 2, 8, LANES),
                vmem(4, 2, 8, LANES),
                vmem(4, 2, 8, LANES),
                vmem(4, 2, 8, LANES),
                vmem(4, 2, 8, LANES),
                vmem(4, 2, 8, LANES),
                vmem(4, 4, 8, LANES),
                vmem(4, 4, 8, LANES),
                vmem(3, *FIELD),
                vmem(*FIELD),
                vmem(*FIELD),
                vmem(*FIELD),
                vmem(*FIELD),
                vmem(2, 9, 2, 8, LANES),
                vmem(2, 9, 2, 8, LANES),
                vmem(2, *FIELD),
                vmem(2, *FIELD),
                vmem(2, 3, *FIELD),
                vmem(2, *FIELD),
                vmem(2, *FIELD),
                vmem(2, *FIELD),
                vmem(2, 6, 2, 2, 8, LANES),
                vmem(2, 6, 2, 2, 8, LANES),
                vmem(ROWS, 8, LANES),
                vmem(ROWS, 8, LANES),
                vmem(32, LANES),
                vmem(2 * REACH + 1, ROWS, 3, 8, LANES),
                vmem(7, 2 * REACH + 1, ROWS, 8, LANES),
                vmem(2, ROWS + 2, 8, LANES),
                vmem(2, ROWS + 2, 8, LANES),
                vmem(GROUP, 3 * ROWS, 8, LANES),
                vmem(ROWS, 8, LANES),
                vmem(3 * ROWS, 8, LANES),
                vmem(5 * ROWS, 8, LANES),
                vmem(7 * ROWS, 8, LANES),
                vmem(3, *FIELD),
                dma(3),
                dma(6),
                dma(2, 9),
                dma(2, 9),
                dma(2, 6),
                dma(2, 6),
                pltpu.SemaphoreType.DMA,
                pltpu.SemaphoreType.DMA,
                dma(16),
                dma(16),
                dma(6),
                dma(6),
                dma(2, 2),
                dma(2, 2),
                dma(3),
                dma(3),
                dma(2, GROUP),
                dma(2, GROUP),
                dma(15),
                dma(15),
            ],
            compiler_params=pltpu.CompilerParams(
                collective_id=0, has_side_effects=True, vmem_limit_bytes=60 * 1024 * 1024
            ),
        )(states, first, wind)
        return (fields + lifted).reshape(1, 3, 64, ROWS, LANES)

    return jax.shard_map(
        body,
        mesh=mesh,
        in_specs=(
            P("tm", None, None, "space", None),
            P(None, "space", None),
            P(None, None, "space", None),
        ),
        out_specs=P("tm", None, None, "space", None),
        check_vma=False,
    )
```

```python
import functools

import jax
import jax.numpy as jnp
import numpy as np
from jax import lax
from jax.experimental import pallas as pl
from jax.experimental.pallas import tpu as pltpu
from jax.sharding import PartitionSpec as P

MESH = pl.DeviceIdType.MESH
CZ = 16
LANES = 128
GROUP = 4
H = 0.08
DT = 0.5 * H
LIFT = 6.0
ROWS = 4
REACH = 3
SPAN = (2 * REACH + 1) * ROWS
MID = REACH * ROWS
FIELD = (4, 4, 2, 8, LANES)


def lagrange_derivative(points):
    number = len(points)
    weights = np.array(
        [1.0 / np.prod([points[i] - points[j] for j in range(number) if j != i]) for i in range(number)]
    )
    derivative = np.zeros((number, number))
    for i in range(number):
        for j in range(number):
            if i != j:
                derivative[i, j] = weights[j] / weights[i] / (points[i] - points[j])
        derivative[i, i] = -np.sum(derivative[i])
    return derivative


POINTS = np.array([-1.0, -1.0 / np.sqrt(5.0), 1.0 / np.sqrt(5.0), 1.0])
WEIGHTS = np.array([1.0, 5.0, 5.0, 1.0]) / 6.0
DER = lagrange_derivative(POINTS)
PRO = np.stack([(1.0 - POINTS) / 2.0, (1.0 + POINTS) / 2.0], axis=1)
RES = PRO.T * WEIGHTS[None, :]


def weighted(terms):
    total = None
    for factor, value in terms:
        factor = float(factor)
        if abs(factor) < 1e-12:
            continue
        piece = value if factor == 1.0 else factor * value
        total = piece if total is None else total + piece
    return total


def kernel(
    steps,
    columns,
    states_hbm,
    start_hbm,
    wind_hbm,
    fields_hbm,
    lifted_hbm,
    states,
    wind,
    begin,
    nv,
    diag,
    xli,
    xhi,
    xlh,
    xhh,
    yl,
    yh,
    zl,
    zh,
    rates,
    first_rate,
    mid_state,
    end_state,
    base,
    send,
    recv,
    duo_begin,
    duo_first,
    duo_rates,
    duo_mid,
    duo_end,
    duo_base,
    duo_send,
    duo_recv,
    leaving,
    passed,
    shuffle,
    flows,
    coef,
    old0,
    old1,
    group,
    partial,
    near,
    mid,
    far,
    result,
    load_sem,
    store_sem,
    fine_send,
    fine_recv,
    duo_out,
    duo_in,
    hop_send,
    hop_recv,
    begin_send,
    begin_recv,
    flow_send,
    flow_recv,
    row_send,
    row_recv,
    group_send,
    group_recv,
    side_send,
    side_recv,
    part_send,
    part_recv,
):
    n = lax.axis_index("tm")
    s = lax.axis_index("space")
    g = n // GROUP
    z = n % GROUP
    groups = steps // GROUP

    sub = lax.broadcasted_iota(jnp.int32, (8, LANES), 0)
    lane = lax.broadcasted_iota(jnp.int32, (8, LANES), 1)
    parity = sub // 4
    row = sub % 4

    def split(even, odd):
        return jnp.where(parity == 0, jnp.float32(even), jnp.float32(odd))

    def remote(src, dst, ssem, rsem, device):
        return pltpu.make_async_remote_copy(
            src_ref=src, dst_ref=dst, send_sem=ssem, recv_sem=rsem, device_id=device, device_id_type=MESH
        )

    has = {-1: s > 0, 1: s < columns - 1}

    def inside(d):
        if d == 0:
            return None
        return s + d >= 0 if d < 0 else s + d < columns

    def both(a, b):
        if a is None:
            return b
        if b is None:
            return a
        return jnp.logical_and(a, b)

    def when(cond, run):
        if cond is None:
            run()
        else:
            pl.when(cond)(run)

    transfers = {}

    def add(name, sends, receives, make, partner):
        transfers.setdefault(name, []).append((sends, receives, make, partner))

    for k, d in enumerate((-1, 1)):
        add(
            "states",
            has[d],
            has[-d],
            functools.partial(
                remote,
                send.at[k, pl.ds(0, 3)],
                recv.at[1 - k, pl.ds(0, 3)],
                fine_send.at[k, 0],
                fine_recv.at[1 - k, 0],
                (n, s + d),
            ),
            None,
        )
        add(
            "begin_trace",
            both(n < steps - 1, has[d]),
            both(n > 0, has[-d]),
            functools.partial(
                remote,
                send.at[k, 2],
                recv.at[1 - k, 3],
                fine_send.at[k, 1],
                fine_recv.at[1 - k, 1],
                (n + 1, s + d),
            ),
            (n - 1, s - d),
        )
        add(
            "first_trace",
            both(n == 0, has[d]),
            both(n == 0, has[-d]),
            functools.partial(
                remote,
                send.at[k, 3],
                recv.at[1 - k, 3],
                fine_send.at[k, 2],
                fine_recv.at[1 - k, 1],
                (n, s + d),
            ),
            None,
        )
        for index, buffer in enumerate((old0, old1)):
            add(
                f"row{index}",
                has[d],
                has[-d],
                functools.partial(
                    remote,
                    buffer.at[:, 1 if d < 0 else ROWS],
                    buffer.at[:, ROWS + 1 if d < 0 else 0],
                    row_send.at[k, index],
                    row_recv.at[1 - k, index],
                    (n, s + d),
                ),
                None,
            )
        for j in range(GROUP - 1):
            rows = 3 - j
            add(
                f"side{j}",
                has[d],
                has[-d],
                functools.partial(
                    remote,
                    group.at[j, pl.ds(ROWS if d < 0 else 2 * ROWS - rows, rows)],
                    group.at[j, pl.ds(2 * ROWS if d < 0 else ROWS - rows, rows)],
                    side_send.at[k, j],
                    side_recv.at[1 - k, j],
                    (n, s + d),
                ),
                None,
            )
    add(
        "begin",
        n < steps - 1,
        n > 0,
        functools.partial(remote, states_hbm.at[2], begin, begin_send, begin_recv, (n + 1, s)),
        (n - 1, s),
    )
    add(
        "hop",
        n < steps - 1,
        n > 0,
        functools.partial(remote, leaving, passed, hop_send, hop_recv, (n + 1, s)),
        None,
    )
    for index, d in enumerate((-3, -2, -1, 1, 2, 3)):
        needed = None if abs(d) == 1 else g >= abs(d)
        add(
            f"flow{abs(d)}",
            both(needed, inside(d)),
            both(needed, inside(-d)),
            functools.partial(
                remote,
                flows.at[REACH],
                flows.at[REACH - d],
                flow_send.at[index],
                flow_recv.at[index],
                (n, s + d),
            ),
            (n, s - d),
        )
    for shift in (1, 2, 3):
        add(
            "group",
            None,
            None,
            functools.partial(
                remote,
                group.at[z, pl.ds(ROWS, ROWS)],
                group.at[z, pl.ds(ROWS, ROWS)],
                group_send.at[shift - 1],
                group_recv.at[shift - 1],
                (g * GROUP + (z + shift) % GROUP, s),
            ),
            (g * GROUP + (z + GROUP - shift) % GROUP, s),
        )
    slot = 0
    for distance, buffer in ((3, far), (2, mid), (1, near)):
        for d in range(-distance, distance + 1):
            add(
                "part",
                both(g + distance < groups, inside(d)),
                both(g >= distance, inside(-d)),
                functools.partial(
                    remote,
                    partial,
                    buffer.at[pl.ds((distance - d) * ROWS, ROWS)],
                    part_send.at[slot],
                    part_recv.at[slot],
                    (n + distance * GROUP, s + d),
                ),
                (n - distance * GROUP, s - d),
            )
            slot += 1

    def start(name):
        for sends, _, make, _ in transfers[name]:
            when(sends, lambda make=make: make().start())

    def arrive(name):
        for _, receives, make, _ in transfers[name]:
            when(receives, lambda make=make: make().wait_recv())

    def sent(name):
        for sends, _, make, _ in transfers[name]:
            when(sends, lambda make=make: make().wait_send())

    load_states = pltpu.make_async_copy(states_hbm, states, load_sem.at[0])
    load_wind = pltpu.make_async_copy(wind_hbm, wind, load_sem.at[1])
    load_first = pltpu.make_async_copy(start_hbm, begin, load_sem.at[2])
    load_states.start()
    load_wind.start()
    pl.when(n == 0)(load_first.start)

    recv[...] = jnp.zeros(recv.shape, jnp.float32)
    duo_recv[...] = jnp.zeros(duo_recv.shape, jnp.float32)
    passed[...] = jnp.zeros(passed.shape, jnp.float32)
    duo_begin[0] = jnp.zeros(FIELD, jnp.float32)
    duo_first[0] = jnp.zeros(FIELD, jnp.float32)
    flows[...] = jnp.zeros(flows.shape, jnp.float32)
    old0[...] = jnp.zeros(old0.shape, jnp.float32)
    old1[...] = jnp.zeros(old1.shape, jnp.float32)
    group[...] = jnp.zeros(group.shape, jnp.float32)
    near[...] = jnp.zeros(near.shape, jnp.float32)
    mid[...] = jnp.zeros(mid.shape, jnp.float32)
    far[...] = jnp.zeros(far.shape, jnp.float32)

    barrier = pltpu.get_barrier_semaphore()
    expected = jnp.int32(0)

    def greet(cond, device):
        when(
            cond,
            lambda: pl.semaphore_signal(barrier, inc=1, device_id=device, device_id_type=MESH),
        )

    for d in (-1, 1):
        greet(has[d], (n, s + d))
        expected = expected + has[d].astype(jnp.int32)
    for name in ("begin_trace", "begin", "flow2", "flow3", "group", "part"):
        for sends, receives, _, partner in transfers[name]:
            greet(receives, partner)
            expected = expected + (1 if sends is None else sends.astype(jnp.int32))

    load_states.wait()

    def pack(lower, upper, low_to, high_to):
        for half in range(2):
            low = None
            high = None
            for r in range(4):
                b, hh = (4 * half + r) // 2, r % 2
                lv = lower[b, hh]
                hv = upper[b, hh]
                lv = pltpu.roll(lv, r, 0) if r else lv
                hv = pltpu.roll(hv, (r + 5) % 8, 0) if r != 3 else hv
                low = lv if low is None else jnp.where(row == r, lv, low)
                high = hv if high is None else jnp.where(row == r, hv, high)
            low_to[half] = low
            high_to[half] = high

    def unpack(low_from, high_from):
        lows, highs = [], []
        for t in range(8):
            half, r = t // 4, t % 4
            lv = low_from[half]
            hv = high_from[half]
            lows.append(pltpu.roll(lv, 8 - r, 0) if r else lv)
            highs.append(pltpu.roll(hv, 3 - r, 0) if r != 3 else hv)
        return (
            jnp.stack(lows).reshape(4, 2, 8, LANES),
            jnp.stack(highs).reshape(4, 2, 8, LANES),
        )

    for k in range(3):
        pack(states[k, 0], states[k, 3], send.at[0, k], send.at[1, k])

    @pl.when(n == 0)
    def _():
        load_first.wait()
        pack(begin[0], begin[3], send.at[0, 3], send.at[1, 3])

    pl.semaphore_wait(barrier, expected)
    start("begin_trace")
    start("first_trace")
    start("states")
    start("begin")

    load_wind.wait()
    for axis in range(3):
        nv[axis] = -wind[axis].astype(jnp.float32).reshape(FIELD)

    for axis in range(3):
        for i in range(2):
            for j in range(2):
                corner = jnp.where(parity == 0, nv[axis, 3 * i, 3 * j, 0], nv[axis, 3 * i, 3 * j, 1])
                shuffle[pl.ds(8 * (2 * i + j), 8)] = corner
        for r in range(ROWS):
            flows[REACH, r, axis] = shuffle[pl.ds(r, 8, stride=4)]

    cxl = LIFT * jnp.minimum(nv[0, 0], 0.0)
    cxh = LIFT * jnp.minimum(-nv[0, 3], 0.0)
    xli[...] = jnp.where(row > 0, -cxl, 0.0)
    xlh[...] = jnp.where(row == 0, -cxl, 0.0)
    xhi[...] = jnp.where(row < 3, -cxh, 0.0)
    xhh[...] = jnp.where(row == 3, -cxh, 0.0)
    cyl = LIFT * jnp.minimum(nv[1, :, 0], 0.0)
    cyh = LIFT * jnp.minimum(-nv[1, :, 3], 0.0)
    yl[...] = jnp.where(lane >= CZ, -cyl, 0.0)
    yh[...] = jnp.where(lane < LANES - CZ, -cyh, 0.0)
    czl = jnp.where(parity == 0, LIFT * jnp.minimum(nv[2, :, :, 0], 0.0), 0.0)
    czh = jnp.where(parity == 1, LIFT * jnp.minimum(-nv[2, :, :, 1], 0.0), 0.0)
    layer = lane % CZ
    zl[...] = jnp.where(layer > 0, -czl, 0.0)
    zh[...] = jnp.where(layer < CZ - 1, -czh, 0.0)
    diag[:, :, 0] = czl
    diag[:, :, 1] = czh
    diag[0] = diag[0] + cxl
    diag[3] = diag[3] + cxh
    diag[:, 0] = diag[:, 0] + cyl
    diag[:, 3] = diag[:, 3] + cyh

    same = [[split(DER[2 * i, 2 * j], DER[2 * i + 1, 2 * j + 1]) for j in range(2)] for i in range(2)]
    cross = [[split(DER[2 * i, 2 * j + 1], DER[2 * i + 1, 2 * j]) for j in range(2)] for i in range(2)]

    def interior(u, out):
        for b in range(4):
            pair = [u[:, b, 0], u[:, b, 1]]
            turned = [pltpu.roll(half, 4, 1) for half in pair]
            for i in range(2):
                own = pair[i]
                along_z = (
                    same[i][0] * pair[0]
                    + cross[i][0] * turned[0]
                    + same[i][1] * pair[1]
                    + cross[i][1] * turned[1]
                )
                total = diag[:, b, i] * own + nv[2, :, b, i] * along_z
                if i == 0:
                    total = total + zl[:, b] * pltpu.roll(turned[1], 1, 2)
                else:
                    total = total + zh[:, b] * pltpu.roll(turned[0], LANES - 1, 2)
                others = [own if c == b else u[:, c, i] for c in range(4)]
                along_y = weighted([(DER[b, c], others[c]) for c in range(4)])
                total = total + nv[1, :, b, i] * along_y
                if b == 0:
                    total = total + yl[:, i] * pltpu.roll(others[3], CZ, 2)
                if b == 3:
                    total = total + yh[:, i] * pltpu.roll(others[0], LANES - CZ, 2)
                along_x = jnp.stack([weighted([(DER[a, c], own[c]) for c in range(4)]) for a in range(4)])
                total = total + nv[0, :, b, i] * along_x
                out[0, b, i] = total[0] + xli[b, i] * pltpu.roll(own[3], 1, 0)
                out[1:3, b, i] = total[1:3]
                out[3, b, i] = total[3] + xhi[b, i] * pltpu.roll(own[0], 7, 0)

    def finish_rate(out, low_from, high_from):
        low, high = unpack(low_from, high_from)
        lower = out[0] + xlh[...] * low
        upper = out[3] + xhh[...] * high
        out[0] = lower
        out[3] = upper
        return lower, upper

    def old_rate(k, carry):
        interior(states.at[k], rates.at[k])
        return carry

    lax.fori_loop(0, 3, old_rate, 0)
    arrive("states")
    for k in range(3):
        finish_rate(rates.at[k], recv.at[0, k], recv.at[1, k])

    base[...] = -DT * rates[0] + (H / 24.0) * (5.0 * rates[0] + 8.0 * rates[1] - rates[2])

    top = (sub // 4) % 2 == 0
    middle = (sub // 2) % 2 == 0
    bottom = sub % 2 == 0
    signs = [jnp.where(bit, jnp.float32(-1.0), jnp.float32(1.0)) for bit in (top, middle, bottom)]
    open_y = jnp.logical_or(jnp.logical_and(middle, lane >= CZ), jnp.logical_and(jnp.logical_not(middle), lane < LANES - CZ))
    open_z = jnp.logical_or(jnp.logical_and(bottom, layer > 0), jnp.logical_and(jnp.logical_not(bottom), layer < CZ - 1))

    def coarse_coefficients(block, carry):
        wide = flows[block]
        center = jnp.ones((ROWS, 8, LANES), jnp.float32)
        for axis in range(3):
            slope = signs[axis] * wide[:, axis]
            jump = jnp.minimum(-slope, 0.0)
            center = center + H * (0.5 * slope + jump)
            coef[1 + axis, block] = (-0.5 * H) * slope
            outer = -H * jump
            if axis == 1:
                outer = jnp.where(open_y, outer, 0.0)
            if axis == 2:
                outer = jnp.where(open_z, outer, 0.0)
            coef[4 + axis, block] = outer
        coef[0, block] = center
        return carry

    def advance(u, low):
        count = u.shape[0]
        own = u[1 : count - 1]
        px = pltpu.roll(u, 4, 1)
        ox = jnp.where(top, px[0 : count - 2], px[2:count])
        px = px[1 : count - 1]
        py = jnp.where(middle, pltpu.roll(own, 6, 1), pltpu.roll(own, 2, 1))
        pz = jnp.where(bottom, pltpu.roll(own, 7, 1), pltpu.roll(own, 1, 1))
        oy = jnp.where(middle, pltpu.roll(py, CZ, 2), pltpu.roll(py, LANES - CZ, 2))
        oz = jnp.where(bottom, pltpu.roll(pz, 1, 2), pltpu.roll(pz, LANES - 1, 2))
        total = None
        for index, value in enumerate((own, px, py, pz, ox, oy, oz)):
            factors = coef[index].reshape(SPAN, 8, LANES)[low + 1 : low + count - 1]
            piece = factors * value
            total = piece if total is None else total + piece
        return total

    res_same = [split(RES[0, 2 * i], RES[1, 2 * i + 1]) for i in range(2)]
    res_cross = [split(RES[0, 2 * i + 1], RES[1, 2 * i]) for i in range(2)]
    pro_same = [split(PRO[2 * i, 0], PRO[2 * i + 1, 1]) for i in range(2)]
    pro_cross = [split(PRO[2 * i, 1], PRO[2 * i + 1, 0]) for i in range(2)]

    def restricted(field):
        for i in range(2):
            lines = weighted([(RES[i, a], field[a]) for a in range(4)])
            for j in range(2):
                pair = weighted([(RES[j, b], lines[b]) for b in range(4)])
                turned = pltpu.roll(pair, 4, 1)
                value = (
                    res_same[0] * pair[0]
                    + res_cross[0] * turned[0]
                    + res_same[1] * pair[1]
                    + res_cross[1] * turned[1]
                )
                shuffle[pl.ds(8 * (2 * i + j), 8)] = value
        return jnp.stack([shuffle[pl.ds(r, 8, stride=4)] for r in range(ROWS)])

    def prolonged(rows):
        for r in range(ROWS):
            shuffle[pl.ds(r, 8, stride=4)] = rows[r]
        corners = []
        for index in range(4):
            value = shuffle[pl.ds(8 * index, 8)]
            turned = pltpu.roll(value, 4, 0)
            corners.append(jnp.stack([pro_same[i] * value + pro_cross[i] * turned for i in range(2)]))
        lines = [
            jnp.stack([weighted([(PRO[b, 0], corners[2 * i]), (PRO[b, 1], corners[2 * i + 1])]) for b in range(4)])
            for i in range(2)
        ]
        return [weighted([(PRO[a, 0], lines[0]), (PRO[a, 1], lines[1])]) for a in range(4)]

    coarse_coefficients(REACH, 0)

    @pl.when(n == 0)
    def _():
        for _, receives, make, _ in transfers["first_trace"]:
            when(receives, lambda make=make: make().wait_recv())
        duo_begin[0] = begin[...]
        interior(begin, duo_first.at[0])
        finish_rate(duo_first.at[0], recv.at[0, 3], recv.at[1, 3])

    duo_begin[1] = states[2]
    duo_first[1] = rates[2]
    duo_rates[0] = rates[...]
    duo_rates[1] = jnp.zeros((3,) + FIELD, jnp.float32)

    def duo_copy(k, d, slot):
        return remote(
            duo_send.at[k, slot],
            duo_recv.at[1 - k, slot],
            duo_out.at[k, slot],
            duo_in.at[1 - k, slot],
            (n, s + d),
        )

    def duo_launch(slot):
        for k, d in enumerate((-1, 1)):
            pl.when(has[d])(lambda k=k, d=d: duo_copy(k, d, slot).start())

    def duo_await(slot):
        for k, d in enumerate((-1, 1)):
            pl.when(has[-d])(lambda k=k, d=d: duo_copy(k, d, slot).wait_recv())

    def duo_fresh(target, factor, rate, slot, halo):
        def outer(x, carry):
            if halo is None:
                lower, upper = rate(x)[0], rate(x)[3]
            else:
                lower, upper = finish_rate(rate(x), duo_recv.at[0, halo, x], duo_recv.at[1, halo, x])
            first = duo_base[x, 0] + factor * lower
            last = duo_base[x, 3] + factor * upper
            target[x, 0] = first
            target[x, 3] = last
            pack(first, last, duo_send.at[0, slot, x], duo_send.at[1, slot, x])
            return carry

        def inner(x, carry):
            target[x, 1:3] = duo_base[x, 1:3] + factor * rate(x)[1:3]
            return carry

        lax.fori_loop(0, 2, outer, 0)
        duo_launch(slot)
        lax.fori_loop(0, 2, inner, 0)

    def opening(x, carry):
        duo_base[x] = (
            duo_begin[x]
            - DT * duo_rates[x, 0]
            + (H / 24.0) * (5.0 * duo_rates[x, 0] + 8.0 * duo_rates[x, 1] - duo_rates[x, 2])
        )
        return carry

    lax.fori_loop(0, 2, opening, 0)
    duo_fresh(duo_mid, DT, lambda x: duo_first.at[x], 0, None)

    def duo_closing(slot):
        def prepare(x, carry):
            duo_base[x] = (
                duo_mid[x]
                - DT * duo_rates[x, 1]
                + (H / 24.0) * (8.0 * duo_rates[x, 1] + 5.0 * duo_rates[x, 2] - duo_rates[x, 0])
            )
            interior(duo_mid.at[x], duo_rates.at[x, 1])
            return carry

        lax.fori_loop(0, 2, prepare, 0)
        duo_await(slot)
        duo_fresh(duo_end, DT, lambda x: duo_rates.at[x, 1], slot + 1, slot)

    def duo_middle(slot):
        def prepare(x, carry):
            duo_base[x] = duo_begin[x] + (H / 24.0) * (5.0 * duo_first[x] + 8.0 * duo_rates[x, 1])
            interior(duo_end.at[x], duo_rates.at[x, 2])
            return carry

        lax.fori_loop(0, 2, prepare, 0)
        duo_await(slot)
        duo_fresh(duo_mid, -H / 24.0, lambda x: duo_rates.at[x, 2], slot + 1, slot)

    def fine_copy(k, d, slot):
        return remote(
            send.at[k, slot],
            recv.at[1 - k, slot],
            fine_send.at[k, slot],
            fine_recv.at[1 - k, slot],
            (n, s + d),
        )

    def launch(slot):
        for k, d in enumerate((-1, 1)):
            pl.when(has[d])(lambda k=k, d=d: fine_copy(k, d, slot).start())

    def await_fine(slot):
        for k, d in enumerate((-1, 1)):
            pl.when(has[-d])(lambda k=k, d=d: fine_copy(k, d, slot).wait_recv())

    def fresh(u, origin, factor, rate, lower, upper, slot):
        first = origin[0] + factor * lower
        last = origin[3] + factor * upper
        u[0] = first
        u[3] = last
        if slot is not None:
            pack(first, last, send.at[0, slot], send.at[1, slot])
            launch(slot)
        u[1:3] = origin[1:3] + factor * rate[1:3]

    def to_closing(slot, out_slot):
        base[...] = (
            mid_state[...]
            - DT * rates[1]
            + (H / 24.0) * (8.0 * rates[1] + 5.0 * rates[2] - rates[0])
        )
        interior(mid_state, rates.at[1])
        await_fine(slot)
        lower, upper = finish_rate(rates.at[1], recv.at[0, slot], recv.at[1, slot])
        fresh(end_state, base, DT, rates.at[1], lower, upper, out_slot)

    def to_middle(slot):
        base[...] = begin[...] + (H / 24.0) * (5.0 * first_rate[...] + 8.0 * rates[1])
        interior(end_state, rates.at[2])
        await_fine(slot)
        lower, upper = finish_rate(rates.at[2], recv.at[0, slot], recv.at[1, slot])
        fresh(mid_state, base, -H / 24.0, rates.at[2], lower, upper, slot + 1)

    duo_closing(0)
    for x in range(2):
        duo_rates[x, 0] = duo_first[x]
        old0[x, 1 : ROWS + 1] = restricted(duo_begin.at[x])
    start("row0")
    start("flow1")
    duo_middle(1)
    duo_closing(2)

    arrive("begin_trace")
    arrive("begin")
    interior(begin, first_rate)
    lower, upper = finish_rate(first_rate, recv.at[0, 3], recv.at[1, 3])

    base[...] = base[...] + begin[...]
    fresh(mid_state, base, DT, first_rate, lower, upper, 4)

    duo_middle(3)
    to_closing(4, 5)
    rates[0] = first_rate[...]
    duo_closing(4)
    for x in range(2):
        old1[x, 1 : ROWS + 1] = restricted(duo_end.at[x])
    start("row1")
    to_middle(5)

    def last_rate(x, carry):
        interior(duo_end.at[x], duo_rates.at[x, 2])
        return carry

    lax.fori_loop(0, 2, last_rate, 0)
    arrive("row0")
    low = MID - 1
    h_rates0 = [advance(old0[x], low) - old0[x, 1 : ROWS + 1] for x in range(2)]
    duo_await(5)
    offsets = []
    for x in range(2):
        finish_rate(duo_rates.at[x, 2], duo_recv.at[0, 5, x], duo_recv.at[1, 5, x])
    quadratures = [
        restricted(
            [
                (H / 6.0) * (duo_first[x, a] + 4.0 * duo_rates[x, 1, a] + duo_rates[x, 2, a])
                for a in range(4)
            ]
        )
        for x in range(2)
    ]
    arrive("row1")
    for x in (1, 0):
        h_rate0 = h_rates0[x]
        h_rate1 = advance(old1[x], low) - old1[x, 1 : ROWS + 1]
        trapezoid = 0.5 * (h_rate0 + h_rate1)
        offset = -h_rate0 + trapezoid + (quadratures[x] - trapezoid)
        if x == 1:
            leaving[...] = offset
            start("hop")
    is_first = n == 0
    offset = offset + jnp.where(is_first, old0[0, 1 : ROWS + 1] + h_rates0[0], 0.0)

    to_closing(6, 7)
    arrive("hop")
    group[z, pl.ds(ROWS, ROWS)] = offset + passed[...]
    start("group")
    start("flow2")

    to_middle(7)
    for j in range(GROUP):

        @pl.when(z != j)
        def _():
            remote(
                group.at[j, pl.ds(ROWS, ROWS)],
                group.at[j, pl.ds(ROWS, ROWS)],
                group_send.at[0],
                group_recv.at[(z + GROUP - 1 - j) % GROUP],
                (n, s),
            ).wait_recv()

        if j < GROUP - 1:
            start(f"side{j}")
    start("flow3")
    arrive("flow1")
    coarse_coefficients(REACH - 1, 0)
    coarse_coefficients(REACH + 1, 0)
    to_closing(8, None)
    stores = [
        pltpu.make_async_copy(field, fields_hbm.at[index], store_sem.at[3 + index])
        for index, field in enumerate((begin, mid_state, end_state))
    ]
    for store in stores:
        store.start()
    before0 = restricted(begin)
    before1 = restricted(end_state)
    for j in range(GROUP - 1):
        arrive(f"side{j}")
    y = group[0]
    y = advance(y, MID - 4) + group[1, 1:11]
    y = advance(y, MID - 3) + group[2, 2:10]
    y = advance(y, MID - 2)[1:5] + group[3, 4:8]
    partial[...] = y
    start("part")
    arrive("flow2")
    arrive("flow3")
    lax.fori_loop(0, REACH - 1, coarse_coefficients, 0)
    lax.fori_loop(REACH + 2, 2 * REACH + 1, coarse_coefficients, 0)
    arrive("part")
    y = far[...]
    for step in range(4):
        y = advance(y, step)
    y = y + mid[...]
    for step in range(4, 8):
        y = advance(y, step)
    y = y + near[...]
    for j in range(3):
        count = 12 - 2 * j
        stepped = advance(y, MID - 4 + j) + group[j, j + 1 : 11 - j]
        y = jnp.where(z > j, stepped, y[1 : count - 1])
    finish = advance(y, MID - 1) + group[z, pl.ds(ROWS, ROWS)]
    begin_rows = jnp.where(is_first, before0, y[1:5])
    delta0 = begin_rows - before0
    delta1 = finish - before1

    for index, delta in enumerate((delta0, 0.5 * (delta0 + delta1), delta1)):
        lifted = prolonged(delta)
        for a in range(4):
            result[index, a] = lifted[a]
        pltpu.make_async_copy(result.at[index], lifted_hbm.at[index], store_sem.at[index]).start()
    for index in range(3):
        pltpu.make_async_copy(result.at[index], lifted_hbm.at[index], store_sem.at[index]).wait()
    for store in stores:
        store.wait()

    for name in transfers:
        sent(name)
    for k, d in enumerate((-1, 1)):
        for slot in range(4, 9):
            pl.when(has[d])(lambda k=k, d=d, slot=slot: fine_copy(k, d, slot).wait_send())
        for slot in range(6):
            pl.when(has[d])(lambda k=k, d=d, slot=slot: duo_copy(k, d, slot).wait_send())


def solution(mesh):
    steps = mesh.shape["tm"]
    columns = mesh.shape["space"]

    def body(node_states, initial_state, velocity):
        states = node_states.reshape((3,) + FIELD)
        first = initial_state.reshape(FIELD)
        wind = velocity.reshape(3, 4, 4, 16, LANES)
        f32 = jnp.float32
        vmem = lambda *shape: pltpu.VMEM(shape, f32)
        dma = lambda *shape: pltpu.SemaphoreType.DMA(shape)
        fields, lifted = pl.pallas_call(
            functools.partial(kernel, steps, columns),
            out_shape=[jax.ShapeDtypeStruct((3,) + FIELD, f32)] * 2,
            in_specs=[pl.BlockSpec(memory_space=pltpu.HBM)] * 3,
            out_specs=[pl.BlockSpec(memory_space=pl.ANY)] * 2,
            scratch_shapes=[
                vmem(3, *FIELD),
                pltpu.VMEM((3, 4, 4, 16, LANES), jnp.bfloat16),
                vmem(*FIELD),
                vmem(3, *FIELD),
                vmem(*FIELD),
                vmem(4, 2, 8, LANES),
                vmem(4, 2, 8, LANES),
                vmem(4, 2, 8, LANES),
                vmem(4, 2, 8, LANES),
                vmem(4, 2, 8, LANES),
                vmem(4, 2, 8, LANES),
                vmem(4, 4, 8, LANES),
                vmem(4, 4, 8, LANES),
                vmem(3, *FIELD),
                vmem(*FIELD),
                vmem(*FIELD),
                vmem(*FIELD),
                vmem(*FIELD),
                vmem(2, 9, 2, 8, LANES),
                vmem(2, 9, 2, 8, LANES),
                vmem(2, *FIELD),
                vmem(2, *FIELD),
                vmem(2, 3, *FIELD),
                vmem(2, *FIELD),
                vmem(2, *FIELD),
                vmem(2, *FIELD),
                vmem(2, 6, 2, 2, 8, LANES),
                vmem(2, 6, 2, 2, 8, LANES),
                vmem(ROWS, 8, LANES),
                vmem(ROWS, 8, LANES),
                vmem(32, LANES),
                vmem(2 * REACH + 1, ROWS, 3, 8, LANES),
                vmem(7, 2 * REACH + 1, ROWS, 8, LANES),
                vmem(2, ROWS + 2, 8, LANES),
                vmem(2, ROWS + 2, 8, LANES),
                vmem(GROUP, 3 * ROWS, 8, LANES),
                vmem(ROWS, 8, LANES),
                vmem(3 * ROWS, 8, LANES),
                vmem(5 * ROWS, 8, LANES),
                vmem(7 * ROWS, 8, LANES),
                vmem(3, *FIELD),
                dma(3),
                dma(6),
                dma(2, 9),
                dma(2, 9),
                dma(2, 6),
                dma(2, 6),
                pltpu.SemaphoreType.DMA,
                pltpu.SemaphoreType.DMA,
                pltpu.SemaphoreType.DMA,
                pltpu.SemaphoreType.DMA,
                dma(6),
                dma(6),
                dma(2, 2),
                dma(2, 2),
                dma(3),
                dma(3),
                dma(2, GROUP),
                dma(2, GROUP),
                dma(15),
                dma(15),
            ],
            compiler_params=pltpu.CompilerParams(
                collective_id=0, has_side_effects=True, vmem_limit_bytes=60 * 1024 * 1024
            ),
        )(states, first, wind)
        return (fields + lifted).reshape(1, 3, 64, ROWS, LANES)

    return jax.shard_map(
        body,
        mesh=mesh,
        in_specs=(
            P("tm", None, None, "space", None),
            P(None, "space", None),
            P(None, None, "space", None),
        ),
        out_specs=P("tm", None, None, "space", None),
        check_vma=False,
    )
```

```python
import functools

import jax
import jax.numpy as jnp
import numpy as np
from jax import lax
from jax.experimental import pallas as pl
from jax.experimental.pallas import tpu as pltpu
from jax.sharding import PartitionSpec as P

MESH = pl.DeviceIdType.MESH
CZ = 16
LANES = 128
GROUP = 4
H = 0.08
DT = 0.5 * H
LIFT = 6.0
ROWS = 4
REACH = 1
SPAN = (2 * REACH + 1) * ROWS
MID = REACH * ROWS
FIELD = (4, 4, 2, 8, LANES)


def lagrange_derivative(points):
    number = len(points)
    weights = np.array(
        [1.0 / np.prod([points[i] - points[j] for j in range(number) if j != i]) for i in range(number)]
    )
    derivative = np.zeros((number, number))
    for i in range(number):
        for j in range(number):
            if i != j:
                derivative[i, j] = weights[j] / weights[i] / (points[i] - points[j])
        derivative[i, i] = -np.sum(derivative[i])
    return derivative


POINTS = np.array([-1.0, -1.0 / np.sqrt(5.0), 1.0 / np.sqrt(5.0), 1.0])
WEIGHTS = np.array([1.0, 5.0, 5.0, 1.0]) / 6.0
DER = lagrange_derivative(POINTS)
PRO = np.stack([(1.0 - POINTS) / 2.0, (1.0 + POINTS) / 2.0], axis=1)
RES = PRO.T * WEIGHTS[None, :]


def weighted(terms):
    total = None
    for factor, value in terms:
        factor = float(factor)
        if abs(factor) < 1e-12:
            continue
        piece = value if factor == 1.0 else factor * value
        total = piece if total is None else total + piece
    return total


def kernel(
    steps,
    columns,
    states_hbm,
    start_hbm,
    wind_hbm,
    fields_hbm,
    lifted_hbm,
    states,
    wind,
    begin,
    nv,
    diag,
    xli,
    xhi,
    xlh,
    xhh,
    yl,
    yh,
    zl,
    zh,
    rates,
    first_rate,
    mid_state,
    end_state,
    base,
    send,
    recv,
    duo_begin,
    duo_first,
    duo_rates,
    duo_mid,
    duo_end,
    duo_base,
    duo_send,
    duo_recv,
    leaving,
    passed,
    shuffle,
    flows,
    coef,
    old0,
    old1,
    group,
    partial,
    near,
    result,
    load_sem,
    store_sem,
    fine_send,
    fine_recv,
    duo_out,
    duo_in,
    hop_send,
    hop_recv,
    begin_send,
    begin_recv,
    flow_send,
    flow_recv,
    row_send,
    row_recv,
    group_send,
    group_recv,
    side_send,
    side_recv,
    part_send,
    part_recv,
):
    n = lax.axis_index("tm")
    s = lax.axis_index("space")
    g = n // GROUP
    z = n % GROUP
    groups = steps // GROUP

    sub = lax.broadcasted_iota(jnp.int32, (8, LANES), 0)
    lane = lax.broadcasted_iota(jnp.int32, (8, LANES), 1)
    parity = sub // 4
    row = sub % 4

    def split(even, odd):
        return jnp.where(parity == 0, jnp.float32(even), jnp.float32(odd))

    def remote(src, dst, ssem, rsem, device):
        return pltpu.make_async_remote_copy(
            src_ref=src, dst_ref=dst, send_sem=ssem, recv_sem=rsem, device_id=device, device_id_type=MESH
        )

    has = {-1: s > 0, 1: s < columns - 1}

    def inside(d):
        if d == 0:
            return None
        return s + d >= 0 if d < 0 else s + d < columns

    def both(a, b):
        if a is None:
            return b
        if b is None:
            return a
        return jnp.logical_and(a, b)

    def when(cond, run):
        if cond is None:
            run()
        else:
            pl.when(cond)(run)

    transfers = {}

    def add(name, sends, receives, make, partner):
        transfers.setdefault(name, []).append((sends, receives, make, partner))

    for k, d in enumerate((-1, 1)):
        add(
            "states",
            has[d],
            has[-d],
            functools.partial(
                remote,
                send.at[k, pl.ds(0, 3)],
                recv.at[1 - k, pl.ds(0, 3)],
                fine_send.at[k, 0],
                fine_recv.at[1 - k, 0],
                (n, s + d),
            ),
            None,
        )
        add(
            "begin_trace",
            both(n < steps - 1, has[d]),
            both(n > 0, has[-d]),
            functools.partial(
                remote,
                send.at[k, 2],
                recv.at[1 - k, 3],
                fine_send.at[k, 1],
                fine_recv.at[1 - k, 1],
                (n + 1, s + d),
            ),
            (n - 1, s - d),
        )
        add(
            "first_trace",
            both(n == 0, has[d]),
            both(n == 0, has[-d]),
            functools.partial(
                remote,
                send.at[k, 3],
                recv.at[1 - k, 3],
                fine_send.at[k, 2],
                fine_recv.at[1 - k, 1],
                (n, s + d),
            ),
            None,
        )
        for index, buffer in enumerate((old0, old1)):
            add(
                f"row{index}",
                has[d],
                has[-d],
                functools.partial(
                    remote,
                    buffer.at[:, 1 if d < 0 else ROWS],
                    buffer.at[:, ROWS + 1 if d < 0 else 0],
                    row_send.at[k, index],
                    row_recv.at[1 - k, index],
                    (n, s + d),
                ),
                None,
            )
        for j in range(GROUP - 1):
            rows = 3 - j
            add(
                f"side{j}",
                has[d],
                has[-d],
                functools.partial(
                    remote,
                    group.at[j, pl.ds(ROWS if d < 0 else 2 * ROWS - rows, rows)],
                    group.at[j, pl.ds(2 * ROWS if d < 0 else ROWS - rows, rows)],
                    side_send.at[k, j],
                    side_recv.at[1 - k, j],
                    (n, s + d),
                ),
                None,
            )
    add(
        "begin",
        n < steps - 1,
        n > 0,
        functools.partial(remote, states_hbm.at[2], begin, begin_send, begin_recv, (n + 1, s)),
        (n - 1, s),
    )
    add(
        "hop",
        n < steps - 1,
        n > 0,
        functools.partial(remote, leaving, passed, hop_send, hop_recv, (n + 1, s)),
        None,
    )
    for index, d in enumerate((-1, 1)):
        edge = pl.ds(0 if d < 0 else 1, ROWS - 1)
        add(
            "flow",
            has[d],
            has[-d],
            functools.partial(
                remote,
                flows.at[REACH, edge],
                flows.at[REACH - d, edge],
                flow_send.at[index],
                flow_recv.at[index],
                (n, s + d),
            ),
            None,
        )
    for shift in (1, 2, 3):
        add(
            "group",
            None,
            None,
            functools.partial(
                remote,
                group.at[z, pl.ds(ROWS, ROWS)],
                group.at[z, pl.ds(ROWS, ROWS)],
                group_send.at[shift - 1],
                group_recv.at[shift - 1],
                (g * GROUP + (z + shift) % GROUP, s),
            ),
            (g * GROUP + (z + GROUP - shift) % GROUP, s),
        )
    for d in (-1, 0, 1):
        add(
            "part",
            both(g < groups - 1, inside(d)),
            both(g > 0, inside(-d)),
            functools.partial(
                remote,
                partial,
                near.at[pl.ds((1 - d) * ROWS, ROWS)],
                part_send.at[d + 1],
                part_recv.at[d + 1],
                (n + GROUP, s + d),
            ),
            (n - GROUP, s - d),
        )

    def start(name):
        for sends, _, make, _ in transfers[name]:
            when(sends, lambda make=make: make().start())

    def arrive(name):
        for _, receives, make, _ in transfers[name]:
            when(receives, lambda make=make: make().wait_recv())

    def sent(name):
        for sends, _, make, _ in transfers[name]:
            when(sends, lambda make=make: make().wait_send())

    load_states = pltpu.make_async_copy(states_hbm, states, load_sem.at[0])
    load_wind = pltpu.make_async_copy(wind_hbm, wind, load_sem.at[1])
    load_first = pltpu.make_async_copy(start_hbm, begin, load_sem.at[2])
    load_states.start()
    load_wind.start()
    pl.when(n == 0)(load_first.start)

    recv[...] = jnp.zeros(recv.shape, jnp.float32)
    duo_recv[...] = jnp.zeros(duo_recv.shape, jnp.float32)
    passed[...] = jnp.zeros(passed.shape, jnp.float32)
    duo_begin[0] = jnp.zeros(FIELD, jnp.float32)
    duo_first[0] = jnp.zeros(FIELD, jnp.float32)
    flows[...] = jnp.zeros(flows.shape, jnp.float32)
    old0[...] = jnp.zeros(old0.shape, jnp.float32)
    old1[...] = jnp.zeros(old1.shape, jnp.float32)
    group[...] = jnp.zeros(group.shape, jnp.float32)
    near[...] = jnp.zeros(near.shape, jnp.float32)

    barrier = pltpu.get_barrier_semaphore()
    expected = jnp.int32(0)

    def greet(cond, device):
        when(
            cond,
            lambda: pl.semaphore_signal(barrier, inc=1, device_id=device, device_id_type=MESH),
        )

    for d in (-1, 1):
        greet(has[d], (n, s + d))
        expected = expected + has[d].astype(jnp.int32)
    for name in ("begin_trace", "begin", "group", "part"):
        for sends, receives, _, partner in transfers[name]:
            greet(receives, partner)
            expected = expected + (1 if sends is None else sends.astype(jnp.int32))

    load_states.wait()

    def pack(lower, upper, low_to, high_to):
        for half in range(2):
            low = None
            high = None
            for r in range(4):
                b, hh = (4 * half + r) // 2, r % 2
                lv = lower[b, hh]
                hv = upper[b, hh]
                lv = pltpu.roll(lv, r, 0) if r else lv
                hv = pltpu.roll(hv, (r + 5) % 8, 0) if r != 3 else hv
                low = lv if low is None else jnp.where(row == r, lv, low)
                high = hv if high is None else jnp.where(row == r, hv, high)
            low_to[half] = low
            high_to[half] = high

    def unpack(low_from, high_from):
        lows, highs = [], []
        for t in range(8):
            half, r = t // 4, t % 4
            lv = low_from[half]
            hv = high_from[half]
            lows.append(pltpu.roll(lv, 8 - r, 0) if r else lv)
            highs.append(pltpu.roll(hv, 3 - r, 0) if r != 3 else hv)
        return (
            jnp.stack(lows).reshape(4, 2, 8, LANES),
            jnp.stack(highs).reshape(4, 2, 8, LANES),
        )

    for k in range(3):
        pack(states[k, 0], states[k, 3], send.at[0, k], send.at[1, k])

    @pl.when(n == 0)
    def _():
        load_first.wait()
        pack(begin[0], begin[3], send.at[0, 3], send.at[1, 3])

    pl.semaphore_wait(barrier, expected)
    start("begin_trace")
    start("first_trace")
    start("states")
    start("begin")

    load_wind.wait()
    for axis in range(3):
        nv[axis] = -wind[axis].astype(jnp.float32).reshape(FIELD)

    for axis in range(3):
        for i in range(2):
            for j in range(2):
                corner = jnp.where(parity == 0, nv[axis, 3 * i, 3 * j, 0], nv[axis, 3 * i, 3 * j, 1])
                shuffle[pl.ds(8 * (2 * i + j), 8)] = corner
        for r in range(ROWS):
            flows[REACH, r, axis] = shuffle[pl.ds(r, 8, stride=4)]

    cxl = LIFT * jnp.minimum(nv[0, 0], 0.0)
    cxh = LIFT * jnp.minimum(-nv[0, 3], 0.0)
    xli[...] = jnp.where(row > 0, -cxl, 0.0)
    xlh[...] = jnp.where(row == 0, -cxl, 0.0)
    xhi[...] = jnp.where(row < 3, -cxh, 0.0)
    xhh[...] = jnp.where(row == 3, -cxh, 0.0)
    cyl = LIFT * jnp.minimum(nv[1, :, 0], 0.0)
    cyh = LIFT * jnp.minimum(-nv[1, :, 3], 0.0)
    yl[...] = jnp.where(lane >= CZ, -cyl, 0.0)
    yh[...] = jnp.where(lane < LANES - CZ, -cyh, 0.0)
    czl = jnp.where(parity == 0, LIFT * jnp.minimum(nv[2, :, :, 0], 0.0), 0.0)
    czh = jnp.where(parity == 1, LIFT * jnp.minimum(-nv[2, :, :, 1], 0.0), 0.0)
    layer = lane % CZ
    zl[...] = jnp.where(layer > 0, -czl, 0.0)
    zh[...] = jnp.where(layer < CZ - 1, -czh, 0.0)
    diag[:, :, 0] = czl
    diag[:, :, 1] = czh
    diag[0] = diag[0] + cxl
    diag[3] = diag[3] + cxh
    diag[:, 0] = diag[:, 0] + cyl
    diag[:, 3] = diag[:, 3] + cyh

    same = [[split(DER[2 * i, 2 * j], DER[2 * i + 1, 2 * j + 1]) for j in range(2)] for i in range(2)]
    cross = [[split(DER[2 * i, 2 * j + 1], DER[2 * i + 1, 2 * j]) for j in range(2)] for i in range(2)]

    def interior(u, out):
        for b in range(4):
            pair = [u[:, b, 0], u[:, b, 1]]
            turned = [pltpu.roll(half, 4, 1) for half in pair]
            for i in range(2):
                own = pair[i]
                along_z = (
                    same[i][0] * pair[0]
                    + cross[i][0] * turned[0]
                    + same[i][1] * pair[1]
                    + cross[i][1] * turned[1]
                )
                total = diag[:, b, i] * own + nv[2, :, b, i] * along_z
                if i == 0:
                    total = total + zl[:, b] * pltpu.roll(turned[1], 1, 2)
                else:
                    total = total + zh[:, b] * pltpu.roll(turned[0], LANES - 1, 2)
                others = [own if c == b else u[:, c, i] for c in range(4)]
                along_y = weighted([(DER[b, c], others[c]) for c in range(4)])
                total = total + nv[1, :, b, i] * along_y
                if b == 0:
                    total = total + yl[:, i] * pltpu.roll(others[3], CZ, 2)
                if b == 3:
                    total = total + yh[:, i] * pltpu.roll(others[0], LANES - CZ, 2)
                along_x = jnp.stack([weighted([(DER[a, c], own[c]) for c in range(4)]) for a in range(4)])
                total = total + nv[0, :, b, i] * along_x
                out[0, b, i] = total[0] + xli[b, i] * pltpu.roll(own[3], 1, 0)
                out[1:3, b, i] = total[1:3]
                out[3, b, i] = total[3] + xhi[b, i] * pltpu.roll(own[0], 7, 0)

    def finish_rate(out, low_from, high_from):
        low, high = unpack(low_from, high_from)
        lower = out[0] + xlh[...] * low
        upper = out[3] + xhh[...] * high
        out[0] = lower
        out[3] = upper
        return lower, upper

    def old_rate(k, carry):
        interior(states.at[k], rates.at[k])
        return carry

    lax.fori_loop(0, 3, old_rate, 0)
    arrive("states")
    for k in range(3):
        finish_rate(rates.at[k], recv.at[0, k], recv.at[1, k])

    base[...] = -DT * rates[0] + (H / 24.0) * (5.0 * rates[0] + 8.0 * rates[1] - rates[2])

    top = (sub // 4) % 2 == 0
    middle = (sub // 2) % 2 == 0
    bottom = sub % 2 == 0
    signs = [jnp.where(bit, jnp.float32(-1.0), jnp.float32(1.0)) for bit in (top, middle, bottom)]
    open_y = jnp.logical_or(jnp.logical_and(middle, lane >= CZ), jnp.logical_and(jnp.logical_not(middle), lane < LANES - CZ))
    open_z = jnp.logical_or(jnp.logical_and(bottom, layer > 0), jnp.logical_and(jnp.logical_not(bottom), layer < CZ - 1))

    def coarse_coefficients(block, carry):
        wide = flows[block]
        center = jnp.ones((ROWS, 8, LANES), jnp.float32)
        for axis in range(3):
            slope = signs[axis] * wide[:, axis]
            jump = jnp.minimum(-slope, 0.0)
            center = center + H * (0.5 * slope + jump)
            coef[1 + axis, block] = (-0.5 * H) * slope
            outer = -H * jump
            if axis == 1:
                outer = jnp.where(open_y, outer, 0.0)
            if axis == 2:
                outer = jnp.where(open_z, outer, 0.0)
            coef[4 + axis, block] = outer
        coef[0, block] = center
        return carry

    def advance(u, low):
        count = u.shape[0]
        own = u[1 : count - 1]
        px = pltpu.roll(u, 4, 1)
        ox = jnp.where(top, px[0 : count - 2], px[2:count])
        px = px[1 : count - 1]
        py = jnp.where(middle, pltpu.roll(own, 6, 1), pltpu.roll(own, 2, 1))
        pz = jnp.where(bottom, pltpu.roll(own, 7, 1), pltpu.roll(own, 1, 1))
        oy = jnp.where(middle, pltpu.roll(py, CZ, 2), pltpu.roll(py, LANES - CZ, 2))
        oz = jnp.where(bottom, pltpu.roll(pz, 1, 2), pltpu.roll(pz, LANES - 1, 2))
        total = None
        for index, value in enumerate((own, px, py, pz, ox, oy, oz)):
            factors = coef[index].reshape(SPAN, 8, LANES)[low + 1 : low + count - 1]
            piece = factors * value
            total = piece if total is None else total + piece
        return total

    res_same = [split(RES[0, 2 * i], RES[1, 2 * i + 1]) for i in range(2)]
    res_cross = [split(RES[0, 2 * i + 1], RES[1, 2 * i]) for i in range(2)]
    pro_same = [split(PRO[2 * i, 0], PRO[2 * i + 1, 1]) for i in range(2)]
    pro_cross = [split(PRO[2 * i, 1], PRO[2 * i + 1, 0]) for i in range(2)]

    def restricted(field):
        for i in range(2):
            lines = weighted([(RES[i, a], field[a]) for a in range(4)])
            for j in range(2):
                pair = weighted([(RES[j, b], lines[b]) for b in range(4)])
                turned = pltpu.roll(pair, 4, 1)
                value = (
                    res_same[0] * pair[0]
                    + res_cross[0] * turned[0]
                    + res_same[1] * pair[1]
                    + res_cross[1] * turned[1]
                )
                shuffle[pl.ds(8 * (2 * i + j), 8)] = value
        return jnp.stack([shuffle[pl.ds(r, 8, stride=4)] for r in range(ROWS)])

    def prolonged(rows):
        for r in range(ROWS):
            shuffle[pl.ds(r, 8, stride=4)] = rows[r]
        corners = []
        for index in range(4):
            value = shuffle[pl.ds(8 * index, 8)]
            turned = pltpu.roll(value, 4, 0)
            corners.append(jnp.stack([pro_same[i] * value + pro_cross[i] * turned for i in range(2)]))
        lines = [
            jnp.stack([weighted([(PRO[b, 0], corners[2 * i]), (PRO[b, 1], corners[2 * i + 1])]) for b in range(4)])
            for i in range(2)
        ]
        return [weighted([(PRO[a, 0], lines[0]), (PRO[a, 1], lines[1])]) for a in range(4)]

    coarse_coefficients(REACH, 0)

    @pl.when(n == 0)
    def _():
        for _, receives, make, _ in transfers["first_trace"]:
            when(receives, lambda make=make: make().wait_recv())
        duo_begin[0] = begin[...]
        interior(begin, duo_first.at[0])
        finish_rate(duo_first.at[0], recv.at[0, 3], recv.at[1, 3])

    duo_begin[1] = states[2]
    duo_first[1] = rates[2]
    duo_rates[0] = rates[...]
    duo_rates[1] = jnp.zeros((3,) + FIELD, jnp.float32)

    def duo_copy(k, d, slot):
        return remote(
            duo_send.at[k, slot],
            duo_recv.at[1 - k, slot],
            duo_out.at[k, slot],
            duo_in.at[1 - k, slot],
            (n, s + d),
        )

    def duo_launch(slot):
        for k, d in enumerate((-1, 1)):
            pl.when(has[d])(lambda k=k, d=d: duo_copy(k, d, slot).start())

    def duo_await(slot):
        for k, d in enumerate((-1, 1)):
            pl.when(has[-d])(lambda k=k, d=d: duo_copy(k, d, slot).wait_recv())

    def duo_fresh(target, factor, rate, slot, halo):
        def outer(x, carry):
            if halo is None:
                lower, upper = rate(x)[0], rate(x)[3]
            else:
                lower, upper = finish_rate(rate(x), duo_recv.at[0, halo, x], duo_recv.at[1, halo, x])
            first = duo_base[x, 0] + factor * lower
            last = duo_base[x, 3] + factor * upper
            target[x, 0] = first
            target[x, 3] = last
            pack(first, last, duo_send.at[0, slot, x], duo_send.at[1, slot, x])
            return carry

        def inner(x, carry):
            target[x, 1:3] = duo_base[x, 1:3] + factor * rate(x)[1:3]
            return carry

        lax.fori_loop(0, 2, outer, 0)
        duo_launch(slot)
        lax.fori_loop(0, 2, inner, 0)

    def opening(x, carry):
        duo_base[x] = (
            duo_begin[x]
            - DT * duo_rates[x, 0]
            + (H / 24.0) * (5.0 * duo_rates[x, 0] + 8.0 * duo_rates[x, 1] - duo_rates[x, 2])
        )
        return carry

    lax.fori_loop(0, 2, opening, 0)
    duo_fresh(duo_mid, DT, lambda x: duo_first.at[x], 0, None)

    def duo_closing(slot):
        def prepare(x, carry):
            duo_base[x] = (
                duo_mid[x]
                - DT * duo_rates[x, 1]
                + (H / 24.0) * (8.0 * duo_rates[x, 1] + 5.0 * duo_rates[x, 2] - duo_rates[x, 0])
            )
            interior(duo_mid.at[x], duo_rates.at[x, 1])
            return carry

        lax.fori_loop(0, 2, prepare, 0)
        duo_await(slot)
        duo_fresh(duo_end, DT, lambda x: duo_rates.at[x, 1], slot + 1, slot)

    def duo_middle(slot):
        def prepare(x, carry):
            duo_base[x] = duo_begin[x] + (H / 24.0) * (5.0 * duo_first[x] + 8.0 * duo_rates[x, 1])
            interior(duo_end.at[x], duo_rates.at[x, 2])
            return carry

        lax.fori_loop(0, 2, prepare, 0)
        duo_await(slot)
        duo_fresh(duo_mid, -H / 24.0, lambda x: duo_rates.at[x, 2], slot + 1, slot)

    def fine_copy(k, d, slot):
        return remote(
            send.at[k, slot],
            recv.at[1 - k, slot],
            fine_send.at[k, slot],
            fine_recv.at[1 - k, slot],
            (n, s + d),
        )

    def launch(slot):
        for k, d in enumerate((-1, 1)):
            pl.when(has[d])(lambda k=k, d=d: fine_copy(k, d, slot).start())

    def await_fine(slot):
        for k, d in enumerate((-1, 1)):
            pl.when(has[-d])(lambda k=k, d=d: fine_copy(k, d, slot).wait_recv())

    def fresh(u, origin, factor, rate, lower, upper, slot):
        first = origin[0] + factor * lower
        last = origin[3] + factor * upper
        u[0] = first
        u[3] = last
        if slot is not None:
            pack(first, last, send.at[0, slot], send.at[1, slot])
            launch(slot)
        u[1:3] = origin[1:3] + factor * rate[1:3]

    def to_closing(slot, out_slot):
        base[...] = (
            mid_state[...]
            - DT * rates[1]
            + (H / 24.0) * (8.0 * rates[1] + 5.0 * rates[2] - rates[0])
        )
        interior(mid_state, rates.at[1])
        await_fine(slot)
        lower, upper = finish_rate(rates.at[1], recv.at[0, slot], recv.at[1, slot])
        fresh(end_state, base, DT, rates.at[1], lower, upper, out_slot)

    def to_middle(slot):
        base[...] = begin[...] + (H / 24.0) * (5.0 * first_rate[...] + 8.0 * rates[1])
        interior(end_state, rates.at[2])
        await_fine(slot)
        lower, upper = finish_rate(rates.at[2], recv.at[0, slot], recv.at[1, slot])
        fresh(mid_state, base, -H / 24.0, rates.at[2], lower, upper, slot + 1)

    duo_closing(0)
    for x in range(2):
        duo_rates[x, 0] = duo_first[x]
        old0[x, 1 : ROWS + 1] = restricted(duo_begin.at[x])
    start("row0")
    start("flow")
    duo_middle(1)
    duo_closing(2)

    arrive("begin_trace")
    arrive("begin")
    interior(begin, first_rate)
    lower, upper = finish_rate(first_rate, recv.at[0, 3], recv.at[1, 3])

    base[...] = base[...] + begin[...]
    fresh(mid_state, base, DT, first_rate, lower, upper, 4)

    duo_middle(3)
    to_closing(4, 5)
    rates[0] = first_rate[...]
    duo_closing(4)
    for x in range(2):
        old1[x, 1 : ROWS + 1] = restricted(duo_end.at[x])
    start("row1")
    to_middle(5)

    def last_rate(x, carry):
        interior(duo_end.at[x], duo_rates.at[x, 2])
        return carry

    lax.fori_loop(0, 2, last_rate, 0)
    arrive("row0")
    low = MID - 1
    h_rates0 = [advance(old0[x], low) - old0[x, 1 : ROWS + 1] for x in range(2)]
    duo_await(5)
    offsets = []
    for x in range(2):
        finish_rate(duo_rates.at[x, 2], duo_recv.at[0, 5, x], duo_recv.at[1, 5, x])
    quadratures = [
        restricted(
            [
                (H / 6.0) * (duo_first[x, a] + 4.0 * duo_rates[x, 1, a] + duo_rates[x, 2, a])
                for a in range(4)
            ]
        )
        for x in range(2)
    ]
    arrive("row1")
    for x in (1, 0):
        h_rate0 = h_rates0[x]
        h_rate1 = advance(old1[x], low) - old1[x, 1 : ROWS + 1]
        trapezoid = 0.5 * (h_rate0 + h_rate1)
        offset = -h_rate0 + trapezoid + (quadratures[x] - trapezoid)
        if x == 1:
            leaving[...] = offset
            start("hop")
    is_first = n == 0
    offset = offset + jnp.where(is_first, old0[0, 1 : ROWS + 1] + h_rates0[0], 0.0)

    to_closing(6, 7)
    arrive("hop")
    group[z, pl.ds(ROWS, ROWS)] = offset + passed[...]
    start("group")

    to_middle(7)
    for j in range(GROUP):

        @pl.when(z != j)
        def _():
            remote(
                group.at[j, pl.ds(ROWS, ROWS)],
                group.at[j, pl.ds(ROWS, ROWS)],
                group_send.at[0],
                group_recv.at[(z + GROUP - 1 - j) % GROUP],
                (n, s),
            ).wait_recv()

        if j < GROUP - 1:
            start(f"side{j}")
    arrive("flow")
    coarse_coefficients(REACH - 1, 0)
    coarse_coefficients(REACH + 1, 0)
    to_closing(8, None)
    stores = [
        pltpu.make_async_copy(field, fields_hbm.at[index], store_sem.at[3 + index])
        for index, field in enumerate((begin, mid_state, end_state))
    ]
    for store in stores:
        store.start()
    before0 = restricted(begin)
    before1 = restricted(end_state)
    for j in range(GROUP - 1):
        arrive(f"side{j}")
    arrive("part")
    y = near[...]
    line = [y[4:8]]
    for j in range(GROUP):
        y = advance(y, j) + group[j, j + 1 : 11 - j]
        line.append(y[3 - j : 7 - j])
    partial[...] = y
    start("part")
    begin_rows, finish = line[0], line[1]
    for j in range(1, GROUP):
        begin_rows = jnp.where(z == j, line[j], begin_rows)
        finish = jnp.where(z == j, line[j + 1], finish)
    begin_rows = jnp.where(is_first, before0, begin_rows)
    delta0 = begin_rows - before0
    delta1 = finish - before1

    for index, delta in enumerate((delta0, 0.5 * (delta0 + delta1), delta1)):
        lifted = prolonged(delta)
        for a in range(4):
            result[index, a] = lifted[a]
        pltpu.make_async_copy(result.at[index], lifted_hbm.at[index], store_sem.at[index]).start()
    for index in range(3):
        pltpu.make_async_copy(result.at[index], lifted_hbm.at[index], store_sem.at[index]).wait()
    for store in stores:
        store.wait()

    for name in transfers:
        sent(name)
    for k, d in enumerate((-1, 1)):
        for slot in range(4, 9):
            pl.when(has[d])(lambda k=k, d=d, slot=slot: fine_copy(k, d, slot).wait_send())
        for slot in range(6):
            pl.when(has[d])(lambda k=k, d=d, slot=slot: duo_copy(k, d, slot).wait_send())


def solution(mesh):
    steps = mesh.shape["tm"]
    columns = mesh.shape["space"]

    def body(node_states, initial_state, velocity):
        states = node_states.reshape((3,) + FIELD)
        first = initial_state.reshape(FIELD)
        wind = velocity.reshape(3, 4, 4, 16, LANES)
        f32 = jnp.float32
        vmem = lambda *shape: pltpu.VMEM(shape, f32)
        dma = lambda *shape: pltpu.SemaphoreType.DMA(shape)
        fields, lifted = pl.pallas_call(
            functools.partial(kernel, steps, columns),
            out_shape=[jax.ShapeDtypeStruct((3,) + FIELD, f32)] * 2,
            in_specs=[pl.BlockSpec(memory_space=pltpu.HBM)] * 3,
            out_specs=[pl.BlockSpec(memory_space=pl.ANY)] * 2,
            scratch_shapes=[
                vmem(3, *FIELD),
                pltpu.VMEM((3, 4, 4, 16, LANES), jnp.bfloat16),
                vmem(*FIELD),
                vmem(3, *FIELD),
                vmem(*FIELD),
                vmem(4, 2, 8, LANES),
                vmem(4, 2, 8, LANES),
                vmem(4, 2, 8, LANES),
                vmem(4, 2, 8, LANES),
                vmem(4, 2, 8, LANES),
                vmem(4, 2, 8, LANES),
                vmem(4, 4, 8, LANES),
                vmem(4, 4, 8, LANES),
                vmem(3, *FIELD),
                vmem(*FIELD),
                vmem(*FIELD),
                vmem(*FIELD),
                vmem(*FIELD),
                vmem(2, 9, 2, 8, LANES),
                vmem(2, 9, 2, 8, LANES),
                vmem(2, *FIELD),
                vmem(2, *FIELD),
                vmem(2, 3, *FIELD),
                vmem(2, *FIELD),
                vmem(2, *FIELD),
                vmem(2, *FIELD),
                vmem(2, 6, 2, 2, 8, LANES),
                vmem(2, 6, 2, 2, 8, LANES),
                vmem(ROWS, 8, LANES),
                vmem(ROWS, 8, LANES),
                vmem(32, LANES),
                vmem(2 * REACH + 1, ROWS, 3, 8, LANES),
                vmem(7, 2 * REACH + 1, ROWS, 8, LANES),
                vmem(2, ROWS + 2, 8, LANES),
                vmem(2, ROWS + 2, 8, LANES),
                vmem(GROUP, 3 * ROWS, 8, LANES),
                vmem(ROWS, 8, LANES),
                vmem(3 * ROWS, 8, LANES),
                vmem(3, *FIELD),
                dma(3),
                dma(6),
                dma(2, 9),
                dma(2, 9),
                dma(2, 6),
                dma(2, 6),
                pltpu.SemaphoreType.DMA,
                pltpu.SemaphoreType.DMA,
                pltpu.SemaphoreType.DMA,
                pltpu.SemaphoreType.DMA,
                dma(2),
                dma(2),
                dma(2, 2),
                dma(2, 2),
                dma(3),
                dma(3),
                dma(2, GROUP),
                dma(2, GROUP),
                dma(3),
                dma(3),
            ],
            compiler_params=pltpu.CompilerParams(
                collective_id=0, has_side_effects=True, vmem_limit_bytes=60 * 1024 * 1024
            ),
        )(states, first, wind)
        return (fields + lifted).reshape(1, 3, 64, ROWS, LANES)

    return jax.shard_map(
        body,
        mesh=mesh,
        in_specs=(
            P("tm", None, None, "space", None),
            P(None, "space", None),
            P(None, None, "space", None),
        ),
        out_specs=P("tm", None, None, "space", None),
        check_vma=False,
    )
```

```python
import functools

import jax
import jax.numpy as jnp
import numpy as np
from jax import lax
from jax.experimental import pallas as pl
from jax.experimental.pallas import tpu as pltpu
from jax.sharding import PartitionSpec as P

MESH = pl.DeviceIdType.MESH
CZ = 16
LANES = 128
GROUP = 4
H = 0.08
DT = 0.5 * H
LIFT = 6.0
ROWS = 4
REACH = 3
SPAN = (2 * REACH + 1) * ROWS
MID = REACH * ROWS
FIELD = (4, 4, 2, 8, LANES)


def lagrange_derivative(points):
    number = len(points)
    weights = np.array(
        [1.0 / np.prod([points[i] - points[j] for j in range(number) if j != i]) for i in range(number)]
    )
    derivative = np.zeros((number, number))
    for i in range(number):
        for j in range(number):
            if i != j:
                derivative[i, j] = weights[j] / weights[i] / (points[i] - points[j])
        derivative[i, i] = -np.sum(derivative[i])
    return derivative


POINTS = np.array([-1.0, -1.0 / np.sqrt(5.0), 1.0 / np.sqrt(5.0), 1.0])
WEIGHTS = np.array([1.0, 5.0, 5.0, 1.0]) / 6.0
DER = lagrange_derivative(POINTS)
PRO = np.stack([(1.0 - POINTS) / 2.0, (1.0 + POINTS) / 2.0], axis=1)
RES = PRO.T * WEIGHTS[None, :]


def weighted(terms):
    total = None
    for factor, value in terms:
        factor = float(factor)
        if abs(factor) < 1e-12:
            continue
        piece = value if factor == 1.0 else factor * value
        total = piece if total is None else total + piece
    return total


def kernel(
    steps,
    columns,
    states_hbm,
    start_hbm,
    wind_hbm,
    fields_hbm,
    lifted_hbm,
    states,
    wind,
    begin,
    nv,
    diag,
    xli,
    xhi,
    xlh,
    xhh,
    yl,
    yh,
    zl,
    zh,
    rates,
    first_rate,
    mid_state,
    end_state,
    base,
    send,
    recv,
    duo_begin,
    duo_first,
    duo_rates,
    duo_mid,
    duo_end,
    duo_base,
    duo_send,
    duo_recv,
    leaving,
    passed,
    shuffle,
    flows,
    coef,
    old0,
    old1,
    group,
    partial,
    near,
    mid,
    far,
    result,
    load_sem,
    store_sem,
    fine_send,
    fine_recv,
    duo_out,
    duo_in,
    hop_send,
    hop_recv,
    begin_send,
    begin_recv,
    flow_send,
    flow_recv,
    row_send,
    row_recv,
    group_send,
    group_recv,
    side_send,
    side_recv,
    part_send,
    part_recv,
):
    n = lax.axis_index("tm")
    s = lax.axis_index("space")
    g = n // GROUP
    z = n % GROUP
    groups = steps // GROUP

    sub = lax.broadcasted_iota(jnp.int32, (8, LANES), 0)
    lane = lax.broadcasted_iota(jnp.int32, (8, LANES), 1)
    parity = sub // 4
    row = sub % 4

    def split(even, odd):
        return jnp.where(parity == 0, jnp.float32(even), jnp.float32(odd))

    def remote(src, dst, ssem, rsem, device):
        return pltpu.make_async_remote_copy(
            src_ref=src, dst_ref=dst, send_sem=ssem, recv_sem=rsem, device_id=device, device_id_type=MESH
        )

    has = {-1: s > 0, 1: s < columns - 1}

    def inside(d):
        if d == 0:
            return None
        return s + d >= 0 if d < 0 else s + d < columns

    def both(a, b):
        if a is None:
            return b
        if b is None:
            return a
        return jnp.logical_and(a, b)

    def when(cond, run):
        if cond is None:
            run()
        else:
            pl.when(cond)(run)

    transfers = {}

    def add(name, sends, receives, make, partner):
        transfers.setdefault(name, []).append((sends, receives, make, partner))

    for k, d in enumerate((-1, 1)):
        add(
            "states",
            has[d],
            has[-d],
            functools.partial(
                remote,
                send.at[k, pl.ds(0, 3)],
                recv.at[1 - k, pl.ds(0, 3)],
                fine_send.at[k, 0],
                fine_recv.at[1 - k, 0],
                (n, s + d),
            ),
            None,
        )
        add(
            "begin_trace",
            both(n < steps - 1, has[d]),
            both(n > 0, has[-d]),
            functools.partial(
                remote,
                send.at[k, 2],
                recv.at[1 - k, 3],
                fine_send.at[k, 1],
                fine_recv.at[1 - k, 1],
                (n + 1, s + d),
            ),
            (n - 1, s - d),
        )
        add(
            "first_trace",
            both(n == 0, has[d]),
            both(n == 0, has[-d]),
            functools.partial(
                remote,
                send.at[k, 3],
                recv.at[1 - k, 3],
                fine_send.at[k, 2],
                fine_recv.at[1 - k, 1],
                (n, s + d),
            ),
            None,
        )
        for index, buffer in enumerate((old0, old1)):
            add(
                f"row{index}",
                has[d],
                has[-d],
                functools.partial(
                    remote,
                    buffer.at[:, 1 if d < 0 else ROWS],
                    buffer.at[:, ROWS + 1 if d < 0 else 0],
                    row_send.at[k, index],
                    row_recv.at[1 - k, index],
                    (n, s + d),
                ),
                None,
            )
        for j in range(GROUP - 1):
            rows = 3 - j
            add(
                f"side{j}",
                has[d],
                has[-d],
                functools.partial(
                    remote,
                    group.at[j, pl.ds(ROWS if d < 0 else 2 * ROWS - rows, rows)],
                    group.at[j, pl.ds(2 * ROWS if d < 0 else ROWS - rows, rows)],
                    side_send.at[k, j],
                    side_recv.at[1 - k, j],
                    (n, s + d),
                ),
                None,
            )
    def begin_copy(piece):
        where_to = (piece // 4, piece % 4)
        return remote(
            states_hbm.at[(2,) + where_to],
            begin.at[where_to],
            begin_send.at[piece],
            begin_recv.at[piece],
            (n + 1, s),
        )

    def begin_start(piece):
        pl.when(n < steps - 1)(lambda: begin_copy(piece).start())

    add(
        "hop",
        n < steps - 1,
        n > 0,
        functools.partial(remote, leaving, passed, hop_send, hop_recv, (n + 1, s)),
        None,
    )
    for index, d in enumerate((-3, -2, -1, 1, 2, 3)):
        needed = None if abs(d) == 1 else g >= abs(d)
        add(
            f"flow{abs(d)}",
            both(needed, inside(d)),
            both(needed, inside(-d)),
            functools.partial(
                remote,
                flows.at[REACH],
                flows.at[REACH - d],
                flow_send.at[index],
                flow_recv.at[index],
                (n, s + d),
            ),
            (n, s - d),
        )
    for shift in (1, 2, 3):
        add(
            "group",
            None,
            None,
            functools.partial(
                remote,
                group.at[z, pl.ds(ROWS, ROWS)],
                group.at[z, pl.ds(ROWS, ROWS)],
                group_send.at[shift - 1],
                group_recv.at[shift - 1],
                (g * GROUP + (z + shift) % GROUP, s),
            ),
            (g * GROUP + (z + GROUP - shift) % GROUP, s),
        )
    slot = 0
    for distance, buffer in ((3, far), (2, mid), (1, near)):
        for d in range(-distance, distance + 1):
            add(
                "part",
                both(g + distance < groups, inside(d)),
                both(g >= distance, inside(-d)),
                functools.partial(
                    remote,
                    partial,
                    buffer.at[pl.ds((distance - d) * ROWS, ROWS)],
                    part_send.at[slot],
                    part_recv.at[slot],
                    (n + distance * GROUP, s + d),
                ),
                (n - distance * GROUP, s - d),
            )
            slot += 1

    def start(name):
        for sends, _, make, _ in transfers[name]:
            when(sends, lambda make=make: make().start())

    def arrive(name):
        for _, receives, make, _ in transfers[name]:
            when(receives, lambda make=make: make().wait_recv())

    def sent(name):
        for sends, _, make, _ in transfers[name]:
            when(sends, lambda make=make: make().wait_send())

    load_states = pltpu.make_async_copy(states_hbm, states, load_sem.at[0])
    load_wind = pltpu.make_async_copy(wind_hbm, wind, load_sem.at[1])
    load_first = pltpu.make_async_copy(start_hbm, begin, load_sem.at[2])
    load_states.start()
    load_wind.start()
    pl.when(n == 0)(load_first.start)

    recv[...] = jnp.zeros(recv.shape, jnp.float32)
    duo_recv[...] = jnp.zeros(duo_recv.shape, jnp.float32)
    passed[...] = jnp.zeros(passed.shape, jnp.float32)
    duo_begin[0] = jnp.zeros(FIELD, jnp.float32)
    duo_first[0] = jnp.zeros(FIELD, jnp.float32)
    flows[...] = jnp.zeros(flows.shape, jnp.float32)
    old0[...] = jnp.zeros(old0.shape, jnp.float32)
    old1[...] = jnp.zeros(old1.shape, jnp.float32)
    group[...] = jnp.zeros(group.shape, jnp.float32)
    near[...] = jnp.zeros(near.shape, jnp.float32)
    mid[...] = jnp.zeros(mid.shape, jnp.float32)
    far[...] = jnp.zeros(far.shape, jnp.float32)

    barrier = pltpu.get_barrier_semaphore()
    expected = jnp.int32(0)

    def greet(cond, device):
        when(
            cond,
            lambda: pl.semaphore_signal(barrier, inc=1, device_id=device, device_id_type=MESH),
        )

    for d in (-1, 1):
        greet(has[d], (n, s + d))
        expected = expected + has[d].astype(jnp.int32)
    greet(n > 0, (n - 1, s))
    expected = expected + (n < steps - 1).astype(jnp.int32)
    for name in ("begin_trace", "flow2", "flow3", "group", "part"):
        for sends, receives, _, partner in transfers[name]:
            greet(receives, partner)
            expected = expected + (1 if sends is None else sends.astype(jnp.int32))

    load_states.wait()

    def pack(lower, upper, low_to, high_to):
        for half in range(2):
            low = None
            high = None
            for r in range(4):
                b, hh = (4 * half + r) // 2, r % 2
                lv = lower[b, hh]
                hv = upper[b, hh]
                lv = pltpu.roll(lv, r, 0) if r else lv
                hv = pltpu.roll(hv, (r + 5) % 8, 0) if r != 3 else hv
                low = lv if low is None else jnp.where(row == r, lv, low)
                high = hv if high is None else jnp.where(row == r, hv, high)
            low_to[half] = low
            high_to[half] = high

    def unpack(low_from, high_from):
        lows, highs = [], []
        for t in range(8):
            half, r = t // 4, t % 4
            lv = low_from[half]
            hv = high_from[half]
            lows.append(pltpu.roll(lv, 8 - r, 0) if r else lv)
            highs.append(pltpu.roll(hv, 3 - r, 0) if r != 3 else hv)
        return (
            jnp.stack(lows).reshape(4, 2, 8, LANES),
            jnp.stack(highs).reshape(4, 2, 8, LANES),
        )

    for k in range(3):
        pack(states[k, 0], states[k, 3], send.at[0, k], send.at[1, k])

    @pl.when(n == 0)
    def _():
        load_first.wait()
        pack(begin[0], begin[3], send.at[0, 3], send.at[1, 3])

    pl.semaphore_wait(barrier, expected)
    start("begin_trace")
    start("first_trace")
    start("states")
    for piece in range(4):
        begin_start(piece)

    load_wind.wait()
    for axis in range(3):
        nv[axis] = -wind[axis].astype(jnp.float32).reshape(FIELD)

    for axis in range(3):
        for i in range(2):
            for j in range(2):
                corner = jnp.where(parity == 0, nv[axis, 3 * i, 3 * j, 0], nv[axis, 3 * i, 3 * j, 1])
                shuffle[pl.ds(8 * (2 * i + j), 8)] = corner
        for r in range(ROWS):
            flows[REACH, r, axis] = shuffle[pl.ds(r, 8, stride=4)]

    cxl = LIFT * jnp.minimum(nv[0, 0], 0.0)
    cxh = LIFT * jnp.minimum(-nv[0, 3], 0.0)
    xli[...] = jnp.where(row > 0, -cxl, 0.0)
    xlh[...] = jnp.where(row == 0, -cxl, 0.0)
    xhi[...] = jnp.where(row < 3, -cxh, 0.0)
    xhh[...] = jnp.where(row == 3, -cxh, 0.0)
    cyl = LIFT * jnp.minimum(nv[1, :, 0], 0.0)
    cyh = LIFT * jnp.minimum(-nv[1, :, 3], 0.0)
    yl[...] = jnp.where(lane >= CZ, -cyl, 0.0)
    yh[...] = jnp.where(lane < LANES - CZ, -cyh, 0.0)
    czl = jnp.where(parity == 0, LIFT * jnp.minimum(nv[2, :, :, 0], 0.0), 0.0)
    czh = jnp.where(parity == 1, LIFT * jnp.minimum(-nv[2, :, :, 1], 0.0), 0.0)
    layer = lane % CZ
    zl[...] = jnp.where(layer > 0, -czl, 0.0)
    zh[...] = jnp.where(layer < CZ - 1, -czh, 0.0)
    diag[:, :, 0] = czl
    diag[:, :, 1] = czh
    diag[0] = diag[0] + cxl
    diag[3] = diag[3] + cxh
    diag[:, 0] = diag[:, 0] + cyl
    diag[:, 3] = diag[:, 3] + cyh

    same = [[split(DER[2 * i, 2 * j], DER[2 * i + 1, 2 * j + 1]) for j in range(2)] for i in range(2)]
    cross = [[split(DER[2 * i, 2 * j + 1], DER[2 * i + 1, 2 * j]) for j in range(2)] for i in range(2)]

    def interior(u, out):
        for b in range(4):
            pair = [u[:, b, 0], u[:, b, 1]]
            turned = [pltpu.roll(half, 4, 1) for half in pair]
            for i in range(2):
                own = pair[i]
                along_z = (
                    same[i][0] * pair[0]
                    + cross[i][0] * turned[0]
                    + same[i][1] * pair[1]
                    + cross[i][1] * turned[1]
                )
                total = diag[:, b, i] * own + nv[2, :, b, i] * along_z
                if i == 0:
                    total = total + zl[:, b] * pltpu.roll(turned[1], 1, 2)
                else:
                    total = total + zh[:, b] * pltpu.roll(turned[0], LANES - 1, 2)
                others = [own if c == b else u[:, c, i] for c in range(4)]
                along_y = weighted([(DER[b, c], others[c]) for c in range(4)])
                total = total + nv[1, :, b, i] * along_y
                if b == 0:
                    total = total + yl[:, i] * pltpu.roll(others[3], CZ, 2)
                if b == 3:
                    total = total + yh[:, i] * pltpu.roll(others[0], LANES - CZ, 2)
                along_x = jnp.stack([weighted([(DER[a, c], own[c]) for c in range(4)]) for a in range(4)])
                total = total + nv[0, :, b, i] * along_x
                out[0, b, i] = total[0] + xli[b, i] * pltpu.roll(own[3], 1, 0)
                out[1:3, b, i] = total[1:3]
                out[3, b, i] = total[3] + xhi[b, i] * pltpu.roll(own[0], 7, 0)

    def finish_rate(out, low_from, high_from):
        low, high = unpack(low_from, high_from)
        lower = out[0] + xlh[...] * low
        upper = out[3] + xhh[...] * high
        out[0] = lower
        out[3] = upper
        return lower, upper

    def old_rate(k, carry):
        interior(states.at[k], rates.at[k])
        return carry

    lax.fori_loop(0, 3, old_rate, 0)
    arrive("states")
    for k in range(3):
        finish_rate(rates.at[k], recv.at[0, k], recv.at[1, k])

    base[...] = -DT * rates[0] + (H / 24.0) * (5.0 * rates[0] + 8.0 * rates[1] - rates[2])

    top = (sub // 4) % 2 == 0
    middle = (sub // 2) % 2 == 0
    bottom = sub % 2 == 0
    signs = [jnp.where(bit, jnp.float32(-1.0), jnp.float32(1.0)) for bit in (top, middle, bottom)]
    open_y = jnp.logical_or(jnp.logical_and(middle, lane >= CZ), jnp.logical_and(jnp.logical_not(middle), lane < LANES - CZ))
    open_z = jnp.logical_or(jnp.logical_and(bottom, layer > 0), jnp.logical_and(jnp.logical_not(bottom), layer < CZ - 1))

    def coarse_coefficients(block, carry):
        wide = flows[block]
        center = jnp.ones((ROWS, 8, LANES), jnp.float32)
        for axis in range(3):
            slope = signs[axis] * wide[:, axis]
            jump = jnp.minimum(-slope, 0.0)
            center = center + H * (0.5 * slope + jump)
            coef[1 + axis, block] = (-0.5 * H) * slope
            outer = -H * jump
            if axis == 1:
                outer = jnp.where(open_y, outer, 0.0)
            if axis == 2:
                outer = jnp.where(open_z, outer, 0.0)
            coef[4 + axis, block] = outer
        coef[0, block] = center
        return carry

    def advance(u, low):
        count = u.shape[0]
        own = u[1 : count - 1]
        px = pltpu.roll(u, 4, 1)
        ox = jnp.where(top, px[0 : count - 2], px[2:count])
        px = px[1 : count - 1]
        py = jnp.where(middle, pltpu.roll(own, 6, 1), pltpu.roll(own, 2, 1))
        pz = jnp.where(bottom, pltpu.roll(own, 7, 1), pltpu.roll(own, 1, 1))
        oy = jnp.where(middle, pltpu.roll(py, CZ, 2), pltpu.roll(py, LANES - CZ, 2))
        oz = jnp.where(bottom, pltpu.roll(pz, 1, 2), pltpu.roll(pz, LANES - 1, 2))
        total = None
        for index, value in enumerate((own, px, py, pz, ox, oy, oz)):
            factors = coef[index].reshape(SPAN, 8, LANES)[low + 1 : low + count - 1]
            piece = factors * value
            total = piece if total is None else total + piece
        return total

    res_same = [split(RES[0, 2 * i], RES[1, 2 * i + 1]) for i in range(2)]
    res_cross = [split(RES[0, 2 * i + 1], RES[1, 2 * i]) for i in range(2)]
    pro_same = [split(PRO[2 * i, 0], PRO[2 * i + 1, 1]) for i in range(2)]
    pro_cross = [split(PRO[2 * i, 1], PRO[2 * i + 1, 0]) for i in range(2)]

    def restricted(field):
        for i in range(2):
            lines = weighted([(RES[i, a], field[a]) for a in range(4)])
            for j in range(2):
                pair = weighted([(RES[j, b], lines[b]) for b in range(4)])
                turned = pltpu.roll(pair, 4, 1)
                value = (
                    res_same[0] * pair[0]
                    + res_cross[0] * turned[0]
                    + res_same[1] * pair[1]
                    + res_cross[1] * turned[1]
                )
                shuffle[pl.ds(8 * (2 * i + j), 8)] = value
        return jnp.stack([shuffle[pl.ds(r, 8, stride=4)] for r in range(ROWS)])

    def prolonged(rows):
        for r in range(ROWS):
            shuffle[pl.ds(r, 8, stride=4)] = rows[r]
        corners = []
        for index in range(4):
            value = shuffle[pl.ds(8 * index, 8)]
            turned = pltpu.roll(value, 4, 0)
            corners.append(jnp.stack([pro_same[i] * value + pro_cross[i] * turned for i in range(2)]))
        lines = [
            jnp.stack([weighted([(PRO[b, 0], corners[2 * i]), (PRO[b, 1], corners[2 * i + 1])]) for b in range(4)])
            for i in range(2)
        ]
        return [weighted([(PRO[a, 0], lines[0]), (PRO[a, 1], lines[1])]) for a in range(4)]

    coarse_coefficients(REACH, 0)

    @pl.when(n == 0)
    def _():
        for _, receives, make, _ in transfers["first_trace"]:
            when(receives, lambda make=make: make().wait_recv())
        duo_begin[0] = begin[...]
        interior(begin, duo_first.at[0])
        finish_rate(duo_first.at[0], recv.at[0, 3], recv.at[1, 3])

    duo_begin[1] = states[2]
    duo_first[1] = rates[2]
    duo_rates[0] = rates[...]
    duo_rates[1] = jnp.zeros((3,) + FIELD, jnp.float32)

    def duo_copy(k, d, slot):
        return remote(
            duo_send.at[k, slot],
            duo_recv.at[1 - k, slot],
            duo_out.at[k, slot],
            duo_in.at[1 - k, slot],
            (n, s + d),
        )

    def duo_launch(slot):
        for k, d in enumerate((-1, 1)):
            pl.when(has[d])(lambda k=k, d=d: duo_copy(k, d, slot).start())

    def duo_await(slot):
        for k, d in enumerate((-1, 1)):
            pl.when(has[-d])(lambda k=k, d=d: duo_copy(k, d, slot).wait_recv())

    def duo_fresh(target, factor, rate, slot, halo):
        def outer(x, carry):
            if halo is None:
                lower, upper = rate(x)[0], rate(x)[3]
            else:
                lower, upper = finish_rate(rate(x), duo_recv.at[0, halo, x], duo_recv.at[1, halo, x])
            first = duo_base[x, 0] + factor * lower
            last = duo_base[x, 3] + factor * upper
            target[x, 0] = first
            target[x, 3] = last
            pack(first, last, duo_send.at[0, slot, x], duo_send.at[1, slot, x])
            return carry

        def inner(x, carry):
            target[x, 1:3] = duo_base[x, 1:3] + factor * rate(x)[1:3]
            return carry

        lax.fori_loop(0, 2, outer, 0)
        duo_launch(slot)
        lax.fori_loop(0, 2, inner, 0)

    def opening(x, carry):
        duo_base[x] = (
            duo_begin[x]
            - DT * duo_rates[x, 0]
            + (H / 24.0) * (5.0 * duo_rates[x, 0] + 8.0 * duo_rates[x, 1] - duo_rates[x, 2])
        )
        return carry

    lax.fori_loop(0, 2, opening, 0)
    duo_fresh(duo_mid, DT, lambda x: duo_first.at[x], 0, None)

    def duo_closing(slot):
        def prepare(x, carry):
            begin_start(4 + 2 * slot + x)
            duo_base[x] = (
                duo_mid[x]
                - DT * duo_rates[x, 1]
                + (H / 24.0) * (8.0 * duo_rates[x, 1] + 5.0 * duo_rates[x, 2] - duo_rates[x, 0])
            )
            interior(duo_mid.at[x], duo_rates.at[x, 1])
            return carry

        lax.fori_loop(0, 2, prepare, 0)
        duo_await(slot)
        duo_fresh(duo_end, DT, lambda x: duo_rates.at[x, 1], slot + 1, slot)

    def duo_middle(slot):
        def prepare(x, carry):
            begin_start(4 + 2 * slot + x)
            duo_base[x] = duo_begin[x] + (H / 24.0) * (5.0 * duo_first[x] + 8.0 * duo_rates[x, 1])
            interior(duo_end.at[x], duo_rates.at[x, 2])
            return carry

        lax.fori_loop(0, 2, prepare, 0)
        duo_await(slot)
        duo_fresh(duo_mid, -H / 24.0, lambda x: duo_rates.at[x, 2], slot + 1, slot)

    duo_closing(0)
    for x in range(2):
        duo_rates[x, 0] = duo_first[x]
        old0[x, 1 : ROWS + 1] = restricted(duo_begin.at[x])
    start("row0")
    start("flow1")
    duo_middle(1)
    duo_closing(2)
    duo_middle(3)
    duo_closing(4)
    for x in range(2):
        old1[x, 1 : ROWS + 1] = restricted(duo_end.at[x])
    start("row1")

    def last_rate(x, carry):
        begin_start(14 + x)
        interior(duo_end.at[x], duo_rates.at[x, 2])
        return carry

    lax.fori_loop(0, 2, last_rate, 0)
    arrive("row0")
    low = MID - 1
    h_rates0 = [advance(old0[x], low) - old0[x, 1 : ROWS + 1] for x in range(2)]
    duo_await(5)
    offsets = []
    for x in range(2):
        finish_rate(duo_rates.at[x, 2], duo_recv.at[0, 5, x], duo_recv.at[1, 5, x])
    quadratures = [
        restricted(
            [
                (H / 6.0) * (duo_first[x, a] + 4.0 * duo_rates[x, 1, a] + duo_rates[x, 2, a])
                for a in range(4)
            ]
        )
        for x in range(2)
    ]
    arrive("row1")
    for x in (1, 0):
        h_rate0 = h_rates0[x]
        h_rate1 = advance(old1[x], low) - old1[x, 1 : ROWS + 1]
        trapezoid = 0.5 * (h_rate0 + h_rate1)
        offset = -h_rate0 + trapezoid + (quadratures[x] - trapezoid)
        if x == 1:
            leaving[...] = offset
            start("hop")
    is_first = n == 0
    offset = offset + jnp.where(is_first, old0[0, 1 : ROWS + 1] + h_rates0[0], 0.0)

    arrive("begin_trace")
    for piece in range(16):
        pl.when(n > 0)(lambda piece=piece: begin_copy(piece).wait_recv())
    interior(begin, first_rate)
    lower, upper = finish_rate(first_rate, recv.at[0, 3], recv.at[1, 3])

    def fine_copy(k, d, slot):
        return remote(
            send.at[k, slot],
            recv.at[1 - k, slot],
            fine_send.at[k, slot],
            fine_recv.at[1 - k, slot],
            (n, s + d),
        )

    def launch(slot):
        for k, d in enumerate((-1, 1)):
            pl.when(has[d])(lambda k=k, d=d: fine_copy(k, d, slot).start())

    def await_fine(slot):
        for k, d in enumerate((-1, 1)):
            pl.when(has[-d])(lambda k=k, d=d: fine_copy(k, d, slot).wait_recv())

    def fresh(u, origin, factor, rate, lower, upper, slot):
        first = origin[0] + factor * lower
        last = origin[3] + factor * upper
        u[0] = first
        u[3] = last
        if slot is not None:
            pack(first, last, send.at[0, slot], send.at[1, slot])
            launch(slot)
        u[1:3] = origin[1:3] + factor * rate[1:3]

    base[...] = base[...] + begin[...]
    fresh(mid_state, base, DT, first_rate, lower, upper, 4)

    arrive("hop")
    group[z, pl.ds(ROWS, ROWS)] = offset + passed[...]
    start("group")
    start("flow2")

    def to_closing(slot, out_slot):
        base[...] = (
            mid_state[...]
            - DT * rates[1]
            + (H / 24.0) * (8.0 * rates[1] + 5.0 * rates[2] - rates[0])
        )
        interior(mid_state, rates.at[1])
        await_fine(slot)
        lower, upper = finish_rate(rates.at[1], recv.at[0, slot], recv.at[1, slot])
        fresh(end_state, base, DT, rates.at[1], lower, upper, out_slot)

    def to_middle(slot):
        base[...] = begin[...] + (H / 24.0) * (5.0 * first_rate[...] + 8.0 * rates[1])
        interior(end_state, rates.at[2])
        await_fine(slot)
        lower, upper = finish_rate(rates.at[2], recv.at[0, slot], recv.at[1, slot])
        fresh(mid_state, base, -H / 24.0, rates.at[2], lower, upper, slot + 1)

    to_closing(4, 5)
    rates[0] = first_rate[...]
    before0 = restricted(begin)
    for j in range(GROUP):

        @pl.when(z != j)
        def _():
            remote(
                group.at[j, pl.ds(ROWS, ROWS)],
                group.at[j, pl.ds(ROWS, ROWS)],
                group_send.at[0],
                group_recv.at[(z + GROUP - 1 - j) % GROUP],
                (n, s),
            ).wait_recv()

        if j < GROUP - 1:
            start(f"side{j}")
    start("flow3")
    arrive("flow1")
    coarse_coefficients(REACH - 1, 0)
    coarse_coefficients(REACH + 1, 0)
    to_middle(5)
    for j in range(GROUP - 1):
        arrive(f"side{j}")
    y = group[0]
    y = advance(y, MID - 4) + group[1, 1:11]
    y = advance(y, MID - 3) + group[2, 2:10]
    y = advance(y, MID - 2)[1:5] + group[3, 4:8]
    partial[...] = y
    start("part")
    to_closing(6, 7)
    to_middle(7)
    to_closing(8, None)
    stores = [
        pltpu.make_async_copy(field, fields_hbm.at[index], store_sem.at[3 + index])
        for index, field in enumerate((begin, mid_state, end_state))
    ]
    for store in stores:
        store.start()
    before1 = restricted(end_state)
    arrive("flow2")
    arrive("flow3")
    lax.fori_loop(0, REACH - 1, coarse_coefficients, 0)
    lax.fori_loop(REACH + 2, 2 * REACH + 1, coarse_coefficients, 0)
    arrive("part")
    y = far[...]
    for step in range(4):
        y = advance(y, step)
    y = y + mid[...]
    for step in range(4, 8):
        y = advance(y, step)
    y = y + near[...]
    for j in range(3):
        count = 12 - 2 * j
        stepped = advance(y, MID - 4 + j) + group[j, j + 1 : 11 - j]
        y = jnp.where(z > j, stepped, y[1 : count - 1])
    finish = advance(y, MID - 1) + group[z, pl.ds(ROWS, ROWS)]
    begin_rows = jnp.where(is_first, before0, y[1:5])
    delta0 = begin_rows - before0
    delta1 = finish - before1

    for index, delta in enumerate((delta0, 0.5 * (delta0 + delta1), delta1)):
        lifted = prolonged(delta)
        for a in range(4):
            result[index, a] = lifted[a]
        pltpu.make_async_copy(result.at[index], lifted_hbm.at[index], store_sem.at[index]).start()
    for index in range(3):
        pltpu.make_async_copy(result.at[index], lifted_hbm.at[index], store_sem.at[index]).wait()
    for store in stores:
        store.wait()

    for name in transfers:
        sent(name)
    for piece in range(16):
        pl.when(n < steps - 1)(lambda piece=piece: begin_copy(piece).wait_send())
    for k, d in enumerate((-1, 1)):
        for slot in range(4, 9):
            pl.when(has[d])(lambda k=k, d=d, slot=slot: fine_copy(k, d, slot).wait_send())
        for slot in range(6):
            pl.when(has[d])(lambda k=k, d=d, slot=slot: duo_copy(k, d, slot).wait_send())


def solution(mesh):
    steps = mesh.shape["tm"]
    columns = mesh.shape["space"]

    def body(node_states, initial_state, velocity):
        states = node_states.reshape((3,) + FIELD)
        first = initial_state.reshape(FIELD)
        wind = velocity.reshape(3, 4, 4, 16, LANES)
        f32 = jnp.float32
        vmem = lambda *shape: pltpu.VMEM(shape, f32)
        dma = lambda *shape: pltpu.SemaphoreType.DMA(shape)
        fields, lifted = pl.pallas_call(
            functools.partial(kernel, steps, columns),
            out_shape=[jax.ShapeDtypeStruct((3,) + FIELD, f32)] * 2,
            in_specs=[pl.BlockSpec(memory_space=pltpu.HBM)] * 3,
            out_specs=[pl.BlockSpec(memory_space=pl.ANY)] * 2,
            scratch_shapes=[
                vmem(3, *FIELD),
                pltpu.VMEM((3, 4, 4, 16, LANES), jnp.bfloat16),
                vmem(*FIELD),
                vmem(3, *FIELD),
                vmem(*FIELD),
                vmem(4, 2, 8, LANES),
                vmem(4, 2, 8, LANES),
                vmem(4, 2, 8, LANES),
                vmem(4, 2, 8, LANES),
                vmem(4, 2, 8, LANES),
                vmem(4, 2, 8, LANES),
                vmem(4, 4, 8, LANES),
                vmem(4, 4, 8, LANES),
                vmem(3, *FIELD),
                vmem(*FIELD),
                vmem(*FIELD),
                vmem(*FIELD),
                vmem(*FIELD),
                vmem(2, 9, 2, 8, LANES),
                vmem(2, 9, 2, 8, LANES),
                vmem(2, *FIELD),
                vmem(2, *FIELD),
                vmem(2, 3, *FIELD),
                vmem(2, *FIELD),
                vmem(2, *FIELD),
                vmem(2, *FIELD),
                vmem(2, 6, 2, 2, 8, LANES),
                vmem(2, 6, 2, 2, 8, LANES),
                vmem(ROWS, 8, LANES),
                vmem(ROWS, 8, LANES),
                vmem(32, LANES),
                vmem(2 * REACH + 1, ROWS, 3, 8, LANES),
                vmem(7, 2 * REACH + 1, ROWS, 8, LANES),
                vmem(2, ROWS + 2, 8, LANES),
                vmem(2, ROWS + 2, 8, LANES),
                vmem(GROUP, 3 * ROWS, 8, LANES),
                vmem(ROWS, 8, LANES),
                vmem(3 * ROWS, 8, LANES),
                vmem(5 * ROWS, 8, LANES),
                vmem(7 * ROWS, 8, LANES),
                vmem(3, *FIELD),
                dma(3),
                dma(6),
                dma(2, 9),
                dma(2, 9),
                dma(2, 6),
                dma(2, 6),
                pltpu.SemaphoreType.DMA,
                pltpu.SemaphoreType.DMA,
                dma(16),
                dma(16),
                dma(6),
                dma(6),
                dma(2, 2),
                dma(2, 2),
                dma(3),
                dma(3),
                dma(2, GROUP),
                dma(2, GROUP),
                dma(15),
                dma(15),
            ],
            compiler_params=pltpu.CompilerParams(
                collective_id=0, has_side_effects=True, vmem_limit_bytes=60 * 1024 * 1024
            ),
        )(states, first, wind)
        return (fields + lifted).reshape(1, 3, 64, ROWS, LANES)

    return jax.shard_map(
        body,
        mesh=mesh,
        in_specs=(
            P("tm", None, None, "space", None),
            P(None, "space", None),
            P(None, None, "space", None),
        ),
        out_specs=P("tm", None, None, "space", None),
        check_vma=False,
    )
```
